32 devices in a mesh: clip: 16 (over z, y, core), head: 2 (over x).
Axes of the slice: x: 2, y: 2, z: 4, core: 2. Of those that a mesh axis runs over, the one named last changes fastest.
Arguments:
- frames: bfloat16 [32768, 1024], P(('clip', 'head')), may hold values from -6 to 6
- clip_lengths: int32 [64], P('clip'), may hold values from 1 to 1024, as said below
- timesteps: int32 [64], replicated, may hold values from 0 to 999
- w_qkv: float32 [3, 1024, 1024], P(None, 'clip', 'head'), may hold values from -0.25 to 0.25
- w_out: float32 [1024, 1024], P('head', 'clip'), may hold values from -0.75 to 0.75
- w_up: float32 [1024, 2048], P('clip', 'head'), may hold values from -0.1875 to 0.1875
- w_down: float32 [2048, 1024], P('head', 'clip'), may hold values from -0.125 to 0.125
- w_ada: float32 [1024, 6144], P(None, ('clip', 'head')), may hold values from -0.25 to 0.25
- b_ada: float32 [6144], P(('clip', 'head')), may hold values from -1.8 to 1.8
- grad_out: bfloat16 [32768, 1024], P(('clip', 'head')), may hold values from -6 to 6
Outputs:
- mixed: bfloat16 [32768, 1024], P(('clip', 'head'))
- grad_frames: float32 [32768, 1024], P(('clip', 'head'))
- grad_qkv: float32 [3, 1024, 1024], P(None, 'clip', 'head')
- grad_outw: float32 [1024, 1024], P('head', 'clip')
- grad_up: float32 [1024, 2048], P('clip', 'head')
- grad_down: float32 [2048, 1024], P('head', 'clip')
- grad_ada: float32 [1024, 6144], P(None, ('clip', 'head'))
- grad_bias: float32 [6144], P(('clip', 'head'))
The draws below stay inside these ranges and needn't reach their ends.
Inputs may be any that keep to these rules, and one draw needn't show every extreme that they name: `clip_lengths`: in each group of 4 entries exactly one clip, at a place drawn from the seed, has 1024 frames and the others fewer; a group's lengths sum to less than 2048, and the slots after its last clip are padding.
All inputs are finite; a program needn't handle non-finite values.
Results may differ from the reference program's by a relative error of at most 0.02.
The reference program's roundings to bfloat16 on the way count: a program that leaves them out, or rounds other values in their place, can miss the bound.
Values may be sent and summed in bfloat16 or wider, within the bound.
No kernel may reach another device: no remote copies, remote signals or barrier semaphores. Data moves between devices by JAX's collectives and lax.ppermute only.
A program may use at most 320 MiB of HBM per device.

```python
import math
import jax
import jax.numpy as jnp
from jax import lax

D = 1024
FF = 2048
HEADS = 16
HEAD_DIM = 64
FR_GRP = 2048
CLIPS = 4
TOKENS = 32768
ALL_CLIPS = 64
N_CLIP = 16


def draw_clip_lengths(key, part):
    key = jax.random.fold_in(key, 11)
    groups = ALL_CLIPS // CLIPS
    key_long, key_level, key_factor = jax.random.split(key, 3)
    longest_at = jax.random.randint(key_long, (groups, 1), 0, CLIPS)
    level = jax.random.randint(key_level, (groups, CLIPS), 0, 6)
    factor = jax.random.randint(key_factor, (groups, CLIPS), 1, 9)
    weighting = jnp.left_shift(jnp.ones((groups, CLIPS), jnp.int32), level) * factor
    slot_index = jnp.arange(CLIPS, dtype=jnp.int32)[None, :]
    is_longest = slot_index == longest_at
    weighting = jnp.where(is_longest, 0, weighting)
    remaining = FR_GRP // 2 - FR_GRP // 8
    weight_total = jnp.sum(weighting, axis=1, keepdims=True)
    shares = 1 + weighting * remaining // weight_total
    lengths = jnp.where(is_longest, FR_GRP // 2, shares)
    return lengths.reshape(ALL_CLIPS).astype(jnp.int32)


def set_ends(values, own_key, smallest, top_value):
    index_at = [jax.random.randint(jax.random.fold_in(own_key, axis), (), 0, length) for axis, length in enumerate(values.shape)]
    longest = values.shape.index(max(values.shape))
    next_to = index_at[:longest] + [(index_at[longest] + 1) % values.shape[longest]] + index_at[longest + 1:]
    return values.at[tuple(index_at)].set(smallest).at[tuple(next_to)].set(top_value)


def shard_levels(stream_key, extent, cuts, least, high):
    loudness, own = 1.0, jax.random.fold_in(stream_key, 6)
    for dim, blocks in cuts:
        heights = jnp.exp(jax.random.uniform(jax.random.fold_in(own, dim), (blocks,), jnp.float32, least / len(cuts), high / len(cuts)))
        loudness = loudness * jnp.repeat(heights, extent[dim] // blocks).reshape([-1 if axis == dim else 1 for axis in range(len(extent))])
    return loudness


def centred(key, extent, deviation, limit, cuts=(), kind=jnp.bfloat16):
    result = jax.random.normal(key, extent, jnp.float32) * deviation
    if len(cuts) > 0:
        result = shard_levels(key, extent, cuts, -0.22, 0.18) * result
    return jnp.clip(result, min=-limit, max=limit).astype(kind)


def setup_inputs(seed: int = 0) -> dict:
    seeds = jax.random.split(jax.random.key(seed), 11)
    return {
        "frames": centred(seeds[0], (TOKENS, D), 1.0, 6.0, ((0, 32),)),
        "clip_lengths": draw_clip_lengths(jax.random.fold_in(seeds[10], 71), 0),
        "timesteps": set_ends(jax.random.randint(seeds[2], (ALL_CLIPS,), 0, 1000), jax.random.fold_in(seeds[2], 1), 0, 999).astype(jnp.int32),
        "w_qkv": centred(seeds[3], (3, D, D), (D // 2) ** -0.5, 0.25, ((1, 16), (2, 2)), jnp.float32),
        "w_out": centred(seeds[4], (D, D), (D // 16) ** -0.5, 0.75, ((0, 2), (1, 16)), jnp.float32),
        "w_up": centred(seeds[5], (D, FF), D ** -0.5, 0.1875, ((0, 16), (1, 2)), jnp.float32),
        "w_down": centred(seeds[6], (FF, D), FF ** -0.5, 0.125, ((0, 2), (1, 16)), jnp.float32),
        "w_ada": centred(seeds[7], (D, 6 * D), (D // 2) ** -0.5, 0.25, ((1, 32),), jnp.float32),
        "b_ada": centred(seeds[8], (6 * D,), 0.3, 1.8, ((0, 32),), jnp.float32),
        "grad_out": centred(seeds[9], (TOKENS, D), 1.0, 6.0, ((0, 32),)),
    }


HIGHEST = lax.Precision.HIGHEST
MASKED = -1e+30
EPSILON = 1e-06

@jax.custom_vjp
def low(v):
    return lax.optimization_barrier(v.astype(jnp.bfloat16)).astype(jnp.float32)

@jax.custom_vjp
def low_back(v):
    return v

def low_keep(v):
    return (low(v), None)

def low_pass(kept, grad):
    return (grad,)

def back_keep(v):
    return (v, None)

def back_low(kept, grad):
    return (low(grad),)
low.defvjp(low_keep, low_pass)
low_back.defvjp(back_keep, back_low)

def clip_layout(lengths, frame_count):
    ends_at = jnp.cumsum(lengths, dtype=jnp.int32)
    starts_at = ends_at - lengths
    frame_index = jnp.arange(frame_count, dtype=jnp.int32)
    inside = (frame_index[:, None] >= starts_at[None, :]) & (frame_index[:, None] < ends_at[None, :])
    member = inside.astype(jnp.float32)
    segment = lax.optimization_barrier(jnp.sum((frame_index[:, None] >= ends_at[None, :]).astype(jnp.int32), axis=1, dtype=jnp.int32))
    padding = segment == lengths.shape[0]
    begins = lax.optimization_barrier(jnp.sum(jnp.where(inside, starts_at[None, :], 0), axis=1, dtype=jnp.int32)) + jnp.where(padding, ends_at[-1], 0)
    return (member, segment, frame_index - begins)

def time_vector(steps, width):
    halfway = width // 2
    rates = jnp.exp(jnp.arange(halfway, dtype=jnp.float32) * (-math.log(10000.0) / (halfway - 1)))
    angles = steps.astype(jnp.float32)[:, None] * rates[None, :]
    return jnp.concatenate([jnp.sin(angles), jnp.cos(angles)], axis=1)

def rotary_tables(position, head_dim):
    halfway = head_dim // 2
    rates = jnp.exp(jnp.arange(halfway, dtype=jnp.float32) * (-2.0 * math.log(10000.0) / head_dim))
    angles = position.astype(jnp.float32)[:, None] * rates[None, :]
    return (jnp.cos(angles)[:, None, :], jnp.sin(angles)[:, None, :])

def rotate(vectors, cosine, sine):
    halfway = vectors.shape[-1] // 2
    first_half = vectors[..., :halfway]
    second_half = vectors[..., halfway:]
    return jnp.concatenate([first_half * cosine - second_half * sine, second_half * cosine + first_half * sine], axis=-1)

def layer_norm(values):
    centered = values - lax.optimization_barrier(jnp.mean(values, axis=-1, keepdims=True))
    variance = lax.optimization_barrier(jnp.mean(centered * centered, axis=-1, keepdims=True))
    return centered * lax.rsqrt(variance + EPSILON)

def modulate(values, scale, shift):
    return layer_norm(values) * (1.0 + scale) + shift

def one_group(weights, inputs, lengths, steps):
    w_query, w_key, w_value, w_output, w_upward, w_downward, w_adaptive, b_adaptive = weights
    frame_count, width = inputs.shape
    member, segment, position = clip_layout(lengths, frame_count)
    cosine, sine = rotary_tables(position, HEAD_DIM)
    condition = jax.nn.silu(time_vector(steps, width))
    adaptive = jnp.dot(condition, w_adaptive, precision=HIGHEST) + b_adaptive
    modes = jnp.dot(member, adaptive, precision=HIGHEST)
    shift_one, scale_one, gate_one, shift_two, scale_two, gate_two = jnp.split(modes, 6, axis=1)
    normed_one = low(modulate(inputs, scale_one, shift_one))
    head_shape = (frame_count, HEADS, HEAD_DIM)
    query = low(rotate(low_back(jnp.dot(normed_one, w_query, precision=HIGHEST)).reshape(head_shape), cosine, sine))
    keys_all = low(rotate(low_back(jnp.dot(normed_one, w_key, precision=HIGHEST)).reshape(head_shape), cosine, sine))
    values_all = low(low_back(jnp.dot(normed_one, w_value, precision=HIGHEST))).reshape(head_shape)
    block_rows = min(512, frame_count)
    block_count = frame_count // block_rows
    scaling = 1.0 / math.sqrt(HEAD_DIM)

    def attend(item):
        query_block, segment_block = item
        raw_scores = low_back(jnp.einsum('qhd,khd->hqk', query_block, keys_all, precision=HIGHEST))
        same_clip = segment_block[None, :, None] == segment[None, None, :]
        scores = jnp.where(same_clip, raw_scores * scaling, MASKED)
        highest_score = lax.optimization_barrier(jnp.max(scores, axis=-1, keepdims=True))
        unnormed = jnp.exp(scores - highest_score)
        row_total = lax.optimization_barrier(jnp.sum(unnormed, axis=-1, keepdims=True))
        attention = unnormed / row_total
        return jnp.einsum('hqk,khd->qhd', low(attention), values_all, precision=HIGHEST)
    attended = lax.map(jax.checkpoint(attend), (query.reshape(block_count, block_rows, HEADS, HEAD_DIM), segment.reshape(block_count, block_rows)))
    attended = low(low_back(attended.reshape(frame_count, width)))
    branch_one = low_back(jnp.dot(attended, w_output, precision=HIGHEST))
    middle = inputs + gate_one * branch_one
    normed_two = low(modulate(middle, scale_two, shift_two))
    active = low(jax.nn.gelu(low_back(jnp.dot(normed_two, w_upward, precision=HIGHEST)), approximate=True))
    branch_two = low_back(jnp.dot(active, w_downward, precision=HIGHEST))
    return middle + gate_two * branch_two

def reference(frames, clip_lengths, timesteps, w_qkv, w_out, w_up, w_down, w_ada, b_ada, grad_out):
    lengths = clip_lengths.reshape(N_CLIP, CLIPS)
    steps = timesteps.reshape(N_CLIP, CLIPS)

    def whole(inputs, qkv_weight, out_weight, up_weight, down_weight, ada_weight, ada_bias):
        weights = (low(qkv_weight[0]), low(qkv_weight[1]), low(qkv_weight[2]), low(out_weight), low(up_weight), low(down_weight), low(ada_weight), low(ada_bias))

        def group_step(carry, item):
            return (carry, one_group(weights, item[0], item[1], item[2]))
        carry, outputs = lax.scan(jax.checkpoint(group_step), jnp.zeros((), jnp.float32), (inputs.reshape(N_CLIP, FR_GRP, D), lengths, steps))
        return outputs.reshape(TOKENS, D)
    mixed, pullback = jax.vjp(whole, frames.astype(jnp.float32), w_qkv, w_out, w_up, w_down, w_ada, b_ada)
    grads = pullback(grad_out.astype(jnp.float32))
    return (mixed.astype(jnp.bfloat16), grads[0], grads[1], grads[2], grads[3], grads[4], grads[5], grads[6])
```

```python
import functools
import math

import jax
import jax.numpy as jnp
from jax import lax
from jax.experimental import pallas as pl
from jax.experimental.pallas import tpu as pltpu
from jax.sharding import Mesh
from jax.sharding import PartitionSpec as P

HEAD_DIM = 64
HEADS = 16
HIGHEST = lax.Precision.HIGHEST
MASKED = -1e30
EPSILON = 1e-06
VMEM_LIMIT = 60 * 1024 * 1024
F32 = jnp.float32
BF16 = jnp.bfloat16

ALL = ("za", "zb", "core", "hh", "hl")
MOVE = ("core", "hh", "hl")
SUB = ("core", "hl")

NT = (((1,), (1,)), ((), ()))
NN = (((1,), (0,)), ((), ()))
TN = (((0,), (0,)), ((), ()))


def dot(a, b, dims=NN, precision=None):
    return lax.dot_general(a, b, dims, precision=precision, preferred_element_type=F32)


def params(**more):
    return pltpu.CompilerParams(vmem_limit_bytes=VMEM_LIMIT, **more)


def cost(flops, bytes_accessed, transcendentals=0):
    return pl.CostEstimate(
        flops=int(flops), bytes_accessed=int(bytes_accessed), transcendentals=int(transcendentals)
    )


def whole(shape, buffers=None):
    zeros = (0,) * len(shape)
    if buffers is None:
        return pl.BlockSpec(shape, lambda *_: zeros)
    return pl.BlockSpec(shape, lambda *_: zeros, pipeline_mode=pl.Buffered(buffers))


def move_pairs(hl):
    pairs = []
    for core in range(2):
        for place in range(2 * hl):
            source = core * 2 * hl + place
            target = ((place // hl) * 2 + core) * hl + place % hl
            pairs.append((source, target))
    return pairs


def moved(value):
    return lax.ppermute(value, MOVE, move_pairs(lax.axis_size("hl")))


def moved_back(value):
    pairs = [(b, a) for a, b in move_pairs(lax.axis_size("hl"))]
    return lax.ppermute(value, MOVE, pairs)


def from_sub(value, step):
    size = lax.axis_size("hl") * 2
    return lax.ppermute(value, SUB, [((d + step) % size, d) for d in range(size)])


def to_sub(value, step):
    size = lax.axis_size("hl") * 2
    return lax.ppermute(value, SUB, [(d, (d + step) % size) for d in range(size)])


SWAP = [(0, 1), (1, 0)]


def across(value, bit):
    size = lax.axis_size("za")
    return lax.ppermute(value, "za", [(i, i ^ bit) for i in range(size)])


def place_kernel(half, where, own, by_zb, by_hh, both_low, both_high, out):
    zb = where[0]
    hh = where[1]
    out[0, zb, hh] = own[0]
    out[0, 1 - zb, hh] = by_zb[0]
    out[0, zb, 1 - hh] = by_hh[0]

    @pl.when(pl.program_id(0) < half)
    def _():
        out[0, 1 - zb, 1 - hh] = both_low[0]

    @pl.when(pl.program_id(0) >= half)
    def _():
        out[0, 1 - zb, 1 - hh] = both_high[0]


def gather_plane(shard):
    rows, columns = shard.shape
    size = lax.axis_size("za")
    half = size // 2
    held, order, bit = shard[None], [0], half
    while bit:
        held = jnp.concatenate([held, across(held, bit)], axis=0)
        order = order + [at ^ bit for at in order]
        bit //= 2
    by_zb = lax.ppermute(held, "zb", SWAP)
    by_hh = lax.ppermute(held, "hh", SWAP)
    both_low = lax.ppermute(by_zb[:half], "hh", SWAP)
    both_high = lax.ppermute(by_hh[half:], "zb", SWAP)
    where = [lax.axis_index("zb"), lax.axis_index("hh")]
    where += [lax.axis_index("za") ^ at for at in order]
    where = jnp.stack(where).astype(jnp.int32)
    block = (1, rows, columns)
    full = pl.pallas_call(
        functools.partial(place_kernel, half),
        grid_spec=pltpu.PrefetchScalarGridSpec(
            num_scalar_prefetch=1,
            grid=(size,),
            in_specs=[pl.BlockSpec(block, lambda i, w: (i, 0, 0))] * 3
            + [
                pl.BlockSpec(block, lambda i, w: (jnp.minimum(i, half - 1), 0, 0)),
                pl.BlockSpec(block, lambda i, w: (jnp.maximum(i - half, 0), 0, 0)),
            ],
            out_specs=pl.BlockSpec((1, 2, 2, rows, columns), lambda i, w: (w[2 + i], 0, 0, 0, 0)),
        ),
        out_shape=jax.ShapeDtypeStruct((size, 2, 2, rows, columns), shard.dtype),
        compiler_params=params(),
        cost_estimate=cost(0, size * 4 * rows * columns * 4),
        name="place",
    )(where, held, by_zb, by_hh, both_low, both_high)
    return full.reshape(size * 4 * rows, columns)


def reduce_plane(weights):
    size = lax.axis_size("za")
    half = size // 2
    zb, hh = lax.axis_index("zb"), lax.axis_index("hh")

    def piece(dz, dh):
        parts = []
        for terms in weights:
            part = 0.0
            for term in terms:
                rows = term.shape[0] // (size * 4)
                view = term.reshape(size, 2, 2, rows, term.shape[1])
                at = (0, zb ^ dz, hh ^ dh, 0, 0)
                cut = lax.dynamic_slice(view, at, (size, 1, 1, rows, term.shape[1]))
                part = part + cut.reshape(size, rows, -1).astype(F32)
            parts.append(part)
        return parts[0] if len(parts) == 1 else jnp.concatenate(parts, axis=2)

    far = piece(1, 1).astype(BF16)
    low = lax.ppermute(far[:half], "hh", SWAP)
    high = lax.ppermute(far[half:], "zb", SWAP)
    none = jnp.zeros_like(low)
    to_zb = (piece(1, 0) + jnp.concatenate([low, none]).astype(F32)).astype(BF16)
    to_hh = (piece(0, 1) + jnp.concatenate([none, high]).astype(F32)).astype(BF16)
    from_zb = lax.ppermute(to_zb, "zb", SWAP)
    from_hh = lax.ppermute(to_hh, "hh", SWAP)
    total = piece(0, 0) + from_zb.astype(F32) + from_hh.astype(F32)
    mine, bit = lax.axis_index("za"), 1
    while bit < size:
        total = total.astype(BF16)
        pairs = total.reshape(total.shape[0] // 2, 2, *total.shape[1:])
        place = (mine // bit) % 2
        keep = lax.dynamic_index_in_dim(pairs, place, 1, keepdims=False)
        send = lax.dynamic_index_in_dim(pairs, 1 - place, 1, keepdims=False)
        total = keep.astype(F32) + across(send, bit).astype(F32)
        bit *= 2
    return total[0].astype(BF16)


def norm(values):
    centred = values - jnp.mean(values, axis=-1, keepdims=True)
    variance = jnp.mean(centred * centred, axis=-1, keepdims=True)
    inverse = lax.rsqrt(variance + EPSILON)
    return centred * inverse, inverse


def pick(member, table):
    return dot(member, table, precision=HIGHEST)


def first_norm_kernel(x, member, adaptive, out):
    width = x.shape[1]
    normed, _ = norm(x[...].astype(F32))
    shift = pick(member[...], adaptive[:, :width])
    scale = pick(member[...], adaptive[:, width : 2 * width])
    out[...] = (normed * (1.0 + scale) + shift).astype(BF16)


def first_norm(x, member, adaptive):
    rows, width = x.shape
    tile = min(256, rows)
    return pl.pallas_call(
        first_norm_kernel,
        grid=(rows // tile,),
        out_shape=jax.ShapeDtypeStruct((rows, width), BF16),
        in_specs=[
            pl.BlockSpec((tile, width), lambda i: (i, 0)),
            pl.BlockSpec((tile, 8), lambda i: (i, 0)),
            whole(adaptive.shape),
        ],
        out_specs=pl.BlockSpec((tile, width), lambda i: (i, 0)),
        compiler_params=params(),
        cost_estimate=cost(rows * width * 40, rows * width * 4),
        name="first_norm",
    )(x, member, adaptive)


def turn(values, cosine, sine):
    lanes = values.shape[1]
    place = lax.broadcasted_iota(jnp.int32, (1, 128), 1) % HEAD_DIM
    first = place < HEAD_DIM // 2
    parts = []
    for at in range(0, lanes, 128):
        part = values[:, at : at + 128]
        ahead = pltpu.roll(part, 128 - HEAD_DIM // 2, 1)
        behind = pltpu.roll(part, HEAD_DIM // 2, 1)
        swapped = jnp.where(first, ahead, behind)
        parts.append(part * cosine + swapped * sine)
    return parts[0] if len(parts) == 1 else jnp.concatenate(parts, axis=1)


def project_kernel(place, a, w, cosine, sine, out):
    kind = lax.rem(pl.program_id(0), 3)
    product = dot(a[...], w[...])

    @pl.when(kind == 2)
    def _():
        out[...] = product.astype(BF16)

    @pl.when(kind != 2)
    def _():
        scale = jnp.where(kind == 0, HEAD_DIM**-0.5, 1.0)
        out[...] = (turn(product, cosine[...], sine[...]) * scale).astype(BF16)


def project(place, a, w, cosine, sine, lanes):
    rows, width = a.shape
    columns = w.shape[1]
    return pl.pallas_call(
        project_kernel,
        grid_spec=pltpu.PrefetchScalarGridSpec(
            num_scalar_prefetch=1,
            grid=(columns // lanes,),
            in_specs=[
                pl.BlockSpec((rows, width), lambda i, s: (0, 0)),
                pl.BlockSpec((width, lanes), lambda i, s: (0, i)),
                pl.BlockSpec((rows, 128), lambda i, s: (s[0], 0)),
                pl.BlockSpec((rows, 128), lambda i, s: (s[0], 0)),
            ],
            out_specs=pl.BlockSpec((rows, lanes), lambda i, s: (0, i)),
        ),
        out_shape=jax.ShapeDtypeStruct((rows, columns), BF16),
        compiler_params=params(),
        cost_estimate=cost(2 * rows * width * columns, rows * (width + columns) * 2),
        name="project",
    )(place, a, w, cosine, sine)


def lane_mask(lanes, head):
    return lax.broadcasted_iota(jnp.int32, (1, lanes), 1) // HEAD_DIM == head


def piece_start(place, piece, pieces, rows):
    return pl.multiple_of(lax.rem(place[0] + piece, pieces) * rows, rows)


def flip(values):
    return jnp.transpose(values.astype(F32))


def attend_kernel(pieces, heads, step_q, step_k, place, bounds, seg_col, seg_row, *refs):
    inputs = refs[: 3 * pieces]
    outs = refs[3 * pieces : 4 * pieces]
    lse, q_all, k_all, v_flip, o_all, total = refs[4 * pieces :]
    rows, lanes = inputs[0].shape
    for piece in range(pieces):
        start = piece_start(place, piece, pieces, rows)
        q_all[pl.ds(start, rows), :] = inputs[3 * piece][...]
        k_all[pl.ds(start, rows), :] = inputs[3 * piece + 1][...]
        v_flip[:, pl.ds(start, rows)] = flip(inputs[3 * piece + 2][...]).astype(BF16)

    def one_block(i, _):
        at = pl.multiple_of(i * step_q, step_q)
        query = q_all[pl.ds(at, step_q), :]
        masked = [
            jnp.where(lane_mask(lanes, head), query, jnp.zeros_like(query)) for head in range(heads)
        ]
        seg_q = seg_row[0:1, pl.ds(at, step_q)]
        total[...] = jnp.zeros_like(total)

        def one_key(j, carry):
            highest, sums = carry
            key_at = pl.multiple_of(j * step_k, step_k)
            key = k_all[pl.ds(key_at, step_k), :]
            same = seg_col[pl.ds(key_at, step_k), :] == seg_q
            new_highest, new_sums = [], []
            for head in range(heads):
                scores = jnp.where(same, dot(key, masked[head], NT), MASKED)
                top = jnp.maximum(highest[head], jnp.max(scores, axis=0, keepdims=True))
                weight = jnp.exp(scores - top)
                fade = jnp.exp(highest[head] - top)
                new_highest.append(top)
                new_sums.append(sums[head] * fade + jnp.sum(weight, axis=0, keepdims=True))
                span = pl.ds(head * HEAD_DIM, HEAD_DIM)
                value = v_flip[span, pl.ds(key_at, step_k)]
                total[span, :] = total[span, :] * fade + dot(value, weight.astype(BF16))
            return tuple(new_highest), tuple(new_sums)

        empty = tuple(jnp.full((1, step_q), MASKED, F32) for _ in range(heads))
        zero = tuple(jnp.zeros((1, step_q), F32) for _ in range(heads))
        highest, sums = lax.fori_loop(bounds[0, i], bounds[1, i], one_key, (empty, zero))
        for head in range(heads):
            span = pl.ds(head * HEAD_DIM, HEAD_DIM)
            total[span, :] = total[span, :] / sums[head]
            lse[0, head : head + 1, pl.ds(at, step_q)] = highest[head] + jnp.log(sums[head])
        o_all[pl.ds(at, step_q), :] = flip(total[...]).astype(BF16)
        return 0

    lax.fori_loop(0, q_all.shape[0] // step_q, one_block, 0)
    for piece in range(pieces):
        start = piece_start(place, piece, pieces, rows)
        outs[piece][...] = o_all[pl.ds(start, rows), :]


def attend(place, bounds, seg_col, seg_row, qkv, lanes, step_q, step_k):
    pieces = len(qkv)
    rows, columns = qkv[0].shape
    groups = columns // (3 * lanes)
    heads = lanes // HEAD_DIM
    frames = rows * pieces
    specs = []
    for _ in range(pieces):
        for kind in range(3):
            specs.append(pl.BlockSpec((rows, lanes), lambda g, kind=kind: (0, 3 * g + kind)))
    smem = pl.BlockSpec(memory_space=pltpu.SMEM)
    area = frames * frames // 2 * heads * groups
    results = pl.pallas_call(
        functools.partial(attend_kernel, pieces, heads, step_q, step_k),
        grid=(groups,),
        out_shape=[jax.ShapeDtypeStruct((rows, groups * lanes), BF16)] * pieces
        + [jax.ShapeDtypeStruct((groups, heads, frames), F32)],
        in_specs=[smem, smem, whole(seg_col.shape), whole(seg_row.shape)] + specs,
        out_specs=[pl.BlockSpec((rows, lanes), lambda g: (0, g))] * pieces
        + [pl.BlockSpec((1, heads, frames), lambda g: (g, 0, 0))],
        scratch_shapes=[
            pltpu.VMEM((frames, lanes), BF16),
            pltpu.VMEM((frames, lanes), BF16),
            pltpu.VMEM((lanes, frames), BF16),
            pltpu.VMEM((frames, lanes), BF16),
            pltpu.VMEM((lanes, step_q), F32),
        ],
        compiler_params=params(),
        cost_estimate=cost(area * 4 * 256, frames * columns * 4, area),
        name="attend",
    )(place, bounds, seg_col, seg_row, *[array for array in qkv for _ in range(3)])
    return results[:pieces], results[pieces]


def attend_back_kernel(pieces, heads, step_q, step_k, place, bounds, seg_col, seg_row, *refs):
    inputs = refs[: 5 * pieces]
    lse, cosine, sine = refs[5 * pieces : 5 * pieces + 3]
    outs = refs[5 * pieces + 3 : 6 * pieces + 3]
    q_all, k_all, v_all, o_all, do_all, k_flip, dq_all, dk_all, dv_all, total = refs[6 * pieces + 3 :]
    rows, lanes = inputs[0].shape
    for piece in range(pieces):
        start = piece_start(place, piece, pieces, rows)
        span = pl.ds(start, rows)
        for array, ref in zip((q_all, k_all, v_all, o_all, do_all), inputs[5 * piece : 5 * piece + 5]):
            array[span, :] = ref[...]
        k_flip[:, span] = flip(inputs[5 * piece + 1][...]).astype(BF16)
    dk_all[...] = jnp.zeros_like(dk_all)
    dv_all[...] = jnp.zeros_like(dv_all)
    head_rows = lax.broadcasted_iota(jnp.int32, (8, lanes), 0)
    head_lanes = lax.broadcasted_iota(jnp.int32, (8, lanes), 1) // HEAD_DIM
    head_sum = (head_rows == head_lanes).astype(BF16)

    def one_block(i, _):
        at = pl.multiple_of(i * step_q, step_q)
        block = pl.ds(at, step_q)
        query = q_all[block, :]
        grad = do_all[block, :]
        queries, grads = [], []
        for head in range(heads):
            keep = lane_mask(lanes, head)
            queries.append(jnp.where(keep, query, jnp.zeros_like(query)))
            grads.append(jnp.where(keep, grad, jnp.zeros_like(grad)))
        stacked_queries = jnp.concatenate(queries, axis=0)
        stacked_grads = jnp.concatenate(grads, axis=0)
        product = grad.astype(F32) * o_all[block, :].astype(F32)
        coarse = product.astype(BF16)
        fine = (product - coarse.astype(F32)).astype(BF16)
        centre = dot(head_sum, coarse, NT) + dot(head_sum, fine, NT)
        seg_q = seg_row[0:1, block]
        total[...] = jnp.zeros_like(total)

        def one_key(j, _):
            key_at = pl.multiple_of(j * step_k, step_k)
            span = pl.ds(key_at, step_k)
            key = k_all[span, :]
            value = v_all[span, :]
            same = seg_col[span, :] == seg_q
            weights, slopes = [], []
            for head in range(heads):
                scores = dot(key, queries[head], NT) - lse[0, head : head + 1, block]
                weight = jnp.exp(jnp.where(same, scores, MASKED))
                slope = dot(value, grads[head], NT) - centre[head : head + 1, :]
                slope = (weight * slope).astype(BF16)
                weights.append(weight.astype(BF16))
                slopes.append(slope)
                lines = pl.ds(head * HEAD_DIM, HEAD_DIM)
                total[lines, :] += dot(k_flip[lines, span], slope)
            dv_all[span, :] += dot(jnp.concatenate(weights, axis=1), stacked_grads)
            dk_all[span, :] += dot(jnp.concatenate(slopes, axis=1), stacked_queries)
            return 0

        lax.fori_loop(bounds[0, i], bounds[1, i], one_key, 0)
        dq_all[block, :] = flip(total[...]) * HEAD_DIM**-0.5
        return 0

    lax.fori_loop(0, q_all.shape[0] // step_q, one_block, 0)
    for piece in range(pieces):
        start = piece_start(place, piece, pieces, rows)
        span = pl.ds(start, rows)
        cos = cosine[span, :]
        sin = -sine[span, :]
        outs[piece][:, 0:lanes] = turn(dq_all[span, :], cos, sin).astype(BF16)
        outs[piece][:, lanes : 2 * lanes] = turn(dk_all[span, :], cos, sin).astype(BF16)
        outs[piece][:, 2 * lanes : 3 * lanes] = dv_all[span, :].astype(BF16)


def attend_back(
    place, bounds, seg_col, seg_row, qkv, attended, grads, lse, cosine, sine, lanes, group, step_q, step_k
):
    pieces = len(qkv)
    rows = qkv[0].shape[0]
    heads = lanes // HEAD_DIM
    frames = rows * pieces
    specs, arrays = [], []
    for piece in range(pieces):
        for kind in range(3):
            specs.append(pl.BlockSpec((rows, lanes), lambda i, kind=kind: (0, 3 * group + kind)))
            arrays.append(qkv[piece])
        for array in (attended[piece], grads[piece]):
            specs.append(pl.BlockSpec((rows, lanes), lambda i: (0, group)))
            arrays.append(array)
    smem = pl.BlockSpec(memory_space=pltpu.SMEM)
    area = frames * frames // 2 * heads
    return pl.pallas_call(
        functools.partial(attend_back_kernel, pieces, heads, step_q, step_k),
        grid=(1,),
        out_shape=[jax.ShapeDtypeStruct((rows, 3 * lanes), BF16)] * pieces,
        in_specs=[smem, smem, whole(seg_col.shape, 1), whole(seg_row.shape, 1)]
        + specs
        + [
            pl.BlockSpec((1, heads, frames), lambda i: (group, 0, 0)),
            whole(cosine.shape, 1),
            whole(sine.shape, 1),
        ],
        out_specs=[whole((rows, 3 * lanes), 1)] * pieces,
        scratch_shapes=[pltpu.VMEM((frames, lanes), BF16)] * 5
        + [pltpu.VMEM((lanes, frames), BF16)]
        + [pltpu.VMEM((frames, lanes), F32)] * 3
        + [pltpu.VMEM((lanes, step_q), F32)],
        compiler_params=params(),
        cost_estimate=cost(area * 10 * 256, frames * lanes * 16, area),
        name="attend_back",
    )(place, bounds, seg_col, seg_row, *arrays, lse, cosine, sine)


def gelu_pair(h):
    root = math.sqrt(2.0 / math.pi)
    square = h * h
    bend = jnp.tanh(root * h * (1.0 + 0.044715 * square))
    half = 0.5 * (1.0 + bend)
    slope = half + 0.5 * h * (1.0 - bend * bend) * (root * (1.0 + 0.134145 * square))
    return h * half, slope


def middle_kernel(pieces, *refs):
    x, member, member_flip, adaptive, dy = refs[:5]
    refs = refs[5:]
    attended, refs = refs[:pieces], refs[pieces:]
    w_out, refs = refs[:pieces], refs[pieces:]
    w_up, refs = refs[:pieces], refs[pieces:]
    w_down, refs = refs[:pieces], refs[pieces:]
    mixed, dx2, a2_out, d2_out, d1_out, dadaptive = refs[:6]
    refs = refs[6:]
    active, refs = refs[:pieces], refs[pieces:]
    dhidden, refs = refs[:pieces], refs[pieces:]
    dattended = refs[:pieces]
    width = x.shape[1]
    here = member[...]
    gate1, shift2, scale2, gate2 = (
        pick(here, adaptive[:, n * width : (n + 1) * width]) for n in (2, 3, 4, 5)
    )
    branch1 = sum(dot(attended[p][...], w_out[p][...], NT) for p in range(pieces))
    x2 = x[...].astype(F32) + gate1 * branch1
    n2, r2 = norm(x2)
    a2 = (n2 * (1.0 + scale2) + shift2).astype(BF16)
    a2_out[...] = a2
    branch2 = jnp.zeros_like(x2)
    slopes = []
    for p in range(pieces):
        value, slope = gelu_pair(dot(a2, w_up[p][...]))
        value = value.astype(BF16)
        active[p][...] = value
        slopes.append(slope)
        branch2 = branch2 + dot(value, w_down[p][...], NT)
    mixed[...] = (x2 + gate2 * branch2).astype(BF16)
    upstream = dy[...].astype(F32)
    d2 = (upstream * gate2).astype(BF16)
    d2_out[...] = d2
    da2 = jnp.zeros_like(x2)
    for p in range(pieces):
        dh = (dot(d2, w_down[p][...]) * slopes[p]).astype(BF16)
        dhidden[p][...] = dh
        da2 = da2 + dot(dh, w_up[p][...], NT)
    u2 = da2 * (1.0 + scale2)
    back = upstream + r2 * (
        u2 - jnp.mean(u2, axis=-1, keepdims=True) - n2 * jnp.mean(u2 * n2, axis=-1, keepdims=True)
    )
    dx2[...] = back
    d1 = (back * gate1).astype(BF16)
    d1_out[...] = d1
    for p in range(pieces):
        dattended[p][...] = dot(d1, w_out[p][...]).astype(BF16)

    @pl.when(pl.program_id(0) == 0)
    def _():
        dadaptive[...] = jnp.zeros_like(dadaptive)

    for n, term in enumerate((back * branch1, da2, da2 * n2, upstream * branch2)):
        dadaptive[:, n * width : (n + 1) * width] += pick(member_flip[...], term)


def middle(x, member, member_flip, adaptive, dy, attended, weights):
    pieces = len(attended)
    rows, width = x.shape
    head_columns = attended[0].shape[1]
    hidden = 2 * head_columns
    tile = min(256, rows)

    def tiled(columns):
        return pl.BlockSpec((tile, columns), lambda i: (i, 0))

    def shaped(columns, kind):
        return jax.ShapeDtypeStruct((rows, columns), kind)

    def resident(columns, at):
        return pl.BlockSpec((width, columns), lambda i: (0, at), pipeline_mode=pl.Buffered(1))

    cuts = [resident(head_columns, 4), resident(hidden, 0), resident(hidden, 1)]
    work = 2 * rows * width * pieces * (3 * hidden * 2 + head_columns * 2)
    results = pl.pallas_call(
        functools.partial(middle_kernel, pieces),
        grid=(rows // tile,),
        in_specs=[
            tiled(width),
            tiled(8),
            pl.BlockSpec((8, tile), lambda i: (0, i)),
            whole(adaptive.shape, 1),
            tiled(width),
        ]
        + [tiled(head_columns)] * pieces
        + [cut for cut in cuts for _ in range(pieces)],
        out_shape=[
            shaped(width, BF16),
            shaped(width, F32),
            shaped(width, BF16),
            shaped(width, BF16),
            shaped(width, BF16),
            jax.ShapeDtypeStruct((8, 4 * width), F32),
        ]
        + [shaped(hidden, BF16)] * (2 * pieces)
        + [shaped(head_columns, BF16)] * pieces,
        out_specs=[tiled(width)] * 5
        + [whole((8, 4 * width))]
        + [tiled(hidden)] * (2 * pieces)
        + [tiled(head_columns)] * pieces,
        compiler_params=params(),
        cost_estimate=cost(work, rows * width * 30, rows * hidden * pieces),
        name="middle",
    )(x, member, member_flip, adaptive, dy, *attended, *weights, *weights, *weights)
    head, rest = results[:6], results[6:]
    return head, rest[:pieces], rest[pieces : 2 * pieces], rest[2 * pieces :]


def last_kernel(groups, arrivals, *refs):
    x, member, member_flip, adaptive, dx2 = refs[:5]
    refs = refs[5:]
    arrived, refs = refs[:arrivals], refs[arrivals:]
    slopes, refs = refs[:groups], refs[groups:]
    weights, refs = refs[:groups], refs[groups:]
    grad, dadaptive = refs
    width = x.shape[1]
    normed, inverse = norm(x[...].astype(F32))
    scale = pick(member[...], adaptive[:, width : 2 * width])
    da1 = sum(dot(slopes[g][...], weights[g][...], NT) for g in range(groups))
    for piece in arrived:
        da1 = da1 + piece[...].astype(F32)
    u1 = da1 * (1.0 + scale)
    back = inverse * (
        u1
        - jnp.mean(u1, axis=-1, keepdims=True)
        - normed * jnp.mean(u1 * normed, axis=-1, keepdims=True)
    )
    grad[...] = (dx2[...] + back).astype(BF16)

    @pl.when(pl.program_id(0) == 0)
    def _():
        dadaptive[...] = jnp.zeros_like(dadaptive)

    dadaptive[:, :width] += pick(member_flip[...], da1)
    dadaptive[:, width:] += pick(member_flip[...], da1 * normed)


def last(x, member, member_flip, adaptive, dx2, arrived, slopes, weights):
    rows, width = x.shape
    tile = min(256, rows)

    def tiled(columns):
        return pl.BlockSpec((tile, columns), lambda i: (i, 0))

    return pl.pallas_call(
        functools.partial(last_kernel, len(slopes), len(arrived)),
        grid=(rows // tile,),
        in_specs=[
            tiled(width),
            tiled(8),
            pl.BlockSpec((8, tile), lambda i: (0, i)),
            whole(adaptive.shape, 1),
            tiled(width),
        ]
        + [tiled(width)] * len(arrived)
        + [tiled(s.shape[1]) for s in slopes]
        + [
            pl.BlockSpec(
                (width, s.shape[1]), lambda i, g=g: (0, g), pipeline_mode=pl.Buffered(1)
            )
            for g, s in enumerate(slopes)
        ],
        out_shape=[
            jax.ShapeDtypeStruct((rows, width), BF16),
            jax.ShapeDtypeStruct((8, 2 * width), F32),
        ],
        out_specs=[tiled(width), whole((8, 2 * width))],
        compiler_params=params(),
        cost_estimate=cost(2 * rows * width * sum(s.shape[1] for s in slopes), rows * width * 12),
        name="last",
    )(x, member, member_flip, adaptive, dx2, *arrived, *slopes, *[weights] * len(slopes))


def time_vector(steps, width):
    halfway = width // 2
    rates = jnp.exp(jnp.arange(halfway, dtype=F32) * (-math.log(10000.0) / (halfway - 1)))
    angles = steps.astype(F32)[:, None] * rates[None, :]
    return jnp.concatenate([jnp.sin(angles), jnp.cos(angles)], axis=1)


def body(frames, clip_lengths, timesteps, w_qkv, w_out, w_up, w_down, w_ada, b_ada, grad_out):
    rows, width = frames.shape
    clips = clip_lengths.shape[0]
    pieces = lax.axis_size("hl") * 2
    group_rows = rows * pieces
    own_rows = w_qkv.shape[1]
    head_columns = width // pieces
    lanes = min(256, head_columns)
    groups = head_columns // lanes
    step = min(256, group_rows)
    place = lax.axis_index(SUB).astype(jnp.int32)

    qkv_shard = w_qkv.astype(BF16).reshape(3, own_rows, groups, lanes)
    qkv_shard = jnp.transpose(qkv_shard, (1, 2, 0, 3)).reshape(own_rows, groups * 3 * lanes)
    mlp_shard = jnp.concatenate(
        [w_up.astype(BF16), w_down.astype(BF16).T, w_out.astype(BF16).T], axis=1
    )
    lengths = moved(clip_lengths)
    shards = moved(jnp.concatenate([qkv_shard, mlp_shard], axis=1))
    x = moved(frames)
    qkv_full = gather_plane(shards[:, : 3 * head_columns])
    mlp_own = gather_plane(shards[:, 3 * head_columns :])

    def around(value):
        return [value] + [from_sub(value, step) for step in range(1, pieces)]

    mlp_full = around(mlp_own)

    condition = jax.nn.silu(time_vector(timesteps, width))
    columns = w_ada.shape[1]
    devices = [lax.axis_size(axis) for axis in ALL]
    za, zb, cores, hh, hl = devices
    table = (
        jnp.dot(condition, lax.reduce_precision(w_ada, 8, 7), precision=HIGHEST)
        + lax.reduce_precision(b_ada, 8, 7)[None, :]
    )
    table = table.reshape(za, zb, 1, hh, 1, clips, columns)
    table = jnp.broadcast_to(table, (za, zb, cores, hh, hl, clips, columns))
    table = lax.all_to_all(table.reshape(-1, clips, columns), ALL, 0, 0, tiled=True)
    adaptive = jnp.transpose(table, (1, 0, 2)).reshape(clips, -1)
    adaptive = jnp.pad(adaptive, ((0, 8 - clips), (0, 0)))

    ends = jnp.cumsum(lengths, dtype=jnp.int32)
    starts = ends - lengths
    index = jnp.arange(group_rows, dtype=jnp.int32)
    segment = jnp.sum((index[:, None] >= ends[None, :]).astype(jnp.int32), axis=1, dtype=jnp.int32)
    edges = jnp.concatenate([jnp.zeros((1,), jnp.int32), ends])
    begins = jnp.max(jnp.where(index[:, None] >= edges[None, :], edges[None, :], 0), axis=1)
    position = (index - begins).astype(F32)
    lane = jnp.arange(128, dtype=jnp.int32) % HEAD_DIM
    rates = jnp.exp((lane % (HEAD_DIM // 2)).astype(F32) * (-2.0 * math.log(10000.0) / HEAD_DIM))
    angles = position[:, None] * rates[None, :]
    cosine = jnp.cos(angles)
    sine = jnp.sin(angles) * jnp.where(lane < HEAD_DIM // 2, -1.0, 1.0)[None, :]
    seg_col = segment[:, None]
    seg_row = segment[None, :]
    block_first = jnp.arange(0, group_rows, step, dtype=jnp.int32)
    first_seg = jnp.sum((block_first[:, None] >= ends[None, :]).astype(jnp.int32), axis=1)
    last_seg = jnp.sum((block_first[:, None] + (step - 1) >= ends[None, :]).astype(jnp.int32), axis=1)
    closing = jnp.concatenate([ends, jnp.full((1,), group_rows, jnp.int32)])
    low_at = jnp.sum(jnp.where(first_seg[:, None] == jnp.arange(clips + 1)[None, :], edges[None, :], 0), axis=1)
    high_at = jnp.sum(jnp.where(last_seg[:, None] == jnp.arange(clips + 1)[None, :], closing[None, :], 0), axis=1)
    bounds = jnp.stack([low_at // step, (high_at + step - 1) // step]).astype(jnp.int32)
    own_index = place * rows + jnp.arange(rows, dtype=jnp.int32)
    member = ((own_index[:, None] >= starts[None, :]) & (own_index[:, None] < ends[None, :])).astype(F32)
    member = jnp.pad(member, ((0, 0), (0, 8 - clips)))
    member_flip = member.T

    a1 = first_norm(x, member, adaptive)
    dy = moved(lax.optimization_barrier((grad_out, a1))[0])
    a1_all = around(a1)
    places = [((place + piece) % pieces).reshape(1) for piece in range(pieces)]
    qkv = [
        project(places[piece], a1_all[piece], qkv_full, cosine, sine, lanes)
        for piece in range(pieces)
    ]
    at_place = place.reshape(1)
    attended, lse = attend(at_place, bounds, seg_col, seg_row, qkv, lanes, step, step)
    attended_own = [attended[0]] + [
        from_sub_piece(attended, step_) for step_ in range(1, pieces)
    ]

    head, active, dhidden, dattended = middle(
        x, member, member_flip, adaptive, dy, attended_own, mlp_full
    )
    mixed, dx2, a2, d2, d1, dada_late = head
    grads_attended = [dattended[0]] + [
        from_sub_piece(dattended, step_) for step_ in range(1, pieces)
    ]
    mixed_back = moved_back(mixed)

    def summed(left, right):
        parts = [dot(left, part, TN).astype(BF16) for part in right]
        return [parts[0]] + [to_sub(parts[step], step) for step in range(1, pieces)]

    late = reduce_plane([summed(a2, dhidden), summed(d2, active), summed(d1, attended_own)])
    late = moved_back(late)
    hidden_columns = w_up.shape[1]
    grad_up = late[:, :hidden_columns]
    grad_down = late[:, hidden_columns : 2 * hidden_columns]
    grad_outw = late[:, 2 * hidden_columns :]

    slopes, grad_groups = [], []
    for group in range(groups):
        dqkv = attend_back(
            at_place, bounds, seg_col, seg_row, qkv, attended, grads_attended, lse, cosine, sine,
            lanes, group, step, step,
        )
        slopes.append(dqkv)
        total = sum(dot(a1_all[piece], dqkv[piece], TN) for piece in range(pieces)).astype(BF16)
        grad_groups.append(moved_back(reduce_plane([[total]])))
    arrived = []
    for piece in range(1, pieces):
        part = sum(
            dot(slopes[g][piece], qkv_full[:, 3 * lanes * g : 3 * lanes * (g + 1)], NT)
            for g in range(groups)
        ).astype(BF16)
        arrived.append(to_sub(part, piece))
    grad_frames, dada_early = last(
        x, member, member_flip, adaptive, dx2, arrived, [s[0] for s in slopes], qkv_full
    )
    grad_frames = moved_back(grad_frames).astype(F32)

    dadaptive = jnp.concatenate([dada_early, dada_late], axis=1)[:clips]
    dadaptive = jnp.transpose(dadaptive.reshape(clips, -1, columns), (1, 0, 2))
    dadaptive = lax.all_to_all(dadaptive, ALL, 0, 0, tiled=True)
    dadaptive = dadaptive.reshape(za, zb, cores, hh, hl, clips, columns)
    dadaptive = jnp.sum(dadaptive, axis=(2, 4)).reshape(-1, columns)
    grad_ada = dot(condition, dadaptive, TN, HIGHEST)
    grad_bias = jnp.sum(dadaptive, axis=0)

    grad_qkv = jnp.stack(grad_groups, axis=1).reshape(own_rows, groups, 3, lanes)
    grad_qkv = jnp.transpose(grad_qkv, (2, 0, 1, 3)).reshape(w_qkv.shape).astype(F32)
    return (
        mixed_back,
        grad_frames,
        grad_qkv,
        grad_outw.astype(F32).T,
        grad_up.astype(F32),
        grad_down.astype(F32).T,
        grad_ada,
        grad_bias,
    )


def from_sub_piece(parts, step):
    pieces = len(parts)
    return from_sub(parts[pieces - step], step)


def solution(mesh):
    clip, head = mesh.shape["clip"], mesh.shape["head"]
    fine = Mesh(mesh.devices.reshape(clip // 4, 2, 2, 2, head // 2), ALL)
    by_clip = ("za", "zb", "core")
    by_head = ("hh", "hl")
    everywhere = by_clip + by_head
    placed = (
        P(everywhere, None),
        P(by_clip),
        P(),
        P(None, by_clip, by_head),
        P(by_head, by_clip),
        P(by_clip, by_head),
        P(by_head, by_clip),
        P(None, everywhere),
        P(everywhere),
        P(everywhere, None),
    )
    return jax.shard_map(
        body,
        mesh=fine,
        in_specs=placed,
        out_specs=(
            P(everywhere, None),
            P(everywhere, None),
            P(None, by_clip, by_head),
            P(by_head, by_clip),
            P(by_clip, by_head),
            P(by_head, by_clip),
            P(None, everywhere),
            P(everywhere),
        ),
        check_vma=False,
    )
```

```python
import functools
import math

import jax
import jax.numpy as jnp
from jax import lax
from jax.experimental import pallas as pl
from jax.experimental.pallas import tpu as pltpu
from jax.sharding import Mesh
from jax.sharding import PartitionSpec as P

HEAD_DIM = 64
HEADS = 16
HIGHEST = lax.Precision.HIGHEST
MASKED = -1e30
EPSILON = 1e-06
VMEM_LIMIT = 60 * 1024 * 1024
F32 = jnp.float32
BF16 = jnp.bfloat16

ALL = ("za", "zb", "core", "hh", "hl")
MOVE = ("core", "hh", "hl")
SUB = ("core", "hl")

NT = (((1,), (1,)), ((), ()))
NN = (((1,), (0,)), ((), ()))
TN = (((0,), (0,)), ((), ()))


def dot(a, b, dims=NN, precision=None):
    return lax.dot_general(a, b, dims, precision=precision, preferred_element_type=F32)


def params(**more):
    return pltpu.CompilerParams(vmem_limit_bytes=VMEM_LIMIT, **more)


def cost(flops, bytes_accessed, transcendentals=0):
    return pl.CostEstimate(
        flops=int(flops), bytes_accessed=int(bytes_accessed), transcendentals=int(transcendentals)
    )


def whole(shape, buffers=None):
    zeros = (0,) * len(shape)
    if buffers is None:
        return pl.BlockSpec(shape, lambda *_: zeros)
    return pl.BlockSpec(shape, lambda *_: zeros, pipeline_mode=pl.Buffered(buffers))


def moved(value):
    stays = lax.axis_index("core") == lax.axis_index("hh")
    return jnp.where(stays, value, lax.ppermute(value, ("core", "hh"), [(1, 2), (2, 1)]))


def from_sub(value, step):
    size = lax.axis_size("hl") * 2
    return lax.ppermute(value, SUB, [((d + step) % size, d) for d in range(size)])


def to_sub(value, step):
    size = lax.axis_size("hl") * 2
    return lax.ppermute(value, SUB, [(d, (d + step) % size) for d in range(size)])


SWAP = [(0, 1), (1, 0)]


def across(value, bit):
    size = lax.axis_size("za")
    return lax.ppermute(value, "za", [(i, i ^ bit) for i in range(size)])


def place_kernel(half, where, own, by_zb, by_hh, both_low, both_high, out):
    zb = where[0]
    hh = where[1]
    out[0, zb, hh] = own[0]
    out[0, 1 - zb, hh] = by_zb[0]
    out[0, zb, 1 - hh] = by_hh[0]

    @pl.when(pl.program_id(0) < half)
    def _():
        out[0, 1 - zb, 1 - hh] = both_low[0]

    @pl.when(pl.program_id(0) >= half)
    def _():
        out[0, 1 - zb, 1 - hh] = both_high[0]


def gather_line(shard):
    return jnp.stack([shard] + [across(shard, bits) for bits in range(1, lax.axis_size("za"))])


def gather_near(held):
    return held, lax.ppermute(held, "zb", SWAP), lax.ppermute(held, "hh", SWAP)


def gather_far(held, by_zb, by_hh):
    half = held.shape[0] // 2
    both_low = lax.ppermute(by_zb[:half], "hh", SWAP)
    both_high = lax.ppermute(by_hh[half:], "zb", SWAP)
    return held, by_zb, by_hh, both_low, both_high


def gathered(held, by_zb, by_hh, both_low, both_high):
    size, rows, columns = held.shape
    half = size // 2
    where = [lax.axis_index("zb"), lax.axis_index("hh")]
    where += [lax.axis_index("za") ^ bits for bits in range(size)]
    where = jnp.stack(where).astype(jnp.int32)
    block = (1, rows, columns)
    full = pl.pallas_call(
        functools.partial(place_kernel, half),
        grid_spec=pltpu.PrefetchScalarGridSpec(
            num_scalar_prefetch=1,
            grid=(size,),
            in_specs=[pl.BlockSpec(block, lambda i, w: (i, 0, 0))] * 3
            + [
                pl.BlockSpec(block, lambda i, w: (jnp.minimum(i, half - 1), 0, 0)),
                pl.BlockSpec(block, lambda i, w: (jnp.maximum(i - half, 0), 0, 0)),
            ],
            out_specs=pl.BlockSpec((1, 2, 2, rows, columns), lambda i, w: (w[2 + i], 0, 0, 0, 0)),
        ),
        out_shape=jax.ShapeDtypeStruct((size, 2, 2, rows, columns), held.dtype),
        compiler_params=params(),
        cost_estimate=cost(0, size * 4 * rows * columns * 4),
        name="place",
    )(where, held, by_zb, by_hh, both_low, both_high)
    return full.reshape(size * 4 * rows, columns)


FOUR = ((0, 0), (1, 0), (0, 1), (1, 1))


def cut_kernel(counts, where, *refs):
    outs = refs[-4:]
    zb, hh = where[0], where[1]
    first = start = 0
    for count in counts:
        terms = refs[first : first + count]
        columns = terms[0].shape[-1]
        for out, (dz, dh) in zip(outs, FOUR):
            z, h = lax.rem(zb + dz, 2), lax.rem(hh + dh, 2)
            part = terms[0][0, z, h]
            if count > 1:
                part = sum(term[0, z, h].astype(F32) for term in terms).astype(BF16)
            out[0, :, start : start + columns] = part
        first += count
        start += columns


def cut_plane(weights):
    size = lax.axis_size("za")
    where = jnp.stack([lax.axis_index("zb"), lax.axis_index("hh")]).astype(jnp.int32)
    terms = [term for group in weights for term in group]
    rows = terms[0].shape[0] // (size * 4)
    total = sum(group[0].shape[1] for group in weights)
    return pl.pallas_call(
        functools.partial(cut_kernel, [len(group) for group in weights]),
        grid_spec=pltpu.PrefetchScalarGridSpec(
            num_scalar_prefetch=1,
            grid=(size,),
            in_specs=[
                pl.BlockSpec((1, 2, 2, rows, term.shape[1]), lambda i, w: (i, 0, 0, 0, 0))
                for term in terms
            ],
            out_specs=[pl.BlockSpec((1, rows, total), lambda i, w: (i, 0, 0))] * 4,
        ),
        out_shape=[jax.ShapeDtypeStruct((size, rows, total), BF16)] * 4,
        compiler_params=params(),
        cost_estimate=cost(0, sum(2 * term.size for term in terms) + size * 8 * rows * total),
        name="cut",
    )(where, *[term.reshape(size, 2, 2, rows, -1) for term in terms])


def swap_plane(pieces):
    own, to_zb, to_hh, to_both = pieces
    from_both = lax.ppermute(to_both, ("zb", "hh"), [(0, 3), (1, 2), (2, 1), (3, 0)])
    from_hh = lax.ppermute(to_hh, "hh", SWAP)
    from_zb = lax.ppermute(to_zb, "zb", SWAP)
    return own, from_zb, from_hh, from_both


def cut_line(pieces):
    total = sum(piece.astype(F32) for piece in pieces).astype(BF16)
    mine = lax.axis_index("za")
    return [
        lax.dynamic_index_in_dim(total, mine ^ bits, 0, keepdims=False)
        for bits in range(total.shape[0])
    ]


def swap_line(cuts):
    return [cuts[0]] + [across(cut, bits) for bits, cut in enumerate(cuts) if bits]


def total_of(cuts):
    return sum(cut.astype(F32) for cut in cuts).astype(BF16)


def together(*values):
    return lax.optimization_barrier(values)


def norm(values):
    centred = values - jnp.mean(values, axis=-1, keepdims=True)
    variance = jnp.mean(centred * centred, axis=-1, keepdims=True)
    inverse = lax.rsqrt(variance + EPSILON)
    return centred * inverse, inverse


def pick(member, table):
    high = table.astype(BF16)
    rest = table - high.astype(F32)
    middle = rest.astype(BF16)
    low = (rest - middle.astype(F32)).astype(BF16)
    return dot(member, jnp.concatenate([high, middle, low, jnp.zeros_like(low)], axis=0))


def gather(member_flip, term):
    high = term.astype(BF16)
    low = (term - high.astype(F32)).astype(BF16)
    return (dot(member_flip, high) + dot(member_flip, low))[0:8]


def first_norm_kernel(x, member, adaptive, out):
    width = x.shape[1]
    normed, _ = norm(x[...].astype(F32))
    shift = pick(member[...], adaptive[:, :width])
    scale = pick(member[...], adaptive[:, width : 2 * width])
    out[...] = (normed * (1.0 + scale) + shift).astype(BF16)


def first_norm(x, member, adaptive):
    rows, width = x.shape
    tile = min(256, rows)
    return pl.pallas_call(
        first_norm_kernel,
        grid=(rows // tile,),
        out_shape=jax.ShapeDtypeStruct((rows, width), BF16),
        in_specs=[
            pl.BlockSpec((tile, width), lambda i: (i, 0)),
            pl.BlockSpec((tile, 32), lambda i: (i, 0)),
            whole(adaptive.shape),
        ],
        out_specs=pl.BlockSpec((tile, width), lambda i: (i, 0)),
        compiler_params=params(),
        cost_estimate=cost(rows * width * 40, rows * width * 4),
        name="first_norm",
    )(x, member, adaptive)


def turn(values, cosine, sine):
    lanes = values.shape[1]
    place = lax.broadcasted_iota(jnp.int32, (1, 128), 1) % HEAD_DIM
    first = place < HEAD_DIM // 2
    parts = []
    for at in range(0, lanes, 128):
        part = values[:, at : at + 128]
        ahead = pltpu.roll(part, 128 - HEAD_DIM // 2, 1)
        behind = pltpu.roll(part, HEAD_DIM // 2, 1)
        swapped = jnp.where(first, ahead, behind)
        parts.append(part * cosine + swapped * sine)
    return parts[0] if len(parts) == 1 else jnp.concatenate(parts, axis=1)


def project_kernel(lanes, place, a, w, cosine, sine, out):
    for start in range(0, w.shape[1], 3 * lanes):
        products = dot(a[...], w[:, start : start + 3 * lanes])
        for at in range(0, 3 * lanes, 128):
            product = products[:, at : at + 128]
            kind = at // 128 % 3
            if kind < 2:
                product = turn(product, cosine[...], sine[...])
            if kind == 0:
                product = product * HEAD_DIM**-0.5
            out[:, start + at : start + at + 128] = product.astype(BF16)


def project(place, a, w, cosine, sine, lanes):
    rows, width = a.shape
    columns = w.shape[1]
    tile = min(256, rows)
    tiles = rows // tile
    return pl.pallas_call(
        functools.partial(project_kernel, lanes),
        grid_spec=pltpu.PrefetchScalarGridSpec(
            num_scalar_prefetch=1,
            grid=(tiles,),
            in_specs=[
                pl.BlockSpec((tile, width), lambda i, s: (i, 0)),
                whole(w.shape, 1),
                pl.BlockSpec((tile, 128), lambda i, s: (s[0] * tiles + i, 0)),
                pl.BlockSpec((tile, 128), lambda i, s: (s[0] * tiles + i, 0)),
            ],
            out_specs=pl.BlockSpec((tile, columns), lambda i, s: (i, 0)),
        ),
        out_shape=jax.ShapeDtypeStruct((rows, columns), BF16),
        compiler_params=params(),
        cost_estimate=cost(2 * rows * width * columns, rows * (width + columns) * 2),
        name="project",
    )(place, a, w, cosine, sine)


def lane_mask(lanes, head):
    return lax.broadcasted_iota(jnp.int32, (1, lanes), 1) // HEAD_DIM == head


def piece_start(place, piece, pieces, rows):
    return pl.multiple_of(lax.rem(place[0] + piece, pieces) * rows, rows)


def flip(values):
    return jnp.transpose(values.astype(F32))


def spread(ref, span, arrays):
    for at in range(0, ref.shape[1], 128):
        start = at // 384 * 128
        arrays[at // 128 % 3][span, start : start + 128] = ref[:, at : at + 128]


def each_width(count, limit, run):
    for width in range(1, limit + 1):

        @pl.when(count == width)
        def _(width=width):
            run(width)


def attend_kernel(pieces, heads, step, place, bounds, seg_col, seg_row, *refs):
    inputs = refs[:pieces]
    outs = refs[pieces : 2 * pieces]
    lse, q_all, k_all, v_all, o_all, bias = refs[2 * pieces :]
    rows = inputs[0].shape[0]
    for piece in range(pieces):
        span = pl.ds(piece_start(place, piece, pieces, rows), rows)
        spread(inputs[piece], span, (q_all, k_all, v_all))
    frames, lanes = q_all.shape
    lane = lax.broadcasted_iota(jnp.int32, (1, 128), 1)

    def one_block(i, _):
        block = pl.ds(pl.multiple_of(i * step, step), step)
        low = pl.multiple_of(bounds[0, i], 128)

        def run(width):
            width = width * step
            span = pl.ds(low, width)
            same = seg_col[block, :] == seg_row[0:1, span]
            bias[:, 0:width] = jnp.where(same, 0.0, MASKED)
            query, key, value = q_all[block, :], k_all[span, :], v_all[span, :]
            result = jnp.zeros((step, lanes), F32)
            stats = jnp.zeros((step, 128), F32)
            for head in range(heads):
                keep = lane_mask(lanes, head)
                masked = jnp.where(keep, query, jnp.zeros_like(query))
                scores = dot(masked, key, NT) + bias[:, 0:width]
                highest = jnp.max(scores, axis=1, keepdims=True)
                weight = jnp.exp(scores - highest)
                total = jnp.sum(weight, axis=1, keepdims=True)
                part = dot(weight.astype(BF16), value)
                result = jnp.where(keep, part / total, result)
                stats = jnp.where(lane == head, highest + jnp.log(total), stats)
            o_all[block, :] = result.astype(BF16)
            lse[0, block, :] = stats

        each_width(bounds[1, i], frames // step, run)
        return 0

    lax.fori_loop(0, frames // step, one_block, 0)
    for piece in range(pieces):
        outs[piece][...] = o_all[pl.ds(piece_start(place, piece, pieces, rows), rows), :]


def attend(place, bounds, seg_col, seg_row, qkv, lanes, step):
    pieces = len(qkv)
    rows, columns = qkv[0].shape
    groups = columns // (3 * lanes)
    heads = lanes // HEAD_DIM
    frames = rows * pieces
    specs = [pl.BlockSpec((rows, 3 * lanes), lambda g: (0, g))] * pieces
    smem = pl.BlockSpec(memory_space=pltpu.SMEM)
    area = frames * frames // 2 * heads * groups
    results = pl.pallas_call(
        functools.partial(attend_kernel, pieces, heads, step),
        grid=(groups,),
        out_shape=[jax.ShapeDtypeStruct((rows, groups * lanes), BF16)] * pieces
        + [jax.ShapeDtypeStruct((groups, frames, 128), F32)],
        in_specs=[smem, smem, whole(seg_col.shape), whole(seg_row.shape)] + specs,
        out_specs=[pl.BlockSpec((rows, lanes), lambda g: (0, g))] * pieces
        + [pl.BlockSpec((1, frames, 128), lambda g: (g, 0, 0))],
        scratch_shapes=[pltpu.VMEM((frames, lanes), BF16)] * 4 + [pltpu.VMEM((step, frames), F32)],
        compiler_params=params(),
        cost_estimate=cost(area * 4 * 256, frames * columns * 4, area),
        name="attend",
    )(place, bounds, seg_col, seg_row, *qkv)
    return results[:pieces], results[pieces]


def attend_back_kernel(pieces, first, heads, step, place, bounds, seg_col, seg_row, *refs):
    inputs = refs[: 3 * pieces]
    lse, cosine, sine = refs[3 * pieces : 3 * pieces + 3]
    normed = refs[3 * pieces + 3 : 4 * pieces + 3]
    out, grad_w = refs[4 * pieces + 3 : 4 * pieces + 5]
    q_all, k_all, v_all, o_all, do_all, dq_all, dk_all, dv_all, bias, weights, slopes = refs[
        4 * pieces + 5 :
    ]
    rows = inputs[0].shape[0]
    for piece in range(pieces):
        span = pl.ds(piece_start(place, piece, pieces, rows), rows)
        spread(inputs[3 * piece], span, (q_all, k_all, v_all))
        o_all[span, :] = inputs[3 * piece + 1][...]
        do_all[span, :] = inputs[3 * piece + 2][...]
    frames, lanes = q_all.shape
    dk_all[...] = jnp.zeros_like(dk_all)
    dv_all[...] = jnp.zeros_like(dv_all)

    def one_block(i, _):
        block = pl.ds(pl.multiple_of(i * step, step), step)
        low = pl.multiple_of(bounds[0, i], 128)

        def run(width):
            width = width * step
            span = pl.ds(low, width)
            same = seg_col[block, :] == seg_row[0:1, span]
            bias[:, 0:width] = jnp.where(same, 0.0, MASKED)
            query, key, value = q_all[block, :], k_all[span, :], v_all[span, :]
            grad = do_all[block, :]
            product = grad.astype(F32) * o_all[block, :].astype(F32)
            result = jnp.zeros((step, lanes), F32)
            queries, grads = [], []
            for head in range(heads):
                keep = lane_mask(lanes, head)
                queries.append(jnp.where(keep, query, jnp.zeros_like(query)))
                grads.append(jnp.where(keep, grad, jnp.zeros_like(grad)))
                centre = jnp.sum(jnp.where(keep, product, 0.0), axis=1, keepdims=True)
                scores = dot(queries[head], key, NT) + bias[:, 0:width]
                weight = jnp.exp(scores - lse[0, block, first + head : first + head + 1])
                slope = dot(grads[head], value, NT) - centre
                slope = (weight * slope).astype(BF16)
                at = pl.ds(head * step, step)
                weights[at, 0:width] = weight.astype(BF16)
                slopes[at, 0:width] = slope
                result = jnp.where(keep, dot(slope, key), result)
            dq_all[block, :] = result * HEAD_DIM**-0.5
            dv_all[span, :] += dot(weights[:, 0:width], jnp.concatenate(grads, axis=0), TN)
            dk_all[span, :] += dot(slopes[:, 0:width], jnp.concatenate(queries, axis=0), TN)

        each_width(bounds[1, i], frames // step, run)
        return 0

    lax.fori_loop(0, frames // step, one_block, 0)
    for piece in range(pieces):
        span = pl.ds(piece_start(place, piece, pieces, rows), rows)
        cos = cosine[span, :]
        sin = -sine[span, :]
        out[piece, :, 0:lanes] = turn(dq_all[span, :], cos, sin).astype(BF16)
        out[piece, :, lanes : 2 * lanes] = turn(dk_all[span, :], cos, sin).astype(BF16)
        out[piece, :, 2 * lanes : 3 * lanes] = dv_all[span, :].astype(BF16)
    grad_w[...] = sum(dot(normed[p][...], out[p], TN) for p in range(pieces)).astype(BF16)


def attend_back(
    place, bounds, seg_col, seg_row, qkv, attended, grads, lse, cosine, sine, normed, pair, step
):
    pieces = len(qkv)
    rows = qkv[0].shape[0]
    lanes, heads = 128, 128 // HEAD_DIM
    width = normed[0].shape[1]
    per_group = attended[0].shape[1] // lanes // lse.shape[0]
    frames = rows * pieces
    specs, arrays = [], []
    for piece in range(pieces):
        specs.append(pl.BlockSpec((rows, 3 * lanes), lambda i: (0, pair)))
        specs += [pl.BlockSpec((rows, lanes), lambda i: (0, pair))] * 2
        arrays += [qkv[piece], attended[piece], grads[piece]]
    smem = pl.BlockSpec(memory_space=pltpu.SMEM)
    area = frames * frames // 2 * heads
    return pl.pallas_call(
        functools.partial(attend_back_kernel, pieces, pair % per_group * heads, heads, step),
        grid=(1,),
        out_shape=[
            jax.ShapeDtypeStruct((pieces, rows, 3 * lanes), BF16),
            jax.ShapeDtypeStruct((width, 3 * lanes), BF16),
        ],
        in_specs=[smem, smem, whole(seg_col.shape, 1), whole(seg_row.shape, 1)]
        + specs
        + [
            pl.BlockSpec(
                (1, frames, 128), lambda i: (pair // per_group, 0, 0), pipeline_mode=pl.Buffered(1)
            ),
            whole(cosine.shape, 1),
            whole(sine.shape, 1),
        ]
        + [whole(normed[0].shape, 1)] * pieces,
        out_specs=[whole((pieces, rows, 3 * lanes), 1), whole((width, 3 * lanes), 1)],
        scratch_shapes=[pltpu.VMEM((frames, lanes), BF16)] * 5
        + [pltpu.VMEM((frames, lanes), F32)] * 3
        + [pltpu.VMEM((step, frames), F32)]
        + [pltpu.VMEM((heads * step, frames), BF16)] * 2,
        compiler_params=params(),
        cost_estimate=cost(area * 10 * 256, frames * lanes * 16, area),
        name="attend_back",
    )(place, bounds, seg_col, seg_row, *arrays, lse, cosine, sine, *normed)


def gelu_pair(h):
    root = math.sqrt(2.0 / math.pi)
    square = h * h
    bend = jnp.tanh(root * h * (1.0 + 0.044715 * square))
    half = 0.5 * (1.0 + bend)
    slope = half + 0.5 * h * (1.0 - bend * bend) * (root * (1.0 + 0.134145 * square))
    return h * half, slope


def flat(ref, span=slice(None)):
    value = ref[:, 0, :, span]
    return value.reshape(value.shape[0] * value.shape[1], value.shape[2])


def middle_kernel(pieces, place, *refs):
    x, member, member_flip, adaptive, dy = refs[:5]
    refs = refs[5:]
    attended, refs = refs[:pieces], refs[pieces:]
    w_out, refs = refs[:pieces], refs[pieces:]
    w_up, refs = refs[:pieces], refs[pieces:]
    w_down, refs = refs[:pieces], refs[pieces:]
    mixed, dx2, a2_out, d2_out, d1_out, dadaptive = refs[:6]
    refs = refs[6:]
    active, refs = refs[:pieces], refs[pieces:]
    dhidden, refs = refs[:pieces], refs[pieces:]
    dattended = refs[:pieces]
    width = x.shape[1]
    here = member[...]
    gate1, shift2, scale2, gate2 = (
        pick(here, adaptive[:, n * width : (n + 1) * width]) for n in (2, 3, 4, 5)
    )
    branch1 = sum(dot(attended[p][...], flat(w_out[p]), NT) for p in range(pieces))
    x2 = x[...].astype(F32) + gate1 * branch1
    n2, r2 = norm(x2)
    a2 = (n2 * (1.0 + scale2) + shift2).astype(BF16)
    a2_out[...] = a2
    branch2 = jnp.zeros_like(x2)
    slopes = []
    for p in range(pieces):
        value, slope = gelu_pair(dot(a2, flat(w_up[p])))
        value = value.astype(BF16)
        active[p][...] = value
        slopes.append(slope)
        branch2 = branch2 + dot(value, flat(w_down[p]), NT)
    mixed[...] = (x2 + gate2 * branch2).astype(BF16)
    upstream = dy[...].astype(F32)
    d2 = (upstream * gate2).astype(BF16)
    d2_out[...] = d2
    da2 = jnp.zeros_like(x2)
    for p in range(pieces):
        dh = (dot(d2, flat(w_down[p])) * slopes[p]).astype(BF16)
        dhidden[p][...] = dh
        da2 = da2 + dot(dh, flat(w_up[p]), NT)
    u2 = da2 * (1.0 + scale2)
    back = upstream + r2 * (
        u2 - jnp.mean(u2, axis=-1, keepdims=True) - n2 * jnp.mean(u2 * n2, axis=-1, keepdims=True)
    )
    dx2[...] = back
    d1 = (back * gate1).astype(BF16)
    d1_out[...] = d1
    for p in range(pieces):
        dattended[p][...] = dot(d1, flat(w_out[p])).astype(BF16)

    @pl.when(pl.program_id(0) == 0)
    def _():
        dadaptive[...] = jnp.zeros_like(dadaptive)

    for n, term in enumerate((back * branch1, da2, da2 * n2, upstream * branch2)):
        dadaptive[:, n * width : (n + 1) * width] += gather(member_flip[...], term)


def middle(place, x, member, member_flip, adaptive, dy, attended, weights):
    pieces = len(attended)
    rows, width = x.shape
    head_columns = attended[0].shape[1]
    hidden = 2 * head_columns
    tile = min(256, rows)

    def tiled(columns):
        return pl.BlockSpec((tile, columns), lambda i, s: (i, 0))

    def shaped(columns, kind):
        return jax.ShapeDtypeStruct((rows, columns), kind)

    shards, slices, own_rows, _ = weights.shape

    def resident(columns, at):
        return [
            pl.BlockSpec(
                (shards, 1, own_rows, columns),
                lambda i, s, piece=piece: (0, lax.rem(s[0] + piece, slices), 0, at),
                pipeline_mode=pl.Buffered(1),
            )
            for piece in range(pieces)
        ]

    cuts = resident(head_columns, 4) + resident(hidden, 0) + resident(hidden, 1)
    work = 2 * rows * width * pieces * (3 * hidden * 2 + head_columns * 2)
    results = pl.pallas_call(
        functools.partial(middle_kernel, pieces),
        grid_spec=pltpu.PrefetchScalarGridSpec(
        num_scalar_prefetch=1,
        grid=(rows // tile,),
        in_specs=[
            tiled(width),
            tiled(32),
            pl.BlockSpec((16, tile), lambda i, s: (0, i)),
            whole(adaptive.shape, 1),
            tiled(width),
        ]
        + [tiled(head_columns)] * pieces
        + cuts,
        out_specs=[tiled(width)] * 5
        + [whole((8, 4 * width))]
        + [tiled(hidden)] * (2 * pieces)
        + [tiled(head_columns)] * pieces,
        ),
        out_shape=[
            shaped(width, BF16),
            shaped(width, F32),
            shaped(width, BF16),
            shaped(width, BF16),
            shaped(width, BF16),
            jax.ShapeDtypeStruct((8, 4 * width), F32),
        ]
        + [shaped(hidden, BF16)] * (2 * pieces)
        + [shaped(head_columns, BF16)] * pieces,
        compiler_params=params(),
        cost_estimate=cost(work, rows * width * 30, rows * hidden * pieces),
        name="middle",
    )(place, x, member, member_flip, adaptive, dy, *attended, *[weights] * (3 * pieces))
    head, rest = results[:6], results[6:]
    return head, rest[:pieces], rest[pieces : 2 * pieces], rest[2 * pieces :]


def part_kernel(groups, *refs):
    slopes, weights, out = refs[:groups], refs[groups], refs[-1]
    slope = jnp.concatenate([slope[...] for slope in slopes], axis=1)
    out[...] = dot(slope, weights[...], NT).astype(BF16)


def input_part(slopes, weights, piece):
    rows, columns = slopes[0].shape[1:]
    width = weights.shape[0]
    tile = min(256, rows)
    groups = len(slopes)
    return pl.pallas_call(
        functools.partial(part_kernel, groups),
        grid=(rows // tile,),
        in_specs=[pl.BlockSpec((None, tile, columns), lambda i: (piece, i, 0))] * groups
        + [whole(weights.shape, 1)],
        out_shape=jax.ShapeDtypeStruct((rows, width), BF16),
        out_specs=pl.BlockSpec((tile, width), lambda i: (i, 0)),
        compiler_params=params(),
        cost_estimate=cost(2 * rows * width * columns * groups, rows * width * 8),
        name="input_part",
    )(*slopes, weights)


def last_kernel(groups, arrivals, *refs):
    x, member, member_flip, adaptive, dx2 = refs[:5]
    refs = refs[5:]
    arrived, refs = refs[:arrivals], refs[arrivals:]
    slopes, refs = refs[:groups], refs[groups:]
    weights, grad, dadaptive = refs
    width = x.shape[1]
    normed, inverse = norm(x[...].astype(F32))
    scale = pick(member[...], adaptive[:, width : 2 * width])
    slope = jnp.concatenate([slope[...] for slope in slopes], axis=1)
    da1 = dot(slope, weights[...], NT)
    for piece in arrived:
        da1 = da1 + piece[...].astype(F32)
    u1 = da1 * (1.0 + scale)
    back = inverse * (
        u1
        - jnp.mean(u1, axis=-1, keepdims=True)
        - normed * jnp.mean(u1 * normed, axis=-1, keepdims=True)
    )
    grad[...] = (dx2[...] + back).astype(BF16)

    @pl.when(pl.program_id(0) == 0)
    def _():
        dadaptive[...] = jnp.zeros_like(dadaptive)

    dadaptive[:, :width] += gather(member_flip[...], da1)
    dadaptive[:, width:] += gather(member_flip[...], da1 * normed)


def last(x, member, member_flip, adaptive, dx2, arrived, slopes, weights):
    rows, width = x.shape
    tile = min(256, rows)

    def tiled(columns):
        return pl.BlockSpec((tile, columns), lambda i: (i, 0))

    return pl.pallas_call(
        functools.partial(last_kernel, len(slopes), len(arrived)),
        grid=(rows // tile,),
        in_specs=[
            tiled(width),
            tiled(32),
            pl.BlockSpec((16, tile), lambda i: (0, i)),
            whole(adaptive.shape, 1),
            tiled(width),
        ]
        + [tiled(width)] * len(arrived)
        + [pl.BlockSpec((None, tile, s.shape[2]), lambda i: (0, i, 0)) for s in slopes]
        + [whole(weights.shape, 1)],
        out_shape=[
            jax.ShapeDtypeStruct((rows, width), BF16),
            jax.ShapeDtypeStruct((8, 2 * width), F32),
        ],
        out_specs=[tiled(width), whole((8, 2 * width))],
        compiler_params=params(),
        cost_estimate=cost(2 * rows * width * sum(s.shape[2] for s in slopes), rows * width * 12),
        name="last",
    )(x, member, member_flip, adaptive, dx2, *arrived, *slopes, weights)


def time_vector(steps, width):
    halfway = width // 2
    rates = jnp.exp(jnp.arange(halfway, dtype=F32) * (-math.log(10000.0) / (halfway - 1)))
    angles = steps.astype(F32)[:, None] * rates[None, :]
    return jnp.concatenate([jnp.sin(angles), jnp.cos(angles)], axis=1)


def body(frames, clip_lengths, timesteps, w_qkv, w_out, w_up, w_down, w_ada, b_ada, grad_out):
    rows, width = frames.shape
    clips = clip_lengths.shape[0]
    pieces = lax.axis_size("hl") * 2
    group_rows = rows * pieces
    own_rows = w_qkv.shape[1]
    head_columns = width // pieces
    lanes = min(256, head_columns)
    pairs = head_columns // 128
    step = min(256, group_rows)
    place = lax.axis_index(SUB).astype(jnp.int32)

    qkv_shard = w_qkv.astype(BF16).reshape(3, own_rows, pairs, 128)
    qkv_shard = jnp.transpose(qkv_shard, (1, 2, 0, 3)).reshape(own_rows, 3 * head_columns)
    mlp_shard = jnp.concatenate(
        [w_up.astype(BF16), w_down.astype(BF16).T, w_out.astype(BF16).T], axis=1
    )
    qkv_shard = moved(qkv_shard)
    lengths = moved(clip_lengths)

    def around(value):
        return [value] + [from_sub(value, step) for step in range(1, pieces)]

    condition = jax.nn.silu(time_vector(timesteps, width))
    columns = w_ada.shape[1]
    devices = [lax.axis_size(axis) for axis in ALL]
    za, zb, cores, hh, hl = devices
    table = (
        jnp.dot(condition, lax.reduce_precision(w_ada, 8, 7), precision=HIGHEST)
        + lax.reduce_precision(b_ada, 8, 7)[None, :]
    )
    table, qkv_shard, lengths = together(table, qkv_shard, lengths)
    table = table.reshape(za, zb, 1, hh, 1, clips, columns)
    table = jnp.broadcast_to(table, (za, zb, cores, hh, hl, clips, columns))
    table = lax.all_to_all(table.reshape(-1, clips, columns), ALL, 0, 0, tiled=True)
    adaptive = jnp.transpose(table, (1, 0, 2)).reshape(clips, -1)
    adaptive = jnp.pad(adaptive, ((0, 8 - clips), (0, 0)))

    ends = jnp.cumsum(lengths, dtype=jnp.int32)
    starts = ends - lengths
    index = jnp.arange(group_rows, dtype=jnp.int32)
    segment = jnp.sum((index[:, None] >= ends[None, :]).astype(jnp.int32), axis=1, dtype=jnp.int32)
    edges = jnp.concatenate([jnp.zeros((1,), jnp.int32), ends])
    begins = jnp.max(jnp.where(index[:, None] >= edges[None, :], edges[None, :], 0), axis=1)
    position = (index - begins).astype(F32)
    lane = jnp.arange(128, dtype=jnp.int32) % HEAD_DIM
    rates = jnp.exp((lane % (HEAD_DIM // 2)).astype(F32) * (-2.0 * math.log(10000.0) / HEAD_DIM))
    angles = position[:, None] * rates[None, :]
    cosine = jnp.cos(angles)
    sine = jnp.sin(angles) * jnp.where(lane < HEAD_DIM // 2, -1.0, 1.0)[None, :]
    seg_col = segment[:, None]
    seg_row = segment[None, :]
    block_first = jnp.arange(0, group_rows, step, dtype=jnp.int32)
    first_seg = jnp.sum((block_first[:, None] >= ends[None, :]).astype(jnp.int32), axis=1)
    last_seg = jnp.sum((block_first[:, None] + (step - 1) >= ends[None, :]).astype(jnp.int32), axis=1)
    closing = jnp.concatenate([ends, jnp.full((1,), group_rows, jnp.int32)])
    low_at = jnp.sum(jnp.where(first_seg[:, None] == jnp.arange(clips + 1)[None, :], edges[None, :], 0), axis=1)
    high_at = jnp.sum(jnp.where(last_seg[:, None] == jnp.arange(clips + 1)[None, :], closing[None, :], 0), axis=1)
    low_at = low_at // 128 * 128
    widths = (high_at - low_at + step - 1) // step
    low_at = jnp.minimum(low_at, group_rows - widths * step)
    bounds = jnp.stack([low_at, widths]).astype(jnp.int32)
    own_index = place * rows + jnp.arange(rows, dtype=jnp.int32)
    member = ((own_index[:, None] >= starts[None, :]) & (own_index[:, None] < ends[None, :])).astype(F32)
    member = jnp.pad(member, ((0, 0), (0, 8 - clips))).astype(BF16)
    member_flip = jnp.pad(member.T, ((0, 8), (0, 0)))
    member = jnp.concatenate([member, member, member, jnp.zeros_like(member)], axis=1)

    x = moved(frames)
    held = gather_line(qkv_shard)
    held, adaptive, x, cosine, sine, member = together(held, adaptive, x, cosine, sine, member)
    near = gather_near(held)
    a1_all = around(first_norm(x, member, adaptive))
    near, a1_all, mlp_shard, grad_out = together(near, a1_all, mlp_shard, grad_out)
    mlp_full = lax.all_gather(mlp_shard, ALL, axis=0, tiled=True)
    mlp_full = mlp_full.reshape(-1, pieces, own_rows, mlp_shard.shape[1])
    qkv_full = gathered(*gather_far(*near))
    places = [((place + piece) % pieces).reshape(1) for piece in range(pieces)]
    qkv = [
        project(places[piece], a1_all[piece], qkv_full, cosine, sine, lanes)
        for piece in range(pieces)
    ]
    at_place = place.reshape(1)
    qkv, grad_out = together(qkv, grad_out)
    dy = moved(grad_out)
    attended, lse = attend(at_place, bounds, seg_col, seg_row, qkv, lanes, step)
    attended, lse, dy = together(attended, lse, dy)
    attended_own = [attended[0]] + [
        from_sub_piece(attended, step_) for step_ in range(1, pieces)
    ]

    head, active, dhidden, dattended = middle(
        at_place, x, member, member_flip, adaptive, dy, attended_own, mlp_full
    )
    mixed, dx2, a2, d2, d1, dada_late = head
    grads_attended = [dattended[0]] + [
        from_sub_piece(dattended, step_) for step_ in range(1, pieces)
    ]
    mixed_back = moved(mixed)

    def summed(left, right):
        parts = [dot(left, part, TN).astype(BF16) for part in right]
        return [parts[0]] + [to_sub(parts[step], step) for step in range(1, pieces)]

    late = [summed(a2, dhidden), summed(d2, active), summed(d1, attended_own)]

    def back(pair, qkv):
        return attend_back(
            at_place, bounds, seg_col, seg_row, qkv, attended, grads_attended, lse, cosine, sine,
            a1_all, pair, step,
        )

    slopes, grads_qkv = [], []
    early = final = None

    def next_pair():
        slope, grad = back(len(slopes), qkv)
        slopes.append(slope)
        grads_qkv.append(grad)

    next_pair()
    late, slopes, grads_qkv, mixed_back = together(late, slopes, grads_qkv, mixed_back)
    late, qkv = together(cut_plane(late), qkv)
    late = swap_plane(late)
    while len(slopes) < pairs - 1:
        next_pair()
    if pairs > 1:
        early = cut_plane([[grad] for grad in grads_qkv])
    late, early, slopes, grads_qkv = together(late, early, slopes, grads_qkv)
    late, qkv = together(cut_line(late), qkv)
    late = swap_line(late)
    if pairs > 1:
        early = swap_plane(early)
        next_pair()
    late, early, slopes, grads_qkv = together(late, early, slopes, grads_qkv)
    final = cut_plane([grads_qkv[-1:]])
    if pairs > 1:
        early = cut_line(early)
    final, early, slopes = together(final, early, slopes)
    final = swap_plane(final)
    if pairs > 1:
        early = swap_line(early)
    arrived = [to_sub(input_part(slopes, qkv_full, piece), piece) for piece in range(1, pieces)]
    final, early, arrived = together(final, early, arrived)
    final, dx2 = together(cut_line(final), dx2)
    final = swap_line(final)
    grad_frames, dada_early = last(
        x, member, member_flip, adaptive, dx2, arrived, slopes, qkv_full
    )
    late, early, final, grad_frames, dada_early = together(
        late, early, final, grad_frames, dada_early
    )
    grad_frames = moved(grad_frames).astype(F32)
    sums = [total_of(cuts) for cuts in (late, early, final) if cuts]
    sums = moved(jnp.concatenate(sums, axis=1))
    late, rest = sums[:, : mlp_shard.shape[1]], sums[:, mlp_shard.shape[1] :]
    hidden_columns = w_up.shape[1]
    grad_up = late[:, :hidden_columns]
    grad_down = late[:, hidden_columns : 2 * hidden_columns]
    grad_outw = late[:, 2 * hidden_columns :]
    dadaptive = jnp.concatenate([dada_early, dada_late], axis=1)[:clips]
    dadaptive = jnp.transpose(dadaptive.reshape(clips, -1, columns), (1, 0, 2))
    dadaptive = lax.all_to_all(dadaptive, ALL, 0, 0, tiled=True)
    dadaptive = dadaptive.reshape(za, zb, cores, hh, hl, clips, columns)
    dadaptive = jnp.sum(dadaptive, axis=(2, 4)).reshape(-1, columns)
    grad_ada = dot(condition, dadaptive, TN, HIGHEST)
    grad_bias = jnp.sum(dadaptive, axis=0)

    grad_qkv = rest.reshape(own_rows, pairs, 3, 128)
    grad_qkv = jnp.transpose(grad_qkv, (2, 0, 1, 3)).reshape(w_qkv.shape).astype(F32)
    return (
        mixed_back,
        grad_frames,
        grad_qkv,
        grad_outw.astype(F32).T,
        grad_up.astype(F32),
        grad_down.astype(F32).T,
        grad_ada,
        grad_bias,
    )


def from_sub_piece(parts, step):
    pieces = len(parts)
    return from_sub(parts[pieces - step], step)


def solution(mesh):
    clip, head = mesh.shape["clip"], mesh.shape["head"]
    fine = Mesh(mesh.devices.reshape(clip // 4, 2, 2, 2, head // 2), ALL)
    by_clip = ("za", "zb", "core")
    by_head = ("hh", "hl")
    everywhere = by_clip + by_head
    placed = (
        P(everywhere, None),
        P(by_clip),
        P(),
        P(None, by_clip, by_head),
        P(by_head, by_clip),
        P(by_clip, by_head),
        P(by_head, by_clip),
        P(None, everywhere),
        P(everywhere),
        P(everywhere, None),
    )
    return jax.shard_map(
        body,
        mesh=fine,
        in_specs=placed,
        out_specs=(
            P(everywhere, None),
            P(everywhere, None),
            P(None, by_clip, by_head),
            P(by_head, by_clip),
            P(by_clip, by_head),
            P(by_head, by_clip),
            P(None, everywhere),
            P(everywhere),
        ),
        check_vma=False,
    )
```

```python
import functools
import math

import jax
import jax.numpy as jnp
from jax import lax
from jax.experimental import pallas as pl
from jax.experimental.pallas import tpu as pltpu
from jax.sharding import Mesh
from jax.sharding import PartitionSpec as P

HEAD_DIM = 64
HEADS = 16
HIGHEST = lax.Precision.HIGHEST
MASKED = -1e30
EPSILON = 1e-06
VMEM_LIMIT = 60 * 1024 * 1024
F32 = jnp.float32
BF16 = jnp.bfloat16

ALL = ("za", "zb", "core", "hh", "hl")
MOVE = ("core", "hh", "hl")
SUB = ("core", "hl")

NT = (((1,), (1,)), ((), ()))
NN = (((1,), (0,)), ((), ()))
TN = (((0,), (0,)), ((), ()))


def dot(a, b, dims=NN, precision=None):
    return lax.dot_general(a, b, dims, precision=precision, preferred_element_type=F32)


def params(**more):
    return pltpu.CompilerParams(vmem_limit_bytes=VMEM_LIMIT, **more)


def cost(flops, bytes_accessed, transcendentals=0):
    return pl.CostEstimate(
        flops=int(flops), bytes_accessed=int(bytes_accessed), transcendentals=int(transcendentals)
    )


def whole(shape, buffers=None):
    zeros = (0,) * len(shape)
    if buffers is None:
        return pl.BlockSpec(shape, lambda *_: zeros)
    return pl.BlockSpec(shape, lambda *_: zeros, pipeline_mode=pl.Buffered(buffers))


def moved(value):
    stays = lax.axis_index("core") == lax.axis_index("hh")
    return jnp.where(stays, value, lax.ppermute(value, ("core", "hh"), [(1, 2), (2, 1)]))


def from_sub(value, step):
    size = lax.axis_size("hl") * 2
    return lax.ppermute(value, SUB, [((d + step) % size, d) for d in range(size)])


def to_sub(value, step):
    size = lax.axis_size("hl") * 2
    return lax.ppermute(value, SUB, [(d, (d + step) % size) for d in range(size)])


SWAP = [(0, 1), (1, 0)]


def across(value, bit):
    size = lax.axis_size("za")
    return lax.ppermute(value, "za", [(i, i ^ bit) for i in range(size)])


def place_kernel(half, where, own, by_zb, by_hh, both_low, both_high, out):
    zb = where[0]
    hh = where[1]
    out[0, zb, hh] = own[0]
    out[0, 1 - zb, hh] = by_zb[0]
    out[0, zb, 1 - hh] = by_hh[0]

    @pl.when(pl.program_id(0) < half)
    def _():
        out[0, 1 - zb, 1 - hh] = both_low[0]

    @pl.when(pl.program_id(0) >= half)
    def _():
        out[0, 1 - zb, 1 - hh] = both_high[0]


def gather_line(shard):
    return jnp.stack([shard] + [across(shard, bits) for bits in range(1, lax.axis_size("za"))])


def gather_near(held):
    return held, lax.ppermute(held, "zb", SWAP), lax.ppermute(held, "hh", SWAP)


def gather_far(held, by_zb, by_hh):
    half = held.shape[0] // 2
    both_low = lax.ppermute(by_zb[:half], "hh", SWAP)
    both_high = lax.ppermute(by_hh[half:], "zb", SWAP)
    return held, by_zb, by_hh, both_low, both_high


def gathered(held, by_zb, by_hh, both_low, both_high):
    size, rows, columns = held.shape
    half = size // 2
    where = [lax.axis_index("zb"), lax.axis_index("hh")]
    where += [lax.axis_index("za") ^ bits for bits in range(size)]
    where = jnp.stack(where).astype(jnp.int32)
    block = (1, rows, columns)
    full = pl.pallas_call(
        functools.partial(place_kernel, half),
        grid_spec=pltpu.PrefetchScalarGridSpec(
            num_scalar_prefetch=1,
            grid=(size,),
            in_specs=[pl.BlockSpec(block, lambda i, w: (i, 0, 0))] * 3
            + [
                pl.BlockSpec(block, lambda i, w: (jnp.minimum(i, half - 1), 0, 0)),
                pl.BlockSpec(block, lambda i, w: (jnp.maximum(i - half, 0), 0, 0)),
            ],
            out_specs=pl.BlockSpec((1, 2, 2, rows, columns), lambda i, w: (w[2 + i], 0, 0, 0, 0)),
        ),
        out_shape=jax.ShapeDtypeStruct((size, 2, 2, rows, columns), held.dtype),
        compiler_params=params(),
        cost_estimate=cost(0, size * 4 * rows * columns * 4),
        name="place",
    )(where, held, by_zb, by_hh, both_low, both_high)
    return full.reshape(size * 4 * rows, columns)


FOUR = ((0, 0), (1, 0), (0, 1), (1, 1))


def cut_kernel(counts, where, *refs):
    outs = refs[-4:]
    zb, hh = where[0], where[1]
    first = start = 0
    for count in counts:
        terms = refs[first : first + count]
        columns = terms[0].shape[-1]
        for out, (dz, dh) in zip(outs, FOUR):
            z, h = lax.rem(zb + dz, 2), lax.rem(hh + dh, 2)
            part = terms[0][0, z, h]
            if count > 1:
                part = sum(term[0, z, h].astype(F32) for term in terms).astype(BF16)
            out[0, :, start : start + columns] = part
        first += count
        start += columns


def cut_plane(weights):
    size = lax.axis_size("za")
    where = jnp.stack([lax.axis_index("zb"), lax.axis_index("hh")]).astype(jnp.int32)
    terms = [term for group in weights for term in group]
    rows = terms[0].shape[0] // (size * 4)
    total = sum(group[0].shape[1] for group in weights)
    return pl.pallas_call(
        functools.partial(cut_kernel, [len(group) for group in weights]),
        grid_spec=pltpu.PrefetchScalarGridSpec(
            num_scalar_prefetch=1,
            grid=(size,),
            in_specs=[
                pl.BlockSpec((1, 2, 2, rows, term.shape[1]), lambda i, w: (i, 0, 0, 0, 0))
                for term in terms
            ],
            out_specs=[pl.BlockSpec((1, rows, total), lambda i, w: (i, 0, 0))] * 4,
        ),
        out_shape=[jax.ShapeDtypeStruct((size, rows, total), BF16)] * 4,
        compiler_params=params(),
        cost_estimate=cost(0, sum(2 * term.size for term in terms) + size * 8 * rows * total),
        name="cut",
    )(where, *[term.reshape(size, 2, 2, rows, -1) for term in terms])


def swap_plane(pieces):
    own, to_zb, to_hh, to_both = pieces
    from_both = lax.ppermute(to_both, ("zb", "hh"), [(0, 3), (1, 2), (2, 1), (3, 0)])
    from_hh = lax.ppermute(to_hh, "hh", SWAP)
    from_zb = lax.ppermute(to_zb, "zb", SWAP)
    return own, from_zb, from_hh, from_both


def add_up(pieces):
    return sum(piece.astype(F32) for piece in pieces).astype(BF16)


def cut_line(total, bit):
    pairs = total.reshape(total.shape[0] // 2, 2, *total.shape[1:])
    place = (lax.axis_index("za") // bit) % 2
    keep = lax.dynamic_index_in_dim(pairs, place, 1, keepdims=False)
    send = lax.dynamic_index_in_dim(pairs, 1 - place, 1, keepdims=False)
    return keep, send


def swap_line(cuts, bit):
    return cuts[0], across(cuts[1], bit)


def line_rest(pieces):
    total = add_up(pieces)
    count = total.shape[0]
    apart = lax.axis_size("za") // count
    mine = lax.axis_index("za") // apart
    cuts = [lax.dynamic_index_in_dim(total, mine ^ n, 0, keepdims=False) for n in range(count)]
    return add_up([cuts[0]] + [across(cut, n * apart) for n, cut in enumerate(cuts) if n])


def together(*values):
    return lax.optimization_barrier(values)


def norm(values):
    centred = values - jnp.mean(values, axis=-1, keepdims=True)
    variance = jnp.mean(centred * centred, axis=-1, keepdims=True)
    inverse = lax.rsqrt(variance + EPSILON)
    return centred * inverse, inverse


def pick(member, table):
    high = table.astype(BF16)
    rest = table - high.astype(F32)
    middle = rest.astype(BF16)
    low = (rest - middle.astype(F32)).astype(BF16)
    return dot(member, jnp.concatenate([high, middle, low, jnp.zeros_like(low)], axis=0))


def gather(member_flip, term):
    high = term.astype(BF16)
    low = (term - high.astype(F32)).astype(BF16)
    return (dot(member_flip, high) + dot(member_flip, low))[0:8]


def first_norm_kernel(x, member, adaptive, out):
    width = x.shape[1]
    normed, _ = norm(x[...].astype(F32))
    shift = pick(member[...], adaptive[:, :width])
    scale = pick(member[...], adaptive[:, width : 2 * width])
    out[...] = (normed * (1.0 + scale) + shift).astype(BF16)


def first_norm(x, member, adaptive):
    rows, width = x.shape
    tile = min(256, rows)
    return pl.pallas_call(
        first_norm_kernel,
        grid=(rows // tile,),
        out_shape=jax.ShapeDtypeStruct((rows, width), BF16),
        in_specs=[
            pl.BlockSpec((tile, width), lambda i: (i, 0)),
            pl.BlockSpec((tile, 32), lambda i: (i, 0)),
            whole(adaptive.shape),
        ],
        out_specs=pl.BlockSpec((tile, width), lambda i: (i, 0)),
        compiler_params=params(),
        cost_estimate=cost(rows * width * 40, rows * width * 4),
        name="first_norm",
    )(x, member, adaptive)


def turn(values, cosine, sine):
    lanes = values.shape[1]
    place = lax.broadcasted_iota(jnp.int32, (1, 128), 1) % HEAD_DIM
    first = place < HEAD_DIM // 2
    parts = []
    for at in range(0, lanes, 128):
        part = values[:, at : at + 128]
        ahead = pltpu.roll(part, 128 - HEAD_DIM // 2, 1)
        behind = pltpu.roll(part, HEAD_DIM // 2, 1)
        swapped = jnp.where(first, ahead, behind)
        parts.append(part * cosine + swapped * sine)
    return parts[0] if len(parts) == 1 else jnp.concatenate(parts, axis=1)


def project_kernel(lanes, place, a, w, cosine, sine, out):
    for start in range(0, w.shape[1], 3 * lanes):
        products = dot(a[...], w[:, start : start + 3 * lanes])
        for at in range(0, 3 * lanes, 128):
            product = products[:, at : at + 128]
            kind = at // 128 % 3
            if kind < 2:
                product = turn(product, cosine[...], sine[...])
            if kind == 0:
                product = product * HEAD_DIM**-0.5
            out[:, start + at : start + at + 128] = product.astype(BF16)


def project(place, a, w, cosine, sine, lanes):
    rows, width = a.shape
    columns = w.shape[1]
    tile = min(256, rows)
    tiles = rows // tile
    return pl.pallas_call(
        functools.partial(project_kernel, lanes),
        grid_spec=pltpu.PrefetchScalarGridSpec(
            num_scalar_prefetch=1,
            grid=(tiles,),
            in_specs=[
                pl.BlockSpec((tile, width), lambda i, s: (i, 0)),
                whole(w.shape, 1),
                pl.BlockSpec((tile, 128), lambda i, s: (s[0] * tiles + i, 0)),
                pl.BlockSpec((tile, 128), lambda i, s: (s[0] * tiles + i, 0)),
            ],
            out_specs=pl.BlockSpec((tile, columns), lambda i, s: (i, 0)),
        ),
        out_shape=jax.ShapeDtypeStruct((rows, columns), BF16),
        compiler_params=params(),
        cost_estimate=cost(2 * rows * width * columns, rows * (width + columns) * 2),
        name="project",
    )(place, a, w, cosine, sine)


def stack_heads(values, heads):
    none = jnp.zeros_like(values)
    lanes = values.shape[1]
    return jnp.concatenate(
        [jnp.where(lane_mask(lanes, head), values, none) for head in range(heads)], axis=0
    )


def lane_mask(lanes, head):
    return lax.broadcasted_iota(jnp.int32, (1, lanes), 1) // HEAD_DIM == head


def piece_start(place, piece, pieces, rows):
    return pl.multiple_of(lax.rem(place[0] + piece, pieces) * rows, rows)


def flip(values):
    return jnp.transpose(values.astype(F32))


def spread(ref, span, arrays):
    for at in range(0, ref.shape[1], 128):
        start = at // 384 * 128
        arrays[at // 128 % 3][span, start : start + 128] = ref[:, at : at + 128]


def each_width(count, limit, run):
    for width in range(1, limit + 1):

        @pl.when(count == width)
        def _(width=width):
            run(width)


def head_sums(values):
    lanes = values.shape[1]
    row = lax.broadcasted_iota(jnp.int32, (lanes, lanes), 0) // HEAD_DIM
    column = lax.broadcasted_iota(jnp.int32, (lanes, lanes), 1) // HEAD_DIM
    same = (row == column).astype(BF16)
    high = values.astype(BF16)
    low = (values - high.astype(F32)).astype(BF16)
    return dot(high, same) + dot(low, same)


def swap_heads(values):
    parts = [pltpu.roll(values[:, at : at + 128], HEAD_DIM, 1) for at in range(0, values.shape[1], 128)]
    return parts[0] if len(parts) == 1 else jnp.concatenate(parts, axis=1)


def largest_sum(ref, step):
    lanes = ref.shape[1]
    row = lax.broadcasted_iota(jnp.int32, (lanes, lanes), 0) // HEAD_DIM
    column = lax.broadcasted_iota(jnp.int32, (lanes, lanes), 1) // HEAD_DIM
    same = (row == column).astype(BF16)
    largest = jnp.zeros((1, lanes), F32)
    for at in range(0, ref.shape[0], step):
        values = ref[at : at + step, :]
        sums = dot(values * values, same)
        largest = jnp.maximum(largest, jnp.max(sums, axis=0, keepdims=True))
    return largest


def attend_kernel(pieces, heads, step, place, bounds, seg_col, seg_row, *refs):
    inputs = refs[:pieces]
    outs = refs[pieces : 2 * pieces]
    lse, q_all, k_all, v_all, v_even, v_odd, o_all, bias, highest, total, product = refs[2 * pieces :]
    rows = inputs[0].shape[0]
    frames, lanes = q_all.shape
    even = lax.broadcasted_iota(jnp.int32, (1, lanes), 1) // HEAD_DIM % 2 == 0
    for piece in range(pieces):
        span = pl.ds(piece_start(place, piece, pieces, rows), rows)
        spread(inputs[piece], span, (q_all, k_all, v_all))
        value = v_all[span, :]
        v_even[span, :] = jnp.where(even, value, jnp.ones_like(value))
        v_odd[span, :] = jnp.where(even, jnp.ones_like(value), value)
    limit = jnp.sqrt(largest_sum(q_all, 2 * step) * largest_sum(k_all, 2 * step))
    shift = limit * 1.02 - 60.0

    def each_block(run):
        def one_block(i, _):
            block = pl.ds(pl.multiple_of(i * step, step), step)
            run(block, pl.multiple_of(bounds[0, i], 128), bounds[1, i])
            return 0

        lax.fori_loop(0, frames // step, one_block, 0)

    def set_bias(block, span, width):
        same = seg_col[block, :] == seg_row[0:1, span]
        bias[:, 0:width] = jnp.where(same, 0.0, MASKED)

    def shifted(block, low, count):
        def run(width):
            width = width * step
            span = pl.ds(low, width)
            set_bias(block, span, width)
            query, key = q_all[block, :], k_all[span, :]
            above = jnp.zeros((step, lanes), F32)
            below = jnp.ones((step, lanes), F32)
            for head in range(heads):
                masked = jnp.where(lane_mask(lanes, head), query, jnp.zeros_like(query))
                scores = dot(masked, key, NT) + bias[:, 0:width]
                at = head * HEAD_DIM
                weight = jnp.exp(scores - shift[:, at : at + 1]).astype(BF16)
                part = dot(weight, (v_odd if head % 2 else v_even)[span, :])
                above = jnp.where(lane_mask(lanes, head), part, above)
                below = jnp.where(lane_mask(lanes, head ^ 1), part, below)
            sums = swap_heads(below)
            o_all[block, :] = (above / sums).astype(BF16)
            lse[0, block, :] = sums

        each_width(count, frames // step, run)

    def exact(block, low, count):
        query = q_all[block, :]
        highest[...] = jnp.full_like(highest, MASKED)
        total[...] = jnp.zeros_like(total)
        product[...] = jnp.zeros_like(product)

        def one_step(j, _):
            span = pl.ds(pl.multiple_of(low + j * step, 128), step)
            set_bias(block, span, step)
            key, value = k_all[span, :], v_all[span, :]
            for head in range(heads):
                masked = jnp.where(lane_mask(lanes, head), query, jnp.zeros_like(query))
                scores = dot(masked, key, NT) + bias[:, 0:step]
                before = highest[head, :, 0:1]
                top = jnp.maximum(before, jnp.max(scores, axis=1, keepdims=True))
                weight = jnp.exp(scores - top)
                fade = jnp.exp(before - top)
                highest[head] = jnp.broadcast_to(top, (step, 128))
                total[head] = total[head] * fade + jnp.sum(weight, axis=1, keepdims=True)
                product[head] = product[head] * fade + dot(weight.astype(BF16), value)
            return 0

        lax.fori_loop(0, count, one_step, 0)
        result = jnp.zeros((step, lanes), F32)
        logs = jnp.zeros((step, lanes), F32)
        for head in range(heads):
            keep = lane_mask(lanes, head)
            sums = total[head, :, 0:1]
            result = jnp.where(keep, product[head] / sums, result)
            logs = jnp.where(keep, highest[head, :, 0:1] + jnp.log(sums), logs)
        o_all[block, :] = result.astype(BF16)
        lse[0, block, :] = logs

    each_block(shifted)
    safe = jnp.min(lse[0]) > 1e-30

    @pl.when(safe)
    def _():
        lse[0] = shift + jnp.log(lse[0])

    @pl.when(jnp.logical_not(safe))
    def _():
        each_block(exact)

    for piece in range(pieces):
        outs[piece][...] = o_all[pl.ds(piece_start(place, piece, pieces, rows), rows), :]


def attend(place, bounds, seg_col, seg_row, qkv, lanes, step):
    pieces = len(qkv)
    rows, columns = qkv[0].shape
    groups = columns // (3 * lanes)
    heads = lanes // HEAD_DIM
    frames = rows * pieces
    specs = [pl.BlockSpec((rows, 3 * lanes), lambda g: (0, g))] * pieces
    smem = pl.BlockSpec(memory_space=pltpu.SMEM)
    area = frames * frames // 2 * heads * groups
    results = pl.pallas_call(
        functools.partial(attend_kernel, pieces, heads, step),
        grid=(groups,),
        out_shape=[jax.ShapeDtypeStruct((rows, groups * lanes), BF16)] * pieces
        + [jax.ShapeDtypeStruct((groups, frames, lanes), F32)],
        in_specs=[smem, smem, whole(seg_col.shape), whole(seg_row.shape)] + specs,
        out_specs=[pl.BlockSpec((rows, lanes), lambda g: (0, g))] * pieces
        + [pl.BlockSpec((1, frames, lanes), lambda g: (g, 0, 0))],
        scratch_shapes=[pltpu.VMEM((frames, lanes), BF16)] * 6
        + [
            pltpu.VMEM((step, frames), F32),
            pltpu.VMEM((heads, step, 128), F32),
            pltpu.VMEM((heads, step, 128), F32),
            pltpu.VMEM((heads, step, lanes), F32),
        ],
        compiler_params=params(),
        cost_estimate=cost(area * 4 * 256, frames * columns * 4, area),
        name="attend",
    )(place, bounds, seg_col, seg_row, *qkv)
    return results[:pieces], results[pieces]


def attend_back_kernel(pieces, heads, step, place, bounds, seg_col, seg_row, *refs):
    inputs = refs[: 3 * pieces]
    lse = refs[3 * pieces]
    later = refs[3 * pieces + 1 : 4 * pieces + 3]
    out, grad_w = refs[4 * pieces + 3 : 4 * pieces + 5]
    q_all, k_all, v_all, do_all, centre, dq_all, dk_all, dv_all, bias, weights, slopes = refs[
        4 * pieces + 5 : 4 * pieces + 16
    ]
    held, sems = refs[4 * pieces + 16 : -1], refs[-1]
    copies = [
        pltpu.make_async_copy(source, target, sems.at[n])
        for n, (source, target) in enumerate(zip(later, held))
    ]
    for copy in copies:
        copy.start()
    cosine, sine, *normed = held
    rows = inputs[0].shape[0]
    for piece in range(pieces):
        span = pl.ds(piece_start(place, piece, pieces, rows), rows)
        spread(inputs[3 * piece], span, (q_all, k_all, v_all))
        grad = inputs[3 * piece + 2][...]
        do_all[span, :] = grad
        centre[span, :] = head_sums(grad.astype(F32) * inputs[3 * piece + 1][...].astype(F32))
    frames, lanes = q_all.shape
    dk_all[...] = jnp.zeros_like(dk_all)
    dv_all[...] = jnp.zeros_like(dv_all)

    def one_block(i, _):
        block = pl.ds(pl.multiple_of(i * step, step), step)
        low = pl.multiple_of(bounds[0, i], 128)

        def run(width):
            width = width * step
            span = pl.ds(low, width)
            same = seg_col[block, :] == seg_row[0:1, span]
            bias[:, 0:width] = jnp.where(same, 0.0, MASKED)
            query, key, value = q_all[block, :], k_all[span, :], v_all[span, :]
            grad = do_all[block, :]
            queries = stack_heads(query, heads)
            grads = stack_heads(grad, heads)
            for head in range(heads):
                at = slice(head * step, (head + 1) * step)
                column = slice(head * HEAD_DIM, head * HEAD_DIM + 1)
                scores = dot(queries[at], key, NT) + bias[:, 0:width]
                weight = jnp.exp(scores - lse[0, block, column])
                weights[at, 0:width] = weight.astype(BF16)
            for head in range(heads):
                at = slice(head * step, (head + 1) * step)
                column = slice(head * HEAD_DIM, head * HEAD_DIM + 1)
                slope = dot(grads[at], value, NT) - centre[block, column]
                slopes[at, 0:width] = (weights[at, 0:width].astype(F32) * slope).astype(BF16)
            part = dot(slopes[:, 0:width], key)
            result = part[0:step]
            for head in range(1, heads):
                here = part[head * step : (head + 1) * step]
                result = jnp.where(lane_mask(lanes, head), here, result)
            dq_all[block, :] = result * HEAD_DIM**-0.5
            dv_all[span, :] += dot(weights[:, 0:width], grads, TN)
            dk_all[span, :] += dot(slopes[:, 0:width], queries, TN)

        each_width(bounds[1, i], frames // step, run)
        return 0

    lax.fori_loop(0, frames // step, one_block, 0)
    for copy in copies:
        copy.wait()
    for piece in range(pieces):
        span = pl.ds(piece_start(place, piece, pieces, rows), rows)
        cos = cosine[span, :]
        sin = -sine[span, :]
        out[piece, :, 0:lanes] = turn(dq_all[span, :], cos, sin).astype(BF16)
        out[piece, :, lanes : 2 * lanes] = turn(dk_all[span, :], cos, sin).astype(BF16)
        out[piece, :, 2 * lanes : 3 * lanes] = dv_all[span, :].astype(BF16)
    grad_w[...] = sum(dot(normed[p][...], out[p], TN) for p in range(pieces)).astype(BF16)


def attend_back(
    place, bounds, seg_col, seg_row, qkv, attended, grads, lse, cosine, sine, normed, pair, step
):
    pieces = len(qkv)
    rows = qkv[0].shape[0]
    lanes, heads = 128, 128 // HEAD_DIM
    width = normed[0].shape[1]
    per_group = attended[0].shape[1] // lanes // lse.shape[0]
    frames = rows * pieces
    specs, arrays = [], []
    for piece in range(pieces):
        specs.append(pl.BlockSpec((rows, 3 * lanes), lambda i: (0, pair)))
        specs += [pl.BlockSpec((rows, lanes), lambda i: (0, pair))] * 2
        arrays += [qkv[piece], attended[piece], grads[piece]]
    smem = pl.BlockSpec(memory_space=pltpu.SMEM)
    area = frames * frames // 2 * heads
    return pl.pallas_call(
        functools.partial(attend_back_kernel, pieces, heads, step),
        grid=(1,),
        out_shape=[
            jax.ShapeDtypeStruct((pieces, rows, 3 * lanes), BF16),
            jax.ShapeDtypeStruct((width, 3 * lanes), BF16),
        ],
        in_specs=[smem, smem, whole(seg_col.shape, 1), whole(seg_row.shape, 1)]
        + specs
        + [
            pl.BlockSpec(
                (1, frames, 128),
                lambda i: (pair // per_group, 0, pair % per_group),
                pipeline_mode=pl.Buffered(1),
            ),
        ]
        + [pl.BlockSpec(memory_space=pl.ANY)] * (pieces + 2),
        out_specs=[whole((pieces, rows, 3 * lanes), 1), whole((width, 3 * lanes), 1)],
        scratch_shapes=[pltpu.VMEM((frames, lanes), BF16)] * 4
        + [pltpu.VMEM((frames, lanes), F32)] * 4
        + [pltpu.VMEM((step, frames), F32)]
        + [pltpu.VMEM((heads * step, frames), BF16)] * 2
        + [pltpu.VMEM(cosine.shape, F32)] * 2
        + [pltpu.VMEM(normed[0].shape, BF16)] * pieces
        + [pltpu.SemaphoreType.DMA((pieces + 2,))],
        compiler_params=params(),
        cost_estimate=cost(area * 10 * 256, frames * lanes * 16, area),
        name="attend_back",
    )(place, bounds, seg_col, seg_row, *arrays, lse, cosine, sine, *normed)


def gelu_pair(h):
    root = math.sqrt(2.0 / math.pi)
    square = h * h
    bend = jnp.tanh(root * h * (1.0 + 0.044715 * square))
    half = 0.5 * (1.0 + bend)
    slope = half + 0.5 * h * (1.0 - bend * bend) * (root * (1.0 + 0.134145 * square))
    return h * half, slope


def flat(ref, span=slice(None)):
    value = ref[:, 0, :, span]
    return value.reshape(value.shape[0] * value.shape[1], value.shape[2])


def middle_kernel(pieces, place, *refs):
    x, member, member_flip, adaptive, dy = refs[:5]
    refs = refs[5:]
    attended, refs = refs[:pieces], refs[pieces:]
    w_out, refs = refs[:pieces], refs[pieces:]
    w_up, refs = refs[:pieces], refs[pieces:]
    w_down, refs = refs[:pieces], refs[pieces:]
    mixed, dx2, a2_out, d2_out, d1_out, dadaptive = refs[:6]
    refs = refs[6:]
    active, refs = refs[:pieces], refs[pieces:]
    dhidden, refs = refs[:pieces], refs[pieces:]
    dattended = refs[:pieces]
    width = x.shape[1]
    here = member[...]
    gate1, shift2, scale2, gate2 = (
        pick(here, adaptive[:, n * width : (n + 1) * width]) for n in (2, 3, 4, 5)
    )
    branch1 = sum(dot(attended[p][...], flat(w_out[p]), NT) for p in range(pieces))
    x2 = x[...].astype(F32) + gate1 * branch1
    n2, r2 = norm(x2)
    a2 = (n2 * (1.0 + scale2) + shift2).astype(BF16)
    a2_out[...] = a2
    branch2 = jnp.zeros_like(x2)
    slopes = []
    for p in range(pieces):
        value, slope = gelu_pair(dot(a2, flat(w_up[p])))
        value = value.astype(BF16)
        active[p][...] = value
        slopes.append(slope)
        branch2 = branch2 + dot(value, flat(w_down[p]), NT)
    mixed[...] = (x2 + gate2 * branch2).astype(BF16)
    upstream = dy[...].astype(F32)
    d2 = (upstream * gate2).astype(BF16)
    d2_out[...] = d2
    da2 = jnp.zeros_like(x2)
    for p in range(pieces):
        dh = (dot(d2, flat(w_down[p])) * slopes[p]).astype(BF16)
        dhidden[p][...] = dh
        da2 = da2 + dot(dh, flat(w_up[p]), NT)
    u2 = da2 * (1.0 + scale2)
    back = upstream + r2 * (
        u2 - jnp.mean(u2, axis=-1, keepdims=True) - n2 * jnp.mean(u2 * n2, axis=-1, keepdims=True)
    )
    dx2[...] = back
    d1 = (back * gate1).astype(BF16)
    d1_out[...] = d1
    for p in range(pieces):
        dattended[p][...] = dot(d1, flat(w_out[p])).astype(BF16)

    @pl.when(pl.program_id(0) == 0)
    def _():
        dadaptive[...] = jnp.zeros_like(dadaptive)

    for n, term in enumerate((back * branch1, da2, da2 * n2, upstream * branch2)):
        dadaptive[:, n * width : (n + 1) * width] += gather(member_flip[...], term)


def middle(place, x, member, member_flip, adaptive, dy, attended, weights):
    pieces = len(attended)
    rows, width = x.shape
    head_columns = attended[0].shape[1]
    hidden = 2 * head_columns
    tile = min(256, rows)

    def tiled(columns):
        return pl.BlockSpec((tile, columns), lambda i, s: (i, 0))

    def shaped(columns, kind):
        return jax.ShapeDtypeStruct((rows, columns), kind)

    shards, slices, own_rows, _ = weights.shape

    def resident(columns, at):
        return [
            pl.BlockSpec(
                (shards, 1, own_rows, columns),
                lambda i, s, piece=piece: (0, lax.rem(s[0] + piece, slices), 0, at),
                pipeline_mode=pl.Buffered(1),
            )
            for piece in range(pieces)
        ]

    cuts = resident(head_columns, 4) + resident(hidden, 0) + resident(hidden, 1)
    work = 2 * rows * width * pieces * (3 * hidden * 2 + head_columns * 2)
    results = pl.pallas_call(
        functools.partial(middle_kernel, pieces),
        grid_spec=pltpu.PrefetchScalarGridSpec(
        num_scalar_prefetch=1,
        grid=(rows // tile,),
        in_specs=[
            tiled(width),
            tiled(32),
            pl.BlockSpec((16, tile), lambda i, s: (0, i)),
            whole(adaptive.shape, 1),
            tiled(width),
        ]
        + [tiled(head_columns)] * pieces
        + cuts,
        out_specs=[tiled(width)] * 5
        + [whole((8, 4 * width))]
        + [tiled(hidden)] * (2 * pieces)
        + [tiled(head_columns)] * pieces,
        ),
        out_shape=[
            shaped(width, BF16),
            shaped(width, F32),
            shaped(width, BF16),
            shaped(width, BF16),
            shaped(width, BF16),
            jax.ShapeDtypeStruct((8, 4 * width), F32),
        ]
        + [shaped(hidden, BF16)] * (2 * pieces)
        + [shaped(head_columns, BF16)] * pieces,
        compiler_params=params(),
        cost_estimate=cost(work, rows * width * 30, rows * hidden * pieces),
        name="middle",
    )(place, x, member, member_flip, adaptive, dy, *attended, *[weights] * (3 * pieces))
    head, rest = results[:6], results[6:]
    return head, rest[:pieces], rest[pieces : 2 * pieces], rest[2 * pieces :]


def part_kernel(groups, *refs):
    slopes, weights, out = refs[:groups], refs[groups], refs[-1]
    slope = jnp.concatenate([slope[...] for slope in slopes], axis=1)
    out[...] = dot(slope, weights[...], NT).astype(BF16)


def input_part(slopes, weights, piece):
    rows, columns = slopes[0].shape[1:]
    width = weights.shape[0]
    tile = min(256, rows)
    groups = len(slopes)
    return pl.pallas_call(
        functools.partial(part_kernel, groups),
        grid=(rows // tile,),
        in_specs=[pl.BlockSpec((None, tile, columns), lambda i: (piece, i, 0))] * groups
        + [whole(weights.shape, 1)],
        out_shape=jax.ShapeDtypeStruct((rows, width), BF16),
        out_specs=pl.BlockSpec((tile, width), lambda i: (i, 0)),
        compiler_params=params(),
        cost_estimate=cost(2 * rows * width * columns * groups, rows * width * 8),
        name="input_part",
    )(*slopes, weights)


def last_kernel(groups, arrivals, *refs):
    x, member, member_flip, adaptive, dx2 = refs[:5]
    refs = refs[5:]
    arrived, refs = refs[:arrivals], refs[arrivals:]
    slopes, refs = refs[:groups], refs[groups:]
    weights, grad, dadaptive = refs
    width = x.shape[1]
    normed, inverse = norm(x[...].astype(F32))
    scale = pick(member[...], adaptive[:, width : 2 * width])
    slope = jnp.concatenate([slope[...] for slope in slopes], axis=1)
    da1 = dot(slope, weights[...], NT)
    for piece in arrived:
        da1 = da1 + piece[...].astype(F32)
    u1 = da1 * (1.0 + scale)
    back = inverse * (
        u1
        - jnp.mean(u1, axis=-1, keepdims=True)
        - normed * jnp.mean(u1 * normed, axis=-1, keepdims=True)
    )
    grad[...] = (dx2[...] + back).astype(BF16)

    @pl.when(pl.program_id(0) == 0)
    def _():
        dadaptive[...] = jnp.zeros_like(dadaptive)

    dadaptive[:, :width] += gather(member_flip[...], da1)
    dadaptive[:, width:] += gather(member_flip[...], da1 * normed)


def last(half, x, member, member_flip, adaptive, dx2, arrived, slopes, weights):
    rows, width = x.shape[0] // 2, x.shape[1]
    tile = min(256, rows)
    first = half * (rows // tile)

    def tiled(columns):
        return pl.BlockSpec((tile, columns), lambda i: (first + i, 0))

    return pl.pallas_call(
        functools.partial(last_kernel, len(slopes), len(arrived)),
        grid=(rows // tile,),
        in_specs=[
            tiled(width),
            tiled(32),
            pl.BlockSpec((16, tile), lambda i: (0, first + i)),
            whole(adaptive.shape, 1),
            tiled(width),
        ]
        + [tiled(width)] * len(arrived)
        + [pl.BlockSpec((None, tile, s.shape[2]), lambda i: (0, first + i, 0)) for s in slopes]
        + [whole(weights.shape, 1)],
        out_shape=[
            jax.ShapeDtypeStruct((rows, width), BF16),
            jax.ShapeDtypeStruct((8, 2 * width), F32),
        ],
        out_specs=[pl.BlockSpec((tile, width), lambda i: (i, 0)), whole((8, 2 * width))],
        compiler_params=params(),
        cost_estimate=cost(2 * rows * width * sum(s.shape[2] for s in slopes), rows * width * 12),
        name="last",
    )(x, member, member_flip, adaptive, dx2, *arrived, *slopes, weights)


def time_vector(steps, width):
    halfway = width // 2
    rates = jnp.exp(jnp.arange(halfway, dtype=F32) * (-math.log(10000.0) / (halfway - 1)))
    angles = steps.astype(F32)[:, None] * rates[None, :]
    return jnp.concatenate([jnp.sin(angles), jnp.cos(angles)], axis=1)


def body(frames, clip_lengths, timesteps, w_qkv, w_out, w_up, w_down, w_ada, b_ada, grad_out):
    rows, width = frames.shape
    clips = clip_lengths.shape[0]
    pieces = lax.axis_size("hl") * 2
    group_rows = rows * pieces
    own_rows = w_qkv.shape[1]
    head_columns = width // pieces
    lanes = min(256, head_columns)
    pairs = head_columns // 128
    step = min(256, group_rows)
    place = lax.axis_index(SUB).astype(jnp.int32)

    qkv_shard = w_qkv.astype(BF16).reshape(3, own_rows, pairs, 128)
    qkv_shard = jnp.transpose(qkv_shard, (1, 2, 0, 3)).reshape(own_rows, 3 * head_columns)
    mlp_shard = jnp.concatenate(
        [w_up.astype(BF16), w_down.astype(BF16).T, w_out.astype(BF16).T], axis=1
    )
    qkv_shard = moved(qkv_shard)
    lengths = moved(clip_lengths)

    def around(value):
        return [value] + [from_sub(value, step) for step in range(1, pieces)]

    condition = jax.nn.silu(time_vector(timesteps, width))
    columns = w_ada.shape[1]
    devices = [lax.axis_size(axis) for axis in ALL]
    za, zb, cores, hh, hl = devices
    table = (
        jnp.dot(condition, lax.reduce_precision(w_ada, 8, 7), precision=HIGHEST)
        + lax.reduce_precision(b_ada, 8, 7)[None, :]
    )
    table, qkv_shard, lengths = together(table, qkv_shard, lengths)
    table = table.reshape(za, zb, 1, hh, 1, clips, columns)
    table = jnp.broadcast_to(table, (za, zb, cores, hh, hl, clips, columns))
    table = lax.all_to_all(table.reshape(-1, clips, columns), ALL, 0, 0, tiled=True)
    adaptive = jnp.transpose(table, (1, 0, 2)).reshape(clips, -1)
    adaptive = jnp.pad(adaptive, ((0, 8 - clips), (0, 0)))

    ends = jnp.cumsum(lengths, dtype=jnp.int32)
    starts = ends - lengths
    index = jnp.arange(group_rows, dtype=jnp.int32)
    segment = jnp.sum((index[:, None] >= ends[None, :]).astype(jnp.int32), axis=1, dtype=jnp.int32)
    edges = jnp.concatenate([jnp.zeros((1,), jnp.int32), ends])
    begins = jnp.max(jnp.where(index[:, None] >= edges[None, :], edges[None, :], 0), axis=1)
    position = (index - begins).astype(F32)
    lane = jnp.arange(128, dtype=jnp.int32) % HEAD_DIM
    rates = jnp.exp((lane % (HEAD_DIM // 2)).astype(F32) * (-2.0 * math.log(10000.0) / HEAD_DIM))
    angles = position[:, None] * rates[None, :]
    cosine = jnp.cos(angles)
    sine = jnp.sin(angles) * jnp.where(lane < HEAD_DIM // 2, -1.0, 1.0)[None, :]
    seg_col = segment[:, None]
    seg_row = segment[None, :]
    block_first = jnp.arange(0, group_rows, step, dtype=jnp.int32)
    first_seg = jnp.sum((block_first[:, None] >= ends[None, :]).astype(jnp.int32), axis=1)
    last_seg = jnp.sum((block_first[:, None] + (step - 1) >= ends[None, :]).astype(jnp.int32), axis=1)
    closing = jnp.concatenate([ends, jnp.full((1,), group_rows, jnp.int32)])
    low_at = jnp.sum(jnp.where(first_seg[:, None] == jnp.arange(clips + 1)[None, :], edges[None, :], 0), axis=1)
    high_at = jnp.sum(jnp.where(last_seg[:, None] == jnp.arange(clips + 1)[None, :], closing[None, :], 0), axis=1)
    low_at = low_at // 128 * 128
    widths = (high_at - low_at + step - 1) // step
    low_at = jnp.minimum(low_at, group_rows - widths * step)
    bounds = jnp.stack([low_at, widths]).astype(jnp.int32)
    own_index = place * rows + jnp.arange(rows, dtype=jnp.int32)
    member = ((own_index[:, None] >= starts[None, :]) & (own_index[:, None] < ends[None, :])).astype(F32)
    member = jnp.pad(member, ((0, 0), (0, 8 - clips))).astype(BF16)
    member_flip = jnp.pad(member.T, ((0, 8), (0, 0)))
    member = jnp.concatenate([member, member, member, jnp.zeros_like(member)], axis=1)

    x = moved(frames)
    held = gather_line(qkv_shard)
    held, adaptive, x, cosine, sine, member, mlp_shard = together(
        held, adaptive, x, cosine, sine, member, mlp_shard
    )
    near = gather_near(held)
    mlp_full = lax.all_gather(mlp_shard, ALL, axis=0, tiled=True)
    mlp_full = mlp_full.reshape(-1, pieces, own_rows, mlp_shard.shape[1])
    a1 = first_norm(x, member, adaptive)
    near, a1, grad_out = together(near, a1, grad_out)
    far, a1_all = together(gather_far(*near), around(a1))
    qkv_full = gathered(*far)
    places = [((place + piece) % pieces).reshape(1) for piece in range(pieces)]
    qkv = [
        project(places[piece], a1_all[piece], qkv_full, cosine, sine, lanes)
        for piece in range(pieces)
    ]
    at_place = place.reshape(1)
    qkv, grad_out = together(qkv, grad_out)
    dy = moved(grad_out)
    attended, lse = attend(at_place, bounds, seg_col, seg_row, qkv, lanes, step)
    attended, lse, dy = together(attended, lse, dy)
    attended_own = [attended[0]] + [
        from_sub_piece(attended, step_) for step_ in range(1, pieces)
    ]

    head, active, dhidden, dattended = middle(
        at_place, x, member, member_flip, adaptive, dy, attended_own, mlp_full
    )
    mixed, dx2, a2, d2, d1, dada_late = head
    grads_attended = [dattended[0]] + [
        from_sub_piece(dattended, step_) for step_ in range(1, pieces)
    ]
    mixed_back = moved(mixed)

    def summed(left, right):
        parts = [dot(left, part, TN).astype(BF16) for part in right]
        return [parts[0]] + [to_sub(parts[step], step) for step in range(1, pieces)]

    late = [summed(a2, dhidden), summed(d2, active), summed(d1, attended_own)]

    def back(pair, qkv):
        return attend_back(
            at_place, bounds, seg_col, seg_row, qkv, attended, grads_attended, lse, cosine, sine,
            a1_all, pair, step,
        )

    slopes, grads_qkv = [], []
    early = final = None

    def next_pair():
        slope, grad = back(len(slopes), qkv)
        slopes.append(slope)
        grads_qkv.append(grad)

    next_pair()
    late, slopes, grads_qkv, mixed_back = together(late, slopes, grads_qkv, mixed_back)
    late, qkv = together(cut_plane(late), qkv)
    late = swap_plane(late)
    while len(slopes) < pairs - 1:
        next_pair()
    if pairs > 1:
        early = cut_plane([[grad] for grad in grads_qkv])
    late, early, slopes, grads_qkv = together(late, early, slopes, grads_qkv)
    late, qkv = together(cut_line(add_up(late), 1), qkv)
    late = swap_line(late, 1)
    if pairs > 1:
        early = swap_plane(early)
        next_pair()
    late, early, slopes, grads_qkv = together(late, early, slopes, grads_qkv)
    final = cut_plane([grads_qkv[-1:]])
    late = add_up(late)
    if pairs > 1:
        early = cut_line(add_up(early), 1)
    final, early, late, slopes, dx2 = together(final, early, late, slopes, dx2)
    final = swap_plane(final)
    late = line_rest([late])
    if pairs > 1:
        early = swap_line(early, 1)
    parts = [input_part(slopes, qkv_full, piece) for piece in range(1, pieces)]
    final, early, late, parts = together(final, early, late, parts)
    arrived = [to_sub(part, piece) for piece, part in enumerate(parts, 1)]
    final = line_rest(final)
    sums = [late]
    if pairs > 1:
        sums.append(line_rest(early))
    final, sums, arrived, dx2 = together(final, sums, arrived, dx2)
    sums = moved(jnp.concatenate(sums + [final], axis=1))
    def rows_half(half, dx2):
        return last(half, x, member, member_flip, adaptive, dx2, arrived, slopes, qkv_full)

    sums, dx2, (frames_low, dada_low) = together(sums, dx2, rows_half(0, dx2))
    frames_low, (frames_high, dada_high) = together(moved(frames_low), rows_half(1, dx2))
    dada_early = dada_low + dada_high
    late, rest = sums[:, : mlp_shard.shape[1]], sums[:, mlp_shard.shape[1] :]
    hidden_columns = w_up.shape[1]
    grad_up = late[:, :hidden_columns]
    grad_down = late[:, hidden_columns : 2 * hidden_columns]
    grad_outw = late[:, 2 * hidden_columns :]
    dadaptive = jnp.concatenate([dada_early, dada_late], axis=1)[:clips]
    dadaptive = jnp.transpose(dadaptive.reshape(clips, -1, columns), (1, 0, 2))
    dadaptive, frames_high = together(dadaptive, frames_high)
    dadaptive = lax.all_to_all(dadaptive, ALL, 0, 0, tiled=True)
    grad_frames = jnp.concatenate([frames_low, moved(frames_high)], axis=0).astype(F32)
    dadaptive = dadaptive.reshape(za, zb, cores, hh, hl, clips, columns)
    dadaptive = jnp.sum(dadaptive, axis=(2, 4)).reshape(-1, columns)
    grad_ada = dot(condition, dadaptive, TN, HIGHEST)
    grad_bias = jnp.sum(dadaptive, axis=0)

    grad_qkv = rest.reshape(own_rows, pairs, 3, 128)
    grad_qkv = jnp.transpose(grad_qkv, (2, 0, 1, 3)).reshape(w_qkv.shape).astype(F32)
    return (
        mixed_back,
        grad_frames,
        grad_qkv,
        grad_outw.astype(F32).T,
        grad_up.astype(F32),
        grad_down.astype(F32).T,
        grad_ada,
        grad_bias,
    )


def from_sub_piece(parts, step):
    pieces = len(parts)
    return from_sub(parts[pieces - step], step)


def solution(mesh):
    clip, head = mesh.shape["clip"], mesh.shape["head"]
    fine = Mesh(mesh.devices.reshape(clip // 4, 2, 2, 2, head // 2), ALL)
    by_clip = ("za", "zb", "core")
    by_head = ("hh", "hl")
    everywhere = by_clip + by_head
    placed = (
        P(everywhere, None),
        P(by_clip),
        P(),
        P(None, by_clip, by_head),
        P(by_head, by_clip),
        P(by_clip, by_head),
        P(by_head, by_clip),
        P(None, everywhere),
        P(everywhere),
        P(everywhere, None),
    )
    return jax.shard_map(
        body,
        mesh=fine,
        in_specs=placed,
        out_specs=(
            P(everywhere, None),
            P(everywhere, None),
            P(None, by_clip, by_head),
            P(by_head, by_clip),
            P(by_clip, by_head),
            P(by_head, by_clip),
            P(None, everywhere),
            P(everywhere),
        ),
        check_vma=False,
    )
```

```python
import functools
import math

import jax
import jax.numpy as jnp
from jax import lax
from jax.experimental import pallas as pl
from jax.experimental.pallas import tpu as pltpu
from jax.sharding import Mesh
from jax.sharding import PartitionSpec as P

HEAD_DIM = 64
HEADS = 16
HIGHEST = lax.Precision.HIGHEST
MASKED = -1e30
EPSILON = 1e-06
VMEM_LIMIT = 60 * 1024 * 1024
F32 = jnp.float32
BF16 = jnp.bfloat16

ALL = ("za", "zb", "core", "hh", "hl")
MOVE = ("core", "hh", "hl")
SUB = ("core", "hl")

NT = (((1,), (1,)), ((), ()))
NN = (((1,), (0,)), ((), ()))
TN = (((0,), (0,)), ((), ()))


def dot(a, b, dims=NN, precision=None):
    return lax.dot_general(a, b, dims, precision=precision, preferred_element_type=F32)


def params(**more):
    return pltpu.CompilerParams(vmem_limit_bytes=VMEM_LIMIT, **more)


def cost(flops, bytes_accessed, transcendentals=0):
    return pl.CostEstimate(
        flops=int(flops), bytes_accessed=int(bytes_accessed), transcendentals=int(transcendentals)
    )


def whole(shape, buffers=None):
    zeros = (0,) * len(shape)
    if buffers is None:
        return pl.BlockSpec(shape, lambda *_: zeros)
    return pl.BlockSpec(shape, lambda *_: zeros, pipeline_mode=pl.Buffered(buffers))


def sent(value):
    return lax.ppermute(value, ("core", "hh"), [(1, 2), (2, 1)])


def staying():
    return lax.axis_index("core") == lax.axis_index("hh")


def moved(value):
    return jnp.where(staying(), value, sent(value))


def from_sub(value, step):
    size = lax.axis_size("hl") * 2
    return lax.ppermute(value, SUB, [((d + step) % size, d) for d in range(size)])


def to_sub(value, step):
    size = lax.axis_size("hl") * 2
    return lax.ppermute(value, SUB, [(d, (d + step) % size) for d in range(size)])


SWAP = [(0, 1), (1, 0)]


def across(value, bit):
    size = lax.axis_size("za")
    return lax.ppermute(value, "za", [(i, i ^ bit) for i in range(size)])


def gather_line(shard):
    return jnp.stack([shard] + [across(shard, bits) for bits in range(1, lax.axis_size("za"))])


def gather_near(held):
    return held, lax.ppermute(held, "zb", SWAP), lax.ppermute(held, "hh", SWAP)


def gather_far(held, by_zb, by_hh):
    half = held.shape[0] // 2
    both_low = lax.ppermute(by_zb[:half], "hh", SWAP)
    both_high = lax.ppermute(by_hh[half:], "zb", SWAP)
    return held, by_zb, by_hh, both_low, both_high


FOUR = ((0, 0), (1, 0), (0, 1), (1, 1))


def cut_kernel(counts, where, *refs):
    outs = refs[-4:]
    zb, hh = where[0], where[1]
    first = start = 0
    for count in counts:
        terms = refs[first : first + count]
        columns = terms[0].shape[-1]
        for out, (dz, dh) in zip(outs, FOUR):
            z, h = lax.rem(zb + dz, 2), lax.rem(hh + dh, 2)
            part = terms[0][0, z, h]
            if count > 1:
                part = sum(term[0, z, h].astype(F32) for term in terms).astype(BF16)
            out[0, :, start : start + columns] = part
        first += count
        start += columns


def cut_plane(weights):
    size = lax.axis_size("za")
    where = jnp.stack([lax.axis_index("zb"), lax.axis_index("hh")]).astype(jnp.int32)
    terms = [term for group in weights for term in group]
    rows = terms[0].shape[0] // (size * 4)
    total = sum(group[0].shape[1] for group in weights)
    return pl.pallas_call(
        functools.partial(cut_kernel, [len(group) for group in weights]),
        grid_spec=pltpu.PrefetchScalarGridSpec(
            num_scalar_prefetch=1,
            grid=(size,),
            in_specs=[
                pl.BlockSpec((1, 2, 2, rows, term.shape[1]), lambda i, w: (i, 0, 0, 0, 0))
                for term in terms
            ],
            out_specs=[pl.BlockSpec((1, rows, total), lambda i, w: (i, 0, 0))] * 4,
        ),
        out_shape=[jax.ShapeDtypeStruct((size, rows, total), BF16)] * 4,
        compiler_params=params(),
        cost_estimate=cost(0, sum(2 * term.size for term in terms) + size * 8 * rows * total),
        name="cut",
    )(where, *[term.reshape(size, 2, 2, rows, -1) for term in terms])


def swap_plane(pieces):
    own, to_zb, to_hh, to_both = pieces
    from_both = lax.ppermute(to_both, ("zb", "hh"), [(0, 3), (1, 2), (2, 1), (3, 0)])
    from_hh = lax.ppermute(to_hh, "hh", SWAP)
    from_zb = lax.ppermute(to_zb, "zb", SWAP)
    return own, from_zb, from_hh, from_both


def add_up(pieces):
    return sum(piece.astype(F32) for piece in pieces).astype(BF16)


def cut_line(total, bit):
    pairs = total.reshape(total.shape[0] // 2, 2, *total.shape[1:])
    place = (lax.axis_index("za") // bit) % 2
    keep = lax.dynamic_index_in_dim(pairs, place, 1, keepdims=False)
    send = lax.dynamic_index_in_dim(pairs, 1 - place, 1, keepdims=False)
    return keep, send


def swap_line(cuts, bit):
    return cuts[0], across(cuts[1], bit)


def line_rest(pieces):
    total = add_up(pieces)
    count = total.shape[0]
    apart = lax.axis_size("za") // count
    mine = lax.axis_index("za") // apart
    cuts = [lax.dynamic_index_in_dim(total, mine ^ n, 0, keepdims=False) for n in range(count)]
    return [cuts[0]] + [across(cut, n * apart) for n, cut in enumerate(cuts) if n]


def together(*values):
    return lax.optimization_barrier(values)


def norm(values):
    centred = values - jnp.mean(values, axis=-1, keepdims=True)
    variance = jnp.mean(centred * centred, axis=-1, keepdims=True)
    inverse = lax.rsqrt(variance + EPSILON)
    return centred * inverse, inverse


def pick(member, table):
    high = table.astype(BF16)
    rest = table - high.astype(F32)
    middle = rest.astype(BF16)
    low = (rest - middle.astype(F32)).astype(BF16)
    return dot(member, jnp.concatenate([high, middle, low, jnp.zeros_like(low)], axis=0))


def gather(member_flip, term):
    high = term.astype(BF16)
    low = (term - high.astype(F32)).astype(BF16)
    return (dot(member_flip, high) + dot(member_flip, low))[0:8]


def first_norm_kernel(stays, there, here, member, adaptive, out, x):
    width = x.shape[1]
    x[...] = jnp.where(stays[0] == 1, there[...], here[...])
    normed, _ = norm(x[...].astype(F32))
    shift = pick(member[...], adaptive[:, :width])
    scale = pick(member[...], adaptive[:, width : 2 * width])
    out[...] = (normed * (1.0 + scale) + shift).astype(BF16)


def first_norm(stays, there, here, member, adaptive):
    rows, width = here.shape
    tile = min(256, rows)
    tiled = pl.BlockSpec((tile, width), lambda i: (i, 0))
    return pl.pallas_call(
        first_norm_kernel,
        grid=(rows // tile,),
        out_shape=[jax.ShapeDtypeStruct((rows, width), BF16)] * 2,
        in_specs=[
            pl.BlockSpec(memory_space=pltpu.SMEM),
            tiled,
            tiled,
            pl.BlockSpec((tile, 32), lambda i: (i, 0)),
            whole(adaptive.shape),
        ],
        out_specs=[tiled, tiled],
        compiler_params=params(),
        cost_estimate=cost(rows * width * 40, rows * width * 8),
        name="first_norm",
    )(stays, there, here, member, adaptive)


def turn(values, cosine, sine):
    lanes = values.shape[1]
    place = lax.broadcasted_iota(jnp.int32, (1, 128), 1) % HEAD_DIM
    first = place < HEAD_DIM // 2
    parts = []
    for at in range(0, lanes, 128):
        part = values[:, at : at + 128]
        ahead = pltpu.roll(part, 128 - HEAD_DIM // 2, 1)
        behind = pltpu.roll(part, HEAD_DIM // 2, 1)
        swapped = jnp.where(first, ahead, behind)
        parts.append(part * cosine + swapped * sine)
    return parts[0] if len(parts) == 1 else jnp.concatenate(parts, axis=1)


def project_kernel(pieces, tiles, lanes, where, *refs):
    a_refs, refs = refs[:pieces], refs[pieces:]
    own, by_zb, by_hh, both_low, both_high, cosine, sine, out, w, a, weights = refs
    size, rows, columns = own.shape
    i = pl.program_id(0)

    @pl.when(i == 0)
    def _():
        zb, hh = where[0], where[1]
        for n in range(size):
            z = where[2 + n]
            low = n < size // 2
            both = both_low[n] if low else both_high[n - size // 2]
            shards = ((zb, hh, own[n]), (1 - zb, hh, by_zb[n]), (zb, 1 - hh, by_hh[n]))
            for at_zb, at_hh, shard in shards + ((1 - zb, 1 - hh, both),):
                start = pl.multiple_of(((z * 2 + at_zb) * 2 + at_hh) * rows, rows)
                weights[pl.ds(start, rows), :] = shard
        w[...] = weights[...]

    for piece in range(pieces):

        @pl.when(i // tiles == piece)
        def _(piece=piece):
            a[...] = a_refs[piece][...]

    for start in range(0, columns, 3 * lanes):
        products = dot(a[...], weights[:, start : start + 3 * lanes])
        for at in range(0, 3 * lanes, 128):
            product = products[:, at : at + 128]
            kind = at // 128 % 3
            if kind < 2:
                product = turn(product, cosine[...], sine[...])
            if kind == 0:
                product = product * HEAD_DIM**-0.5
            out[:, start + at : start + at + 128] = product.astype(BF16)


def project(place, a_all, shards, cosine, sine, lanes):
    pieces = len(a_all)
    rows, width = a_all[0].shape
    size, own_rows, columns = shards[0].shape
    tile = min(256, rows)
    tiles = rows // tile
    where = [lax.axis_index("zb"), lax.axis_index("hh")]
    where += [lax.axis_index("za") ^ bits for bits in range(size)]
    where += [(place + piece) % pieces for piece in range(pieces)]
    where = jnp.stack(where).astype(jnp.int32)

    def rows_of(piece):
        return pl.BlockSpec(
            (tile, width), lambda i, w: (jnp.clip(i - piece * tiles, 0, tiles - 1), 0)
        )

    def tables():
        return pl.BlockSpec(
            (tile, 128), lambda i, w: (w[2 + size + i // tiles] * tiles + lax.rem(i, tiles), 0)
        )

    return pl.pallas_call(
        functools.partial(project_kernel, pieces, tiles, lanes),
        grid_spec=pltpu.PrefetchScalarGridSpec(
            num_scalar_prefetch=1,
            grid=(pieces * tiles,),
            in_specs=[rows_of(piece) for piece in range(pieces)]
            + [whole(shard.shape, 1) for shard in shards]
            + [tables(), tables()],
            out_specs=[
                pl.BlockSpec((None, tile, columns), lambda i, w: (i // tiles, lax.rem(i, tiles), 0)),
                whole((width, columns), 1),
            ],
            scratch_shapes=[pltpu.VMEM((tile, width), BF16), pltpu.VMEM((width, columns), BF16)],
        ),
        out_shape=[
            jax.ShapeDtypeStruct((pieces, rows, columns), BF16),
            jax.ShapeDtypeStruct((width, columns), BF16),
        ],
        compiler_params=params(),
        cost_estimate=cost(2 * pieces * rows * width * columns, pieces * rows * (width + columns) * 2),
        name="project",
    )(where, *a_all, *shards, cosine, sine)


def stack_heads(values, heads):
    none = jnp.zeros_like(values)
    lanes = values.shape[1]
    return jnp.concatenate(
        [jnp.where(lane_mask(lanes, head), values, none) for head in range(heads)], axis=0
    )


def lane_mask(lanes, head):
    return lax.broadcasted_iota(jnp.int32, (1, lanes), 1) // HEAD_DIM == head


def piece_start(place, piece, pieces, rows):
    return pl.multiple_of(lax.rem(place[0] + piece, pieces) * rows, rows)


def flip(values):
    return jnp.transpose(values.astype(F32))


def spread(ref, span, arrays):
    for at in range(0, ref.shape[1], 128):
        start = at // 384 * 128
        arrays[at // 128 % 3][span, start : start + 128] = ref[:, at : at + 128]


def each_width(count, limit, run):
    for width in range(1, limit + 1):

        @pl.when(count == width)
        def _(width=width):
            run(width)


def head_sums(values):
    lanes = values.shape[1]
    row = lax.broadcasted_iota(jnp.int32, (lanes, lanes), 0) // HEAD_DIM
    column = lax.broadcasted_iota(jnp.int32, (lanes, lanes), 1) // HEAD_DIM
    same = (row == column).astype(BF16)
    high = values.astype(BF16)
    low = (values - high.astype(F32)).astype(BF16)
    return dot(high, same) + dot(low, same)


def swap_heads(values):
    parts = [pltpu.roll(values[:, at : at + 128], HEAD_DIM, 1) for at in range(0, values.shape[1], 128)]
    return parts[0] if len(parts) == 1 else jnp.concatenate(parts, axis=1)


def largest_sum(ref, step):
    lanes = ref.shape[1]
    row = lax.broadcasted_iota(jnp.int32, (lanes, lanes), 0) // HEAD_DIM
    column = lax.broadcasted_iota(jnp.int32, (lanes, lanes), 1) // HEAD_DIM
    same = (row == column).astype(BF16)
    largest = jnp.zeros((1, lanes), F32)
    for at in range(0, ref.shape[0], step):
        values = ref[at : at + step, :]
        sums = dot(values * values, same)
        largest = jnp.maximum(largest, jnp.max(sums, axis=0, keepdims=True))
    return largest


def attend_kernel(pieces, heads, step, place, bounds, seg_col, seg_row, *refs):
    inputs = refs[:pieces]
    outs = refs[pieces : 2 * pieces]
    lse, q_all, k_all, v_all, v_even, v_odd, o_all, bias, highest, total, product = refs[2 * pieces :]
    rows = inputs[0].shape[0]
    frames, lanes = q_all.shape
    even = lax.broadcasted_iota(jnp.int32, (1, lanes), 1) // HEAD_DIM % 2 == 0
    for piece in range(pieces):
        span = pl.ds(piece_start(place, piece, pieces, rows), rows)
        spread(inputs[piece], span, (q_all, k_all, v_all))
        value = v_all[span, :]
        v_even[span, :] = jnp.where(even, value, jnp.ones_like(value))
        v_odd[span, :] = jnp.where(even, jnp.ones_like(value), value)
    limit = jnp.sqrt(largest_sum(q_all, 2 * step) * largest_sum(k_all, 2 * step))
    shift = limit * 1.02 - 60.0

    def each_block(run):
        def one_block(i, _):
            block = pl.ds(pl.multiple_of(i * step, step), step)
            run(block, pl.multiple_of(bounds[0, i], 128), bounds[1, i])
            return 0

        lax.fori_loop(0, frames // step, one_block, 0)

    def set_bias(block, span, width):
        same = seg_col[block, :] == seg_row[0:1, span]
        bias[:, 0:width] = jnp.where(same, 0.0, MASKED)

    def shifted(block, low, count):
        def run(width):
            width = width * step
            span = pl.ds(low, width)
            set_bias(block, span, width)
            query, key = q_all[block, :], k_all[span, :]
            above = jnp.zeros((step, lanes), F32)
            below = jnp.ones((step, lanes), F32)
            for head in range(heads):
                masked = jnp.where(lane_mask(lanes, head), query, jnp.zeros_like(query))
                scores = dot(masked, key, NT) + bias[:, 0:width]
                at = head * HEAD_DIM
                weight = jnp.exp(scores - shift[:, at : at + 1]).astype(BF16)
                part = dot(weight, (v_odd if head % 2 else v_even)[span, :])
                above = jnp.where(lane_mask(lanes, head), part, above)
                below = jnp.where(lane_mask(lanes, head ^ 1), part, below)
            sums = swap_heads(below)
            o_all[block, :] = (above / sums).astype(BF16)
            lse[0, block, :] = sums

        each_width(count, frames // step, run)

    def exact(block, low, count):
        query = q_all[block, :]
        highest[...] = jnp.full_like(highest, MASKED)
        total[...] = jnp.zeros_like(total)
        product[...] = jnp.zeros_like(product)

        def one_step(j, _):
            span = pl.ds(pl.multiple_of(low + j * step, 128), step)
            set_bias(block, span, step)
            key, value = k_all[span, :], v_all[span, :]
            for head in range(heads):
                masked = jnp.where(lane_mask(lanes, head), query, jnp.zeros_like(query))
                scores = dot(masked, key, NT) + bias[:, 0:step]
                before = highest[head, :, 0:1]
                top = jnp.maximum(before, jnp.max(scores, axis=1, keepdims=True))
                weight = jnp.exp(scores - top)
                fade = jnp.exp(before - top)
                highest[head] = jnp.broadcast_to(top, (step, 128))
                total[head] = total[head] * fade + jnp.sum(weight, axis=1, keepdims=True)
                product[head] = product[head] * fade + dot(weight.astype(BF16), value)
            return 0

        lax.fori_loop(0, count, one_step, 0)
        result = jnp.zeros((step, lanes), F32)
        logs = jnp.zeros((step, lanes), F32)
        for head in range(heads):
            keep = lane_mask(lanes, head)
            sums = total[head, :, 0:1]
            result = jnp.where(keep, product[head] / sums, result)
            logs = jnp.where(keep, highest[head, :, 0:1] + jnp.log(sums), logs)
        o_all[block, :] = result.astype(BF16)
        lse[0, block, :] = logs

    each_block(shifted)
    safe = jnp.min(lse[0]) > 1e-30

    @pl.when(safe)
    def _():
        lse[0] = shift + jnp.log(lse[0])

    @pl.when(jnp.logical_not(safe))
    def _():
        each_block(exact)

    for piece in range(pieces):
        outs[piece][...] = o_all[pl.ds(piece_start(place, piece, pieces, rows), rows), :]


def attend(place, bounds, seg_col, seg_row, qkv, lanes, step):
    pieces, rows, columns = qkv.shape
    groups = columns // (3 * lanes)
    heads = lanes // HEAD_DIM
    frames = rows * pieces
    specs = [
        pl.BlockSpec((None, rows, 3 * lanes), lambda g, piece=piece: (piece, 0, g))
        for piece in range(pieces)
    ]
    smem = pl.BlockSpec(memory_space=pltpu.SMEM)
    area = frames * frames // 2 * heads * groups
    results = pl.pallas_call(
        functools.partial(attend_kernel, pieces, heads, step),
        grid=(groups,),
        out_shape=[jax.ShapeDtypeStruct((rows, groups * lanes), BF16)] * pieces
        + [jax.ShapeDtypeStruct((groups, frames, lanes), F32)],
        in_specs=[smem, smem, whole(seg_col.shape), whole(seg_row.shape)] + specs,
        out_specs=[pl.BlockSpec((rows, lanes), lambda g: (0, g))] * pieces
        + [pl.BlockSpec((1, frames, lanes), lambda g: (g, 0, 0))],
        scratch_shapes=[pltpu.VMEM((frames, lanes), BF16)] * 6
        + [
            pltpu.VMEM((step, frames), F32),
            pltpu.VMEM((heads, step, 128), F32),
            pltpu.VMEM((heads, step, 128), F32),
            pltpu.VMEM((heads, step, lanes), F32),
        ],
        compiler_params=params(),
        cost_estimate=cost(area * 4 * 256, frames * columns * 4, area),
        name="attend",
    )(place, bounds, seg_col, seg_row, *[qkv] * pieces)
    return results[:pieces], results[pieces]


def attend_back_kernel(pieces, heads, step, place, bounds, seg_col, seg_row, *refs):
    inputs = refs[: 3 * pieces]
    lse = refs[3 * pieces]
    later = refs[3 * pieces + 1 : 4 * pieces + 3]
    out, grad_w = refs[4 * pieces + 3 : 4 * pieces + 5]
    q_all, k_all, v_all, do_all, centre, dq_all, dk_all, dv_all, bias, weights, slopes = refs[
        4 * pieces + 5 : 4 * pieces + 16
    ]
    held, sems = refs[4 * pieces + 16 : -1], refs[-1]
    copies = [
        pltpu.make_async_copy(source, target, sems.at[n])
        for n, (source, target) in enumerate(zip(later, held))
    ]
    for copy in copies:
        copy.start()
    cosine, sine, *normed = held
    rows = inputs[0].shape[0]
    for piece in range(pieces):
        span = pl.ds(piece_start(place, piece, pieces, rows), rows)
        spread(inputs[3 * piece], span, (q_all, k_all, v_all))
        grad = inputs[3 * piece + 2][...]
        do_all[span, :] = grad
        centre[span, :] = head_sums(grad.astype(F32) * inputs[3 * piece + 1][...].astype(F32))
    frames, lanes = q_all.shape
    dk_all[...] = jnp.zeros_like(dk_all)
    dv_all[...] = jnp.zeros_like(dv_all)

    def one_block(i, _):
        block = pl.ds(pl.multiple_of(i * step, step), step)
        low = pl.multiple_of(bounds[0, i], 128)

        def run(width):
            width = width * step
            span = pl.ds(low, width)
            same = seg_col[block, :] == seg_row[0:1, span]
            bias[:, 0:width] = jnp.where(same, 0.0, MASKED)
            query, key, value = q_all[block, :], k_all[span, :], v_all[span, :]
            grad = do_all[block, :]
            queries = stack_heads(query, heads)
            grads = stack_heads(grad, heads)
            for head in range(heads):
                at = slice(head * step, (head + 1) * step)
                column = slice(head * HEAD_DIM, head * HEAD_DIM + 1)
                scores = dot(queries[at], key, NT) + bias[:, 0:width]
                weight = jnp.exp(scores - lse[0, block, column])
                weights[at, 0:width] = weight.astype(BF16)
            for head in range(heads):
                at = slice(head * step, (head + 1) * step)
                column = slice(head * HEAD_DIM, head * HEAD_DIM + 1)
                slope = dot(grads[at], value, NT) - centre[block, column]
                slopes[at, 0:width] = (weights[at, 0:width].astype(F32) * slope).astype(BF16)
            part = dot(slopes[:, 0:width], key)
            result = part[0:step]
            for head in range(1, heads):
                here = part[head * step : (head + 1) * step]
                result = jnp.where(lane_mask(lanes, head), here, result)
            dq_all[block, :] = result * HEAD_DIM**-0.5
            dv_all[span, :] += dot(weights[:, 0:width], grads, TN)
            dk_all[span, :] += dot(slopes[:, 0:width], queries, TN)

        each_width(bounds[1, i], frames // step, run)
        return 0

    lax.fori_loop(0, frames // step, one_block, 0)
    for copy in copies:
        copy.wait()
    for piece in range(pieces):
        span = pl.ds(piece_start(place, piece, pieces, rows), rows)
        cos = cosine[span, :]
        sin = -sine[span, :]
        slopes_here = (
            turn(dq_all[span, :], cos, sin), turn(dk_all[span, :], cos, sin), dv_all[span, :]
        )
        for kind, slope in enumerate(slopes_here):
            for at in range(0, lanes, 128):
                start = 3 * at + kind * 128
                out[piece, :, start : start + 128] = slope[:, at : at + 128].astype(BF16)
    grad_w[...] = sum(dot(normed[p][...], out[p], TN) for p in range(pieces)).astype(BF16)


def attend_back(
    place, bounds, seg_col, seg_row, qkv, attended, grads, lse, cosine, sine, normed, first, count, step
):
    pieces, rows, _ = qkv.shape
    lanes = 128 * count
    heads = lanes // HEAD_DIM
    block = first // count
    width = normed[0].shape[1]
    per_group = lse.shape[2] // lanes
    frames = rows * pieces
    specs, arrays = [], []
    for piece in range(pieces):
        specs.append(
            pl.BlockSpec((None, rows, 3 * lanes), lambda i, piece=piece: (piece, 0, block), pipeline_mode=pl.Buffered(1))
        )
        specs += [pl.BlockSpec((rows, lanes), lambda i: (0, block), pipeline_mode=pl.Buffered(1))] * 2
        arrays += [qkv, attended[piece], grads[piece]]
    smem = pl.BlockSpec(memory_space=pltpu.SMEM)
    area = frames * frames // 2 * heads
    return pl.pallas_call(
        functools.partial(attend_back_kernel, pieces, heads, step),
        grid=(1,),
        out_shape=[
            jax.ShapeDtypeStruct((pieces, rows, 3 * lanes), BF16),
            jax.ShapeDtypeStruct((width, 3 * lanes), BF16),
        ],
        in_specs=[smem, smem, whole(seg_col.shape, 1), whole(seg_row.shape, 1)]
        + specs
        + [
            pl.BlockSpec(
                (1, frames, lanes),
                lambda i: (block // per_group, 0, block % per_group),
                pipeline_mode=pl.Buffered(1),
            ),
        ]
        + [pl.BlockSpec(memory_space=pl.ANY)] * (pieces + 2),
        out_specs=[whole((pieces, rows, 3 * lanes), 1), whole((width, 3 * lanes), 1)],
        scratch_shapes=[pltpu.VMEM((frames, lanes), BF16)] * 4
        + [pltpu.VMEM((frames, lanes), F32)] * 4
        + [pltpu.VMEM((step, frames), F32)]
        + [pltpu.VMEM((heads * step, frames), BF16)] * 2
        + [pltpu.VMEM(cosine.shape, F32)] * 2
        + [pltpu.VMEM(normed[0].shape, BF16)] * pieces
        + [pltpu.SemaphoreType.DMA((pieces + 2,))],
        compiler_params=params(),
        cost_estimate=cost(area * 10 * 256, frames * lanes * 16, area),
        name="attend_back",
    )(place, bounds, seg_col, seg_row, *arrays, lse, cosine, sine, *normed)


def gelu_pair(h):
    root = math.sqrt(2.0 / math.pi)
    square = h * h
    bend = jnp.tanh(root * h * (1.0 + 0.044715 * square))
    half = 0.5 * (1.0 + bend)
    slope = half + 0.5 * h * (1.0 - bend * bend) * (root * (1.0 + 0.134145 * square))
    return h * half, slope


def flat(ref, span=slice(None)):
    value = ref[:, 0, :, span]
    return value.reshape(value.shape[0] * value.shape[1], value.shape[2])


def middle_kernel(pieces, place, *refs):
    x, member, member_flip, adaptive, dy, dy_moved = refs[:6]
    refs = refs[6:]
    attended, refs = refs[:pieces], refs[pieces:]
    w_out, refs = refs[:pieces], refs[pieces:]
    w_up, refs = refs[:pieces], refs[pieces:]
    w_down, refs = refs[:pieces], refs[pieces:]
    mixed, dx2, a2_out, d2_out, d1_out, dadaptive = refs[:6]
    refs = refs[6:]
    active, refs = refs[:pieces], refs[pieces:]
    dhidden, refs = refs[:pieces], refs[pieces:]
    dattended = refs[:pieces]
    width = x.shape[1]
    here = member[...]
    gate1, shift2, scale2, gate2 = (
        pick(here, adaptive[:, n * width : (n + 1) * width]) for n in (2, 3, 4, 5)
    )
    branch1 = sum(dot(attended[p][...], flat(w_out[p]), NT) for p in range(pieces))
    x2 = x[...].astype(F32) + gate1 * branch1
    n2, r2 = norm(x2)
    a2 = (n2 * (1.0 + scale2) + shift2).astype(BF16)
    a2_out[...] = a2
    branch2 = jnp.zeros_like(x2)
    slopes = []
    for p in range(pieces):
        value, slope = gelu_pair(dot(a2, flat(w_up[p])))
        value = value.astype(BF16)
        active[p][...] = value
        slopes.append(slope)
        branch2 = branch2 + dot(value, flat(w_down[p]), NT)
    mixed[...] = (x2 + gate2 * branch2).astype(BF16)
    upstream = jnp.where(place[1] == 1, dy[...], dy_moved[...]).astype(F32)
    d2 = (upstream * gate2).astype(BF16)
    d2_out[...] = d2
    da2 = jnp.zeros_like(x2)
    for p in range(pieces):
        dh = (dot(d2, flat(w_down[p])) * slopes[p]).astype(BF16)
        dhidden[p][...] = dh
        da2 = da2 + dot(dh, flat(w_up[p]), NT)
    u2 = da2 * (1.0 + scale2)
    back = upstream + r2 * (
        u2 - jnp.mean(u2, axis=-1, keepdims=True) - n2 * jnp.mean(u2 * n2, axis=-1, keepdims=True)
    )
    dx2[...] = back
    d1 = (back * gate1).astype(BF16)
    d1_out[...] = d1
    for p in range(pieces):
        dattended[p][...] = dot(d1, flat(w_out[p])).astype(BF16)

    @pl.when(pl.program_id(0) == 0)
    def _():
        dadaptive[...] = jnp.zeros_like(dadaptive)

    for n, term in enumerate((back * branch1, da2, da2 * n2, upstream * branch2)):
        dadaptive[:, n * width : (n + 1) * width] += gather(member_flip[...], term)


def middle(place, x, member, member_flip, adaptive, dy, dy_moved, attended, weights):
    pieces = len(attended)
    rows, width = x.shape
    head_columns = attended[0].shape[1]
    hidden = 2 * head_columns
    tile = min(256, rows)

    def tiled(columns):
        return pl.BlockSpec((tile, columns), lambda i, s: (i, 0))

    def shaped(columns, kind):
        return jax.ShapeDtypeStruct((rows, columns), kind)

    shards, slices, own_rows, _ = weights.shape

    def resident(columns, at):
        return [
            pl.BlockSpec(
                (shards, 1, own_rows, columns),
                lambda i, s, piece=piece: (0, lax.rem(s[0] + piece, slices), 0, at),
                pipeline_mode=pl.Buffered(1),
            )
            for piece in range(pieces)
        ]

    cuts = resident(head_columns, 4) + resident(hidden, 0) + resident(hidden, 1)
    work = 2 * rows * width * pieces * (3 * hidden * 2 + head_columns * 2)
    results = pl.pallas_call(
        functools.partial(middle_kernel, pieces),
        grid_spec=pltpu.PrefetchScalarGridSpec(
        num_scalar_prefetch=1,
        grid=(rows // tile,),
        in_specs=[
            tiled(width),
            tiled(32),
            pl.BlockSpec((16, tile), lambda i, s: (0, i)),
            whole(adaptive.shape, 1),
            tiled(width),
            tiled(width),
        ]
        + [tiled(head_columns)] * pieces
        + cuts,
        out_specs=[tiled(width)] * 5
        + [whole((8, 4 * width))]
        + [tiled(hidden)] * (2 * pieces)
        + [tiled(head_columns)] * pieces,
        ),
        out_shape=[
            shaped(width, BF16),
            shaped(width, F32),
            shaped(width, BF16),
            shaped(width, BF16),
            shaped(width, BF16),
            jax.ShapeDtypeStruct((8, 4 * width), F32),
        ]
        + [shaped(hidden, BF16)] * (2 * pieces)
        + [shaped(head_columns, BF16)] * pieces,
        compiler_params=params(),
        cost_estimate=cost(work, rows * width * 30, rows * hidden * pieces),
        name="middle",
    )(place, x, member, member_flip, adaptive, dy, dy_moved, *attended, *[weights] * (3 * pieces))
    head, rest = results[:6], results[6:]
    return head, rest[:pieces], rest[pieces : 2 * pieces], rest[2 * pieces :]


def part_kernel(groups, *refs):
    slopes, weights, out = refs[:groups], refs[groups], refs[-1]
    slope = jnp.concatenate([slope[...] for slope in slopes], axis=1)
    out[...] = dot(slope, weights[...], NT).astype(BF16)


def input_part(slopes, weights, piece):
    rows = slopes[0].shape[1]
    width, columns = weights.shape
    tile = min(256, rows)
    groups = len(slopes)
    return pl.pallas_call(
        functools.partial(part_kernel, groups),
        grid=(rows // tile,),
        in_specs=[pl.BlockSpec((None, tile, s.shape[2]), lambda i: (piece, i, 0)) for s in slopes]
        + [whole(weights.shape, 1)],
        out_shape=jax.ShapeDtypeStruct((rows, width), BF16),
        out_specs=pl.BlockSpec((tile, width), lambda i: (i, 0)),
        compiler_params=params(),
        cost_estimate=cost(2 * rows * width * columns, rows * width * 8),
        name="input_part",
    )(*slopes, weights)


def last_kernel(groups, arrivals, *refs):
    x, member, member_flip, adaptive, dx2 = refs[:5]
    refs = refs[5:]
    arrived, refs = refs[:arrivals], refs[arrivals:]
    slopes, refs = refs[:groups], refs[groups:]
    weights, grad, dadaptive = refs
    width = x.shape[1]
    normed, inverse = norm(x[...].astype(F32))
    scale = pick(member[...], adaptive[:, width : 2 * width])
    slope = jnp.concatenate([slope[...] for slope in slopes], axis=1)
    da1 = dot(slope, weights[...], NT)
    for piece in arrived:
        da1 = da1 + piece[...].astype(F32)
    u1 = da1 * (1.0 + scale)
    back = inverse * (
        u1
        - jnp.mean(u1, axis=-1, keepdims=True)
        - normed * jnp.mean(u1 * normed, axis=-1, keepdims=True)
    )
    grad[...] = (dx2[...] + back).astype(BF16)

    @pl.when(pl.program_id(0) == 0)
    def _():
        dadaptive[...] = jnp.zeros_like(dadaptive)

    dadaptive[:, :width] += gather(member_flip[...], da1)
    dadaptive[:, width:] += gather(member_flip[...], da1 * normed)


def last(half, x, member, member_flip, adaptive, dx2, arrived, slopes, weights):
    rows, width = x.shape[0] // 2, x.shape[1]
    tile = min(256, rows)
    first = half * (rows // tile)

    def tiled(columns):
        return pl.BlockSpec((tile, columns), lambda i: (first + i, 0))

    return pl.pallas_call(
        functools.partial(last_kernel, len(slopes), len(arrived)),
        grid=(rows // tile,),
        in_specs=[
            tiled(width),
            tiled(32),
            pl.BlockSpec((16, tile), lambda i: (0, first + i)),
            whole(adaptive.shape, 1),
            tiled(width),
        ]
        + [tiled(width)] * len(arrived)
        + [pl.BlockSpec((None, tile, s.shape[2]), lambda i: (0, first + i, 0)) for s in slopes]
        + [whole(weights.shape, 1)],
        out_shape=[
            jax.ShapeDtypeStruct((rows, width), BF16),
            jax.ShapeDtypeStruct((8, 2 * width), F32),
        ],
        out_specs=[pl.BlockSpec((tile, width), lambda i: (i, 0)), whole((8, 2 * width))],
        compiler_params=params(),
        cost_estimate=cost(2 * rows * width * sum(s.shape[2] for s in slopes), rows * width * 12),
        name="last",
    )(x, member, member_flip, adaptive, dx2, *arrived, *slopes, weights)


def time_vector(steps, width):
    halfway = width // 2
    rates = jnp.exp(jnp.arange(halfway, dtype=F32) * (-math.log(10000.0) / (halfway - 1)))
    angles = steps.astype(F32)[:, None] * rates[None, :]
    return jnp.concatenate([jnp.sin(angles), jnp.cos(angles)], axis=1)


def body(frames, clip_lengths, timesteps, w_qkv, w_out, w_up, w_down, w_ada, b_ada, grad_out):
    rows, width = frames.shape
    clips = clip_lengths.shape[0]
    pieces = lax.axis_size("hl") * 2
    group_rows = rows * pieces
    own_rows = w_qkv.shape[1]
    head_columns = width // pieces
    lanes = min(256, head_columns)
    pairs = head_columns // 128
    step = min(256, group_rows)
    place = lax.axis_index(SUB).astype(jnp.int32)

    qkv_shard = w_qkv.astype(BF16).reshape(3, own_rows, pairs, 128)
    qkv_shard = jnp.transpose(qkv_shard, (1, 2, 0, 3)).reshape(own_rows, 3 * head_columns)
    mlp_shard = jnp.concatenate(
        [w_up.astype(BF16), w_down.astype(BF16).T, w_out.astype(BF16).T], axis=1
    )
    qkv_shard = moved(qkv_shard)
    lengths = moved(clip_lengths)

    def around(value):
        return [value] + [from_sub(value, step) for step in range(1, pieces)]

    condition = jax.nn.silu(time_vector(timesteps, width))
    columns = w_ada.shape[1]
    devices = [lax.axis_size(axis) for axis in ALL]
    za, zb, cores, hh, hl = devices
    table = (
        jnp.dot(condition, lax.reduce_precision(w_ada, 8, 7), precision=HIGHEST)
        + lax.reduce_precision(b_ada, 8, 7)[None, :]
    )
    table, qkv_shard, lengths = together(table, qkv_shard, lengths)
    table = table.reshape(za, zb, 1, hh, 1, clips, columns)
    table = jnp.broadcast_to(table, (za, zb, cores, hh, hl, clips, columns))
    table = lax.all_to_all(table.reshape(-1, clips, columns), ALL, 0, 0, tiled=True)
    adaptive = jnp.transpose(table, (1, 0, 2)).reshape(clips, -1)
    adaptive = jnp.pad(adaptive, ((0, 8 - clips), (0, 0)))

    ends = jnp.cumsum(lengths, dtype=jnp.int32)
    starts = ends - lengths
    index = jnp.arange(group_rows, dtype=jnp.int32)
    segment = jnp.sum((index[:, None] >= ends[None, :]).astype(jnp.int32), axis=1, dtype=jnp.int32)
    edges = jnp.concatenate([jnp.zeros((1,), jnp.int32), ends])
    begins = jnp.max(jnp.where(index[:, None] >= edges[None, :], edges[None, :], 0), axis=1)
    position = (index - begins).astype(F32)
    lane = jnp.arange(128, dtype=jnp.int32) % HEAD_DIM
    rates = jnp.exp((lane % (HEAD_DIM // 2)).astype(F32) * (-2.0 * math.log(10000.0) / HEAD_DIM))
    angles = position[:, None] * rates[None, :]
    cosine = jnp.cos(angles)
    sine = jnp.sin(angles) * jnp.where(lane < HEAD_DIM // 2, -1.0, 1.0)[None, :]
    seg_col = segment[:, None]
    seg_row = segment[None, :]
    block_first = jnp.arange(0, group_rows, step, dtype=jnp.int32)
    first_seg = jnp.sum((block_first[:, None] >= ends[None, :]).astype(jnp.int32), axis=1)
    last_seg = jnp.sum((block_first[:, None] + (step - 1) >= ends[None, :]).astype(jnp.int32), axis=1)
    closing = jnp.concatenate([ends, jnp.full((1,), group_rows, jnp.int32)])
    low_at = jnp.sum(jnp.where(first_seg[:, None] == jnp.arange(clips + 1)[None, :], edges[None, :], 0), axis=1)
    high_at = jnp.sum(jnp.where(last_seg[:, None] == jnp.arange(clips + 1)[None, :], closing[None, :], 0), axis=1)
    low_at = low_at // 128 * 128
    widths = (high_at - low_at + step - 1) // step
    low_at = jnp.minimum(low_at, group_rows - widths * step)
    bounds = jnp.stack([low_at, widths]).astype(jnp.int32)
    own_index = place * rows + jnp.arange(rows, dtype=jnp.int32)
    member = ((own_index[:, None] >= starts[None, :]) & (own_index[:, None] < ends[None, :])).astype(F32)
    member = jnp.pad(member, ((0, 0), (0, 8 - clips))).astype(BF16)
    member_flip = jnp.pad(member.T, ((0, 8), (0, 0)))
    member = jnp.concatenate([member, member, member, jnp.zeros_like(member)], axis=1)

    x = sent(frames)
    stays = staying().astype(jnp.int32)
    held = gather_line(qkv_shard)
    held, adaptive, x, cosine, sine, member, mlp_shard = together(
        held, adaptive, x, cosine, sine, member, mlp_shard
    )
    near = gather_near(held)
    mlp_full = lax.all_gather(mlp_shard, ALL, axis=0, tiled=True)
    mlp_full = mlp_full.reshape(-1, pieces, own_rows, mlp_shard.shape[1])
    a1, x = first_norm(stays.reshape(1), frames, x, member, adaptive)
    near, a1, grad_out = together(near, a1, grad_out)
    far, a1_all = together(gather_far(*near), around(a1))
    qkv, qkv_full = project(place, a1_all, far, cosine, sine, lanes)
    at_place = place.reshape(1)
    qkv, grad_out = together(qkv, grad_out)
    dy = sent(grad_out)
    attended, lse = attend(at_place, bounds, seg_col, seg_row, qkv, lanes, step)
    attended, lse, dy = together(attended, lse, dy)
    attended_own = [attended[0]] + [
        from_sub_piece(attended, step_) for step_ in range(1, pieces)
    ]

    head, active, dhidden, dattended = middle(
        jnp.stack([place, stays]), x, member, member_flip, adaptive, grad_out, dy, attended_own, mlp_full
    )
    mixed, dx2, a2, d2, d1, dada_late = head
    grads_attended = [dattended[0]] + [
        from_sub_piece(dattended, step_) for step_ in range(1, pieces)
    ]
    mixed_back = sent(mixed)

    def summed(left, right):
        parts = [dot(left, part, TN).astype(BF16) for part in right]
        return [parts[0]] + [to_sub(parts[step], step) for step in range(1, pieces)]

    late = [summed(a2, dhidden), summed(d2, active), summed(d1, attended_own)]

    def back(first, count, qkv):
        return attend_back(
            at_place, bounds, seg_col, seg_row, qkv, attended, grads_attended, lse, cosine, sine,
            a1_all, first, count, step,
        )

    slopes, grads_qkv = [], []
    early = final = None

    def next_pairs(first, count):
        slope, grad = back(first, count, qkv)
        slopes.append(slope)
        grads_qkv.append(grad)

    late, grads_attended = together(late, grads_attended)
    late, qkv = together(cut_plane(late), qkv)
    late = swap_plane(late)
    for pair in range(max(pairs - 1, 1)):
        next_pairs(pair, 1)
    if pairs > 1:
        early = cut_plane([[grad] for grad in grads_qkv])
    late, early, slopes, grads_qkv, mixed_back = together(
        late, early, slopes, grads_qkv, mixed_back
    )
    late, qkv = together(cut_line(add_up(late), 1), qkv)
    late = swap_line(late, 1)
    if pairs > 1:
        early = swap_plane(early)
        next_pairs(pairs - 1, 1)
    late, early, slopes, grads_qkv = together(late, early, slopes, grads_qkv)
    final = cut_plane([grads_qkv[-1:]])
    late = add_up(late)
    if pairs > 1:
        early = cut_line(add_up(early), 1)
    final, early, late, slopes, dx2 = together(final, early, late, slopes, dx2)
    final = swap_plane(final)
    late = line_rest([late])
    if pairs > 1:
        early = swap_line(early, 1)
    parts = [input_part(slopes, qkv_full, piece) for piece in range(1, pieces)]
    final, early, late, parts = together(final, early, late, parts)
    arrived = [to_sub(part, piece) for piece, part in enumerate(parts, 1)]
    rest = [line_rest(cuts) for cuts in (early, final) if cuts]
    arrived, dx2, late = together(arrived, dx2, late)

    def rows_half(half, dx2):
        return last(half, x, member, member_flip, adaptive, dx2, arrived, slopes, qkv_full)

    late = moved(add_up(late))
    late, rest, dx2, (frames_low, dada_low) = together(late, rest, dx2, rows_half(0, dx2))
    rest = moved(jnp.concatenate([add_up(cuts) for cuts in rest], axis=1))
    late, rest, frames_low, (frames_high, dada_high) = together(
        late, rest, moved(frames_low), rows_half(1, dx2)
    )
    dada_early = dada_low + dada_high
    hidden_columns = w_up.shape[1]
    grad_up = late[:, :hidden_columns]
    grad_down = late[:, hidden_columns : 2 * hidden_columns]
    grad_outw = late[:, 2 * hidden_columns :]
    dadaptive = jnp.concatenate([dada_early, dada_late], axis=1)[:clips]
    dadaptive = jnp.transpose(dadaptive.reshape(clips, -1, columns), (1, 0, 2))
    dadaptive, frames_high, mixed, mixed_back = together(dadaptive, frames_high, mixed, mixed_back)
    mixed_back = jnp.where(staying(), mixed, mixed_back)
    dadaptive = lax.all_to_all(dadaptive, ALL, 0, 0, tiled=True)
    grad_frames = jnp.concatenate([frames_low, moved(frames_high)], axis=0).astype(F32)
    dadaptive = dadaptive.reshape(za, zb, cores, hh, hl, clips, columns)
    dadaptive = jnp.sum(dadaptive, axis=(2, 4)).reshape(-1, columns)
    grad_ada = dot(condition, dadaptive, TN, HIGHEST)
    grad_bias = jnp.sum(dadaptive, axis=0)

    grad_qkv = rest.reshape(own_rows, pairs, 3, 128)
    grad_qkv = jnp.transpose(grad_qkv, (2, 0, 1, 3)).reshape(w_qkv.shape).astype(F32)
    return (
        mixed_back,
        grad_frames,
        grad_qkv,
        grad_outw.astype(F32).T,
        grad_up.astype(F32),
        grad_down.astype(F32).T,
        grad_ada,
        grad_bias,
    )


def from_sub_piece(parts, step):
    pieces = len(parts)
    return from_sub(parts[pieces - step], step)


def solution(mesh):
    clip, head = mesh.shape["clip"], mesh.shape["head"]
    fine = Mesh(mesh.devices.reshape(clip // 4, 2, 2, 2, head // 2), ALL)
    by_clip = ("za", "zb", "core")
    by_head = ("hh", "hl")
    everywhere = by_clip + by_head
    placed = (
        P(everywhere, None),
        P(by_clip),
        P(),
        P(None, by_clip, by_head),
        P(by_head, by_clip),
        P(by_clip, by_head),
        P(by_head, by_clip),
        P(None, everywhere),
        P(everywhere),
        P(everywhere, None),
    )
    return jax.shard_map(
        body,
        mesh=fine,
        in_specs=placed,
        out_specs=(
            P(everywhere, None),
            P(everywhere, None),
            P(None, by_clip, by_head),
            P(by_head, by_clip),
            P(by_clip, by_head),
            P(by_head, by_clip),
            P(None, everywhere),
            P(everywhere),
        ),
        check_vma=False,
    )
```

```python
import functools
import math

import jax
import jax.numpy as jnp
from jax import lax
from jax.experimental import pallas as pl
from jax.experimental.pallas import tpu as pltpu
from jax.sharding import Mesh
from jax.sharding import PartitionSpec as P

HEAD_DIM = 64
HEADS = 16
HIGHEST = lax.Precision.HIGHEST
MASKED = -1e30
EPSILON = 1e-06
VMEM_LIMIT = 60 * 1024 * 1024
F32 = jnp.float32
BF16 = jnp.bfloat16

ALL = ("za", "zb", "core", "hh", "hl")
MOVE = ("core", "hh", "hl")
SUB = ("core", "hl")

NT = (((1,), (1,)), ((), ()))
NN = (((1,), (0,)), ((), ()))
TN = (((0,), (0,)), ((), ()))


def dot(a, b, dims=NN, precision=None):
    return lax.dot_general(a, b, dims, precision=precision, preferred_element_type=F32)


def params(limit=VMEM_LIMIT):
    return pltpu.CompilerParams(vmem_limit_bytes=limit)


def cost(flops, bytes_accessed, transcendentals=0):
    return pl.CostEstimate(
        flops=int(flops), bytes_accessed=int(bytes_accessed), transcendentals=int(transcendentals)
    )


def whole(shape, buffers=None):
    zeros = (0,) * len(shape)
    if buffers is None:
        return pl.BlockSpec(shape, lambda *_: zeros)
    return pl.BlockSpec(shape, lambda *_: zeros, pipeline_mode=pl.Buffered(buffers))


def sent(value):
    return lax.ppermute(value, ("core", "hh"), [(1, 2), (2, 1)])


def staying():
    return lax.axis_index("core") == lax.axis_index("hh")


def moved(value):
    return jnp.where(staying(), value, sent(value))


def from_sub(value, step):
    size = lax.axis_size("hl") * 2
    return lax.ppermute(value, SUB, [((d + step) % size, d) for d in range(size)])


def to_sub(value, step):
    size = lax.axis_size("hl") * 2
    return lax.ppermute(value, SUB, [(d, (d + step) % size) for d in range(size)])


SWAP = [(0, 1), (1, 0)]


def across(value, bit):
    size = lax.axis_size("za")
    return lax.ppermute(value, "za", [(i, i ^ bit) for i in range(size)])


def gather_line(shard):
    return jnp.stack([shard] + [across(shard, bits) for bits in range(1, lax.axis_size("za"))])


def gather_near(held):
    return held, lax.ppermute(held, "zb", SWAP), lax.ppermute(held, "hh", SWAP)


def gather_far(held, by_zb, by_hh):
    half = held.shape[0] // 2
    both_low = lax.ppermute(by_zb[:half], "hh", SWAP)
    both_high = lax.ppermute(by_hh[half:], "zb", SWAP)
    return held, by_zb, by_hh, both_low, both_high


FOUR = ((0, 0), (1, 0), (0, 1), (1, 1))


def cut_kernel(counts, where, *refs):
    outs = refs[-4:]
    zb, hh = where[0], where[1]
    first = start = 0
    for count in counts:
        terms = refs[first : first + count]
        columns = terms[0].shape[-1]
        for out, (dz, dh) in zip(outs, FOUR):
            z, h = lax.rem(zb + dz, 2), lax.rem(hh + dh, 2)
            part = terms[0][0, z, h]
            if count > 1:
                part = sum(term[0, z, h].astype(F32) for term in terms).astype(BF16)
            out[0, :, start : start + columns] = part
        first += count
        start += columns


def cut_plane(weights):
    size = lax.axis_size("za")
    where = jnp.stack([lax.axis_index("zb"), lax.axis_index("hh")]).astype(jnp.int32)
    terms = [term for group in weights for term in group]
    rows = terms[0].shape[0] // (size * 4)
    total = sum(group[0].shape[1] for group in weights)
    return pl.pallas_call(
        functools.partial(cut_kernel, [len(group) for group in weights]),
        grid_spec=pltpu.PrefetchScalarGridSpec(
            num_scalar_prefetch=1,
            grid=(size,),
            in_specs=[
                pl.BlockSpec((1, 2, 2, rows, term.shape[1]), lambda i, w: (i, 0, 0, 0, 0))
                for term in terms
            ],
            out_specs=[pl.BlockSpec((1, rows, total), lambda i, w: (i, 0, 0))] * 4,
        ),
        out_shape=[jax.ShapeDtypeStruct((size, rows, total), BF16)] * 4,
        compiler_params=params(),
        cost_estimate=cost(0, sum(2 * term.size for term in terms) + size * 8 * rows * total),
        name="cut",
    )(where, *[term.reshape(size, 2, 2, rows, -1) for term in terms])


def swap_plane(pieces):
    own, to_zb, to_hh, to_both = pieces
    from_both = lax.ppermute(to_both, ("zb", "hh"), [(0, 3), (1, 2), (2, 1), (3, 0)])
    from_hh = lax.ppermute(to_hh, "hh", SWAP)
    from_zb = lax.ppermute(to_zb, "zb", SWAP)
    return own, from_zb, from_hh, from_both


def add_up(pieces):
    return sum(piece.astype(F32) for piece in pieces).astype(BF16)


def cut_line(total, bit):
    pairs = total.reshape(total.shape[0] // 2, 2, *total.shape[1:])
    place = (lax.axis_index("za") // bit) % 2
    keep = lax.dynamic_index_in_dim(pairs, place, 1, keepdims=False)
    send = lax.dynamic_index_in_dim(pairs, 1 - place, 1, keepdims=False)
    return keep, send


def swap_line(cuts, bit):
    return cuts[0], across(cuts[1], bit)


def line_rest(pieces):
    total = add_up(pieces)
    count = total.shape[0]
    apart = lax.axis_size("za") // count
    mine = lax.axis_index("za") // apart
    cuts = [lax.dynamic_index_in_dim(total, mine ^ n, 0, keepdims=False) for n in range(count)]
    return [cuts[0]] + [across(cut, n * apart) for n, cut in enumerate(cuts) if n]


def together(*values):
    return lax.optimization_barrier(values)


def norm(values):
    centred = values - jnp.mean(values, axis=-1, keepdims=True)
    variance = jnp.mean(centred * centred, axis=-1, keepdims=True)
    inverse = lax.rsqrt(variance + EPSILON)
    return centred * inverse, inverse


def pick(member, table):
    high = table.astype(BF16)
    rest = table - high.astype(F32)
    middle = rest.astype(BF16)
    low = (rest - middle.astype(F32)).astype(BF16)
    return dot(member, jnp.concatenate([high, middle, low, jnp.zeros_like(low)], axis=0))


def gather(member_flip, term):
    high = term.astype(BF16)
    low = (term - high.astype(F32)).astype(BF16)
    return (dot(member_flip, high) + dot(member_flip, low))[0:8]


def first_norm_kernel(stays, there, here, member, adaptive, out, x):
    width = x.shape[1]
    x[...] = jnp.where(stays[0] == 1, there[...], here[...])
    normed, _ = norm(x[...].astype(F32))
    shift = pick(member[...], adaptive[:, :width])
    scale = pick(member[...], adaptive[:, width : 2 * width])
    out[...] = (normed * (1.0 + scale) + shift).astype(BF16)


def first_norm(stays, there, here, member, adaptive):
    rows, width = here.shape
    tile = min(256, rows)
    tiled = pl.BlockSpec((tile, width), lambda i: (i, 0))
    return pl.pallas_call(
        first_norm_kernel,
        grid=(rows // tile,),
        out_shape=[jax.ShapeDtypeStruct((rows, width), BF16)] * 2,
        in_specs=[
            pl.BlockSpec(memory_space=pltpu.SMEM),
            tiled,
            tiled,
            pl.BlockSpec((tile, 32), lambda i: (i, 0)),
            whole(adaptive.shape),
        ],
        out_specs=[tiled, tiled],
        compiler_params=params(),
        cost_estimate=cost(rows * width * 40, rows * width * 8),
        name="first_norm",
    )(stays, there, here, member, adaptive)


def turn(values, cosine, sine):
    lanes = values.shape[1]
    place = lax.broadcasted_iota(jnp.int32, (1, 128), 1) % HEAD_DIM
    first = place < HEAD_DIM // 2
    parts = []
    for at in range(0, lanes, 128):
        part = values[:, at : at + 128]
        ahead = pltpu.roll(part, 128 - HEAD_DIM // 2, 1)
        behind = pltpu.roll(part, HEAD_DIM // 2, 1)
        swapped = jnp.where(first, ahead, behind)
        parts.append(part * cosine + swapped * sine)
    return parts[0] if len(parts) == 1 else jnp.concatenate(parts, axis=1)


def project_kernel(pieces, tiles, lanes, where, *refs):
    a_refs, refs = refs[:pieces], refs[pieces:]
    own, by_zb, by_hh, both_low, both_high, cosine, sine, out, w, a, weights = refs
    size, rows, columns = own.shape
    i = pl.program_id(0)

    @pl.when(i == 0)
    def _():
        zb, hh = where[0], where[1]
        for n in range(size):
            z = where[2 + n]
            low = n < size // 2
            both = both_low[n] if low else both_high[n - size // 2]
            shards = ((zb, hh, own[n]), (1 - zb, hh, by_zb[n]), (zb, 1 - hh, by_hh[n]))
            for at_zb, at_hh, shard in shards + ((1 - zb, 1 - hh, both),):
                start = pl.multiple_of(((z * 2 + at_zb) * 2 + at_hh) * rows, rows)
                weights[pl.ds(start, rows), :] = shard
        w[...] = weights[...]

    for piece in range(pieces):

        @pl.when(i // tiles == piece)
        def _(piece=piece):
            a[...] = a_refs[piece][...]

    for start in range(0, columns, 3 * lanes):
        products = dot(a[...], weights[:, start : start + 3 * lanes])
        for at in range(0, 3 * lanes, 128):
            product = products[:, at : at + 128]
            kind = at // 128 % 3
            if kind < 2:
                product = turn(product, cosine[...], sine[...])
            if kind == 0:
                product = product * HEAD_DIM**-0.5
            out[:, start + at : start + at + 128] = product.astype(BF16)


def project(place, a_all, shards, cosine, sine, lanes):
    pieces = len(a_all)
    rows, width = a_all[0].shape
    size, own_rows, columns = shards[0].shape
    tile = min(256, rows)
    tiles = rows // tile
    where = [lax.axis_index("zb"), lax.axis_index("hh")]
    where += [lax.axis_index("za") ^ bits for bits in range(size)]
    where += [(place + piece) % pieces for piece in range(pieces)]
    where = jnp.stack(where).astype(jnp.int32)

    def rows_of(piece):
        return pl.BlockSpec(
            (tile, width), lambda i, w: (jnp.clip(i - piece * tiles, 0, tiles - 1), 0)
        )

    def tables():
        return pl.BlockSpec(
            (tile, 128), lambda i, w: (w[2 + size + i // tiles] * tiles + lax.rem(i, tiles), 0)
        )

    return pl.pallas_call(
        functools.partial(project_kernel, pieces, tiles, lanes),
        grid_spec=pltpu.PrefetchScalarGridSpec(
            num_scalar_prefetch=1,
            grid=(pieces * tiles,),
            in_specs=[rows_of(piece) for piece in range(pieces)]
            + [whole(shard.shape, 1) for shard in shards]
            + [tables(), tables()],
            out_specs=[
                pl.BlockSpec((None, tile, columns), lambda i, w: (i // tiles, lax.rem(i, tiles), 0)),
                whole((width, columns), 1),
            ],
            scratch_shapes=[pltpu.VMEM((tile, width), BF16), pltpu.VMEM((width, columns), BF16)],
        ),
        out_shape=[
            jax.ShapeDtypeStruct((pieces, rows, columns), BF16),
            jax.ShapeDtypeStruct((width, columns), BF16),
        ],
        compiler_params=params(),
        cost_estimate=cost(2 * pieces * rows * width * columns, pieces * rows * (width + columns) * 2),
        name="project",
    )(where, *a_all, *shards, cosine, sine)


def stack_heads(values, heads):
    none = jnp.zeros_like(values)
    lanes = values.shape[1]
    return jnp.concatenate(
        [jnp.where(lane_mask(lanes, head), values, none) for head in range(heads)], axis=0
    )


def lane_mask(lanes, head):
    return lax.broadcasted_iota(jnp.int32, (1, lanes), 1) // HEAD_DIM == head


def piece_start(place, piece, pieces, rows):
    return pl.multiple_of(lax.rem(place[0] + piece, pieces) * rows, rows)


def flip(values):
    return jnp.transpose(values.astype(F32))


def spread(ref, span, arrays):
    for at in range(0, ref.shape[1], 128):
        start = at // 384 * 128
        arrays[at // 128 % 3][span, start : start + 128] = ref[:, at : at + 128]


def each_width(count, limit, run):
    for width in range(1, limit + 1):

        @pl.when(count == width)
        def _(width=width):
            run(width)


def head_sums(values):
    lanes = values.shape[1]
    row = lax.broadcasted_iota(jnp.int32, (lanes, lanes), 0) // HEAD_DIM
    column = lax.broadcasted_iota(jnp.int32, (lanes, lanes), 1) // HEAD_DIM
    same = (row == column).astype(BF16)
    high = values.astype(BF16)
    low = (values - high.astype(F32)).astype(BF16)
    return dot(high, same) + dot(low, same)


def swap_heads(values):
    parts = [pltpu.roll(values[:, at : at + 128], HEAD_DIM, 1) for at in range(0, values.shape[1], 128)]
    return parts[0] if len(parts) == 1 else jnp.concatenate(parts, axis=1)


def largest_sum(ref, step):
    lanes = ref.shape[1]
    row = lax.broadcasted_iota(jnp.int32, (lanes, lanes), 0) // HEAD_DIM
    column = lax.broadcasted_iota(jnp.int32, (lanes, lanes), 1) // HEAD_DIM
    same = (row == column).astype(BF16)
    largest = jnp.zeros((1, lanes), F32)
    for at in range(0, ref.shape[0], step):
        values = ref[at : at + step, :]
        sums = dot(values * values, same)
        largest = jnp.maximum(largest, jnp.max(sums, axis=0, keepdims=True))
    return largest


def attend_kernel(pieces, heads, step, place, bounds, seg_col, seg_row, *refs):
    inputs = refs[:pieces]
    outs = refs[pieces : 2 * pieces]
    lse, q_all, k_all, v_all, v_even, v_odd, o_all, bias, highest, total, product = refs[2 * pieces :]
    rows = inputs[0].shape[0]
    frames, lanes = q_all.shape
    even = lax.broadcasted_iota(jnp.int32, (1, lanes), 1) // HEAD_DIM % 2 == 0
    for piece in range(pieces):
        span = pl.ds(piece_start(place, piece, pieces, rows), rows)
        spread(inputs[piece], span, (q_all, k_all, v_all))
        value = v_all[span, :]
        v_even[span, :] = jnp.where(even, value, jnp.ones_like(value))
        v_odd[span, :] = jnp.where(even, jnp.ones_like(value), value)
    limit = jnp.sqrt(largest_sum(q_all, 2 * step) * largest_sum(k_all, 2 * step))
    shift = limit * 1.02 - 60.0

    def each_block(run):
        def one_block(i, _):
            block = pl.ds(pl.multiple_of(i * step, step), step)
            run(block, pl.multiple_of(bounds[0, i], 128), bounds[1, i])
            return 0

        lax.fori_loop(0, frames // step, one_block, 0)

    def set_bias(block, span, width):
        same = seg_col[block, :] == seg_row[0:1, span]
        bias[:, 0:width] = jnp.where(same, 0.0, MASKED)

    def shifted(block, low, count):
        def run(width):
            width = width * step
            span = pl.ds(low, width)
            set_bias(block, span, width)
            query, key = q_all[block, :], k_all[span, :]
            above = jnp.zeros((step, lanes), F32)
            below = jnp.ones((step, lanes), F32)
            for head in range(heads):
                masked = jnp.where(lane_mask(lanes, head), query, jnp.zeros_like(query))
                scores = dot(masked, key, NT) + bias[:, 0:width]
                at = head * HEAD_DIM
                weight = jnp.exp(scores - shift[:, at : at + 1]).astype(BF16)
                part = dot(weight, (v_odd if head % 2 else v_even)[span, :])
                above = jnp.where(lane_mask(lanes, head), part, above)
                below = jnp.where(lane_mask(lanes, head ^ 1), part, below)
            sums = swap_heads(below)
            o_all[block, :] = (above / sums).astype(BF16)
            lse[0, block, :] = sums

        each_width(count, frames // step, run)

    def exact(block, low, count):
        query = q_all[block, :]
        highest[...] = jnp.full_like(highest, MASKED)
        total[...] = jnp.zeros_like(total)
        product[...] = jnp.zeros_like(product)

        def one_step(j, _):
            span = pl.ds(pl.multiple_of(low + j * step, 128), step)
            set_bias(block, span, step)
            key, value = k_all[span, :], v_all[span, :]
            for head in range(heads):
                masked = jnp.where(lane_mask(lanes, head), query, jnp.zeros_like(query))
                scores = dot(masked, key, NT) + bias[:, 0:step]
                before = highest[head, :, 0:1]
                top = jnp.maximum(before, jnp.max(scores, axis=1, keepdims=True))
                weight = jnp.exp(scores - top)
                fade = jnp.exp(before - top)
                highest[head] = jnp.broadcast_to(top, (step, 128))
                total[head] = total[head] * fade + jnp.sum(weight, axis=1, keepdims=True)
                product[head] = product[head] * fade + dot(weight.astype(BF16), value)
            return 0

        lax.fori_loop(0, count, one_step, 0)
        result = jnp.zeros((step, lanes), F32)
        logs = jnp.zeros((step, lanes), F32)
        for head in range(heads):
            keep = lane_mask(lanes, head)
            sums = total[head, :, 0:1]
            result = jnp.where(keep, product[head] / sums, result)
            logs = jnp.where(keep, highest[head, :, 0:1] + jnp.log(sums), logs)
        o_all[block, :] = result.astype(BF16)
        lse[0, block, :] = logs

    each_block(shifted)
    safe = jnp.min(lse[0]) > 1e-30

    @pl.when(safe)
    def _():
        lse[0] = shift + jnp.log(lse[0])

    @pl.when(jnp.logical_not(safe))
    def _():
        each_block(exact)

    for piece in range(pieces):
        outs[piece][...] = o_all[pl.ds(piece_start(place, piece, pieces, rows), rows), :]


def attend(place, bounds, seg_col, seg_row, qkv, lanes, step):
    pieces, rows, columns = qkv.shape
    groups = columns // (3 * lanes)
    heads = lanes // HEAD_DIM
    frames = rows * pieces
    specs = [
        pl.BlockSpec((None, rows, 3 * lanes), lambda g, piece=piece: (piece, 0, g))
        for piece in range(pieces)
    ]
    smem = pl.BlockSpec(memory_space=pltpu.SMEM)
    area = frames * frames // 2 * heads * groups
    results = pl.pallas_call(
        functools.partial(attend_kernel, pieces, heads, step),
        grid=(groups,),
        out_shape=[jax.ShapeDtypeStruct((rows, groups * lanes), BF16)] * pieces
        + [jax.ShapeDtypeStruct((groups, frames, lanes), F32)],
        in_specs=[smem, smem, whole(seg_col.shape), whole(seg_row.shape)] + specs,
        out_specs=[pl.BlockSpec((rows, lanes), lambda g: (0, g))] * pieces
        + [pl.BlockSpec((1, frames, lanes), lambda g: (g, 0, 0))],
        scratch_shapes=[pltpu.VMEM((frames, lanes), BF16)] * 6
        + [
            pltpu.VMEM((step, frames), F32),
            pltpu.VMEM((heads, step, 128), F32),
            pltpu.VMEM((heads, step, 128), F32),
            pltpu.VMEM((heads, step, lanes), F32),
        ],
        compiler_params=params(),
        cost_estimate=cost(area * 4 * 256, frames * columns * 4, area),
        name="attend",
    )(place, bounds, seg_col, seg_row, *[qkv] * pieces)
    return results[:pieces], results[pieces]


def attend_back_kernel(pieces, heads, step, place, bounds, seg_col, seg_row, *refs):
    inputs = refs[: 3 * pieces]
    lse = refs[3 * pieces]
    later = refs[3 * pieces + 1 : 4 * pieces + 3]
    out, grad_w = refs[4 * pieces + 3 : 4 * pieces + 5]
    q_all, k_all, v_all, do_all, centre, dq_all, dk_all, dv_all, bias, weights, slopes = refs[
        4 * pieces + 5 : 4 * pieces + 16
    ]
    held, sems = refs[4 * pieces + 16 : -1], refs[-1]
    copies = [
        pltpu.make_async_copy(source, target, sems.at[n])
        for n, (source, target) in enumerate(zip(later, held))
    ]
    for copy in copies:
        copy.start()
    cosine, sine, *normed = held
    rows = inputs[0].shape[0]
    for piece in range(pieces):
        span = pl.ds(piece_start(place, piece, pieces, rows), rows)
        spread(inputs[3 * piece], span, (q_all, k_all, v_all))
        grad = inputs[3 * piece + 2][...]
        do_all[span, :] = grad
        centre[span, :] = head_sums(grad.astype(F32) * inputs[3 * piece + 1][...].astype(F32))
    frames, lanes = q_all.shape
    dk_all[...] = jnp.zeros_like(dk_all)
    dv_all[...] = jnp.zeros_like(dv_all)

    def one_block(i, _):
        block = pl.ds(pl.multiple_of(i * step, step), step)
        low = pl.multiple_of(bounds[0, i], 128)

        def run(width):
            width = width * step
            span = pl.ds(low, width)
            same = seg_col[block, :] == seg_row[0:1, span]
            bias[:, 0:width] = jnp.where(same, 0.0, MASKED)
            query, key, value = q_all[block, :], k_all[span, :], v_all[span, :]
            grad = do_all[block, :]
            queries = stack_heads(query, heads)
            grads = stack_heads(grad, heads)
            for head in range(heads):
                at = slice(head * step, (head + 1) * step)
                column = slice(head * HEAD_DIM, head * HEAD_DIM + 1)
                scores = dot(queries[at], key, NT) + bias[:, 0:width]
                weight = jnp.exp(scores - lse[0, block, column])
                weights[at, 0:width] = weight.astype(BF16)
            for head in range(heads):
                at = slice(head * step, (head + 1) * step)
                column = slice(head * HEAD_DIM, head * HEAD_DIM + 1)
                slope = dot(grads[at], value, NT) - centre[block, column]
                slopes[at, 0:width] = (weights[at, 0:width].astype(F32) * slope).astype(BF16)
            part = dot(slopes[:, 0:width], key)
            result = part[0:step]
            for head in range(1, heads):
                here = part[head * step : (head + 1) * step]
                result = jnp.where(lane_mask(lanes, head), here, result)
            dq_all[block, :] = result * HEAD_DIM**-0.5
            dv_all[span, :] += dot(weights[:, 0:width], grads, TN)
            dk_all[span, :] += dot(slopes[:, 0:width], queries, TN)

        each_width(bounds[1, i], frames // step, run)
        return 0

    lax.fori_loop(0, frames // step, one_block, 0)
    for copy in copies:
        copy.wait()
    for piece in range(pieces):
        span = pl.ds(piece_start(place, piece, pieces, rows), rows)
        cos = cosine[span, :]
        sin = -sine[span, :]
        slopes_here = (
            turn(dq_all[span, :], cos, sin), turn(dk_all[span, :], cos, sin), dv_all[span, :]
        )
        for kind, slope in enumerate(slopes_here):
            for at in range(0, lanes, 128):
                start = 3 * at + kind * 128
                out[piece, :, start : start + 128] = slope[:, at : at + 128].astype(BF16)
    grad_w[...] = sum(dot(normed[p][...], out[p], TN) for p in range(pieces)).astype(BF16)


def attend_back(
    place, bounds, seg_col, seg_row, qkv, attended, grads, lse, cosine, sine, normed, first, count, step
):
    pieces, rows, _ = qkv.shape
    lanes = 128 * count
    heads = lanes // HEAD_DIM
    block = first // count
    width = normed[0].shape[1]
    per_group = lse.shape[2] // lanes
    frames = rows * pieces
    specs, arrays = [], []
    for piece in range(pieces):
        specs.append(
            pl.BlockSpec((None, rows, 3 * lanes), lambda i, piece=piece: (piece, 0, block), pipeline_mode=pl.Buffered(1))
        )
        specs += [pl.BlockSpec((rows, lanes), lambda i: (0, block), pipeline_mode=pl.Buffered(1))] * 2
        arrays += [qkv, attended[piece], grads[piece]]
    smem = pl.BlockSpec(memory_space=pltpu.SMEM)
    area = frames * frames // 2 * heads
    return pl.pallas_call(
        functools.partial(attend_back_kernel, pieces, heads, step),
        grid=(1,),
        out_shape=[
            jax.ShapeDtypeStruct((pieces, rows, 3 * lanes), BF16),
            jax.ShapeDtypeStruct((width, 3 * lanes), BF16),
        ],
        in_specs=[smem, smem, whole(seg_col.shape, 1), whole(seg_row.shape, 1)]
        + specs
        + [
            pl.BlockSpec(
                (1, frames, lanes),
                lambda i: (block // per_group, 0, block % per_group),
                pipeline_mode=pl.Buffered(1),
            ),
        ]
        + [pl.BlockSpec(memory_space=pl.ANY)] * (pieces + 2),
        out_specs=[whole((pieces, rows, 3 * lanes), 1), whole((width, 3 * lanes), 1)],
        scratch_shapes=[pltpu.VMEM((frames, lanes), BF16)] * 4
        + [pltpu.VMEM((frames, lanes), F32)] * 4
        + [pltpu.VMEM((step, frames), F32)]
        + [pltpu.VMEM((heads * step, frames), BF16)] * 2
        + [pltpu.VMEM(cosine.shape, F32)] * 2
        + [pltpu.VMEM(normed[0].shape, BF16)] * pieces
        + [pltpu.SemaphoreType.DMA((pieces + 2,))],
        compiler_params=params(),
        cost_estimate=cost(area * 10 * 256, frames * lanes * 16, area),
        name="attend_back",
    )(place, bounds, seg_col, seg_row, *arrays, lse, cosine, sine, *normed)


def gelu_pair(h):
    root = math.sqrt(2.0 / math.pi)
    square = h * h
    bend = jnp.tanh(root * h * (1.0 + 0.044715 * square))
    half = 0.5 * (1.0 + bend)
    slope = half + 0.5 * h * (1.0 - bend * bend) * (root * (1.0 + 0.134145 * square))
    return h * half, slope


def flat(ref, span=slice(None)):
    value = ref[:, 0, :, span]
    return value.reshape(value.shape[0] * value.shape[1], value.shape[2])


def middle_kernel(pieces, place, *refs):
    x, member, member_flip, adaptive, dy, dy_moved = refs[:6]
    refs = refs[6:]
    attended, refs = refs[:pieces], refs[pieces:]
    w_out, refs = refs[:pieces], refs[pieces:]
    w_up, refs = refs[:pieces], refs[pieces:]
    w_down, refs = refs[:pieces], refs[pieces:]
    mixed, dx2, a2_out, d2_out, d1_out, dadaptive = refs[:6]
    refs = refs[6:]
    active, refs = refs[:pieces], refs[pieces:]
    dhidden, refs = refs[:pieces], refs[pieces:]
    dattended = refs[:pieces]
    width = x.shape[1]
    here = member[...]
    gate1, shift2, scale2, gate2 = (
        pick(here, adaptive[:, n * width : (n + 1) * width]) for n in (2, 3, 4, 5)
    )
    branch1 = sum(dot(attended[p][...], flat(w_out[p]), NT) for p in range(pieces))
    x2 = x[...].astype(F32) + gate1 * branch1
    n2, r2 = norm(x2)
    a2 = (n2 * (1.0 + scale2) + shift2).astype(BF16)
    a2_out[...] = a2
    branch2 = jnp.zeros_like(x2)
    slopes = []
    for p in range(pieces):
        value, slope = gelu_pair(dot(a2, flat(w_up[p])))
        value = value.astype(BF16)
        active[p][...] = value
        slopes.append(slope)
        branch2 = branch2 + dot(value, flat(w_down[p]), NT)
    mixed[...] = (x2 + gate2 * branch2).astype(BF16)
    upstream = jnp.where(place[1] == 1, dy[...], dy_moved[...]).astype(F32)
    d2 = (upstream * gate2).astype(BF16)
    d2_out[...] = d2
    da2 = jnp.zeros_like(x2)
    for p in range(pieces):
        dh = (dot(d2, flat(w_down[p])) * slopes[p]).astype(BF16)
        dhidden[p][...] = dh
        da2 = da2 + dot(dh, flat(w_up[p]), NT)
    u2 = da2 * (1.0 + scale2)
    back = upstream + r2 * (
        u2 - jnp.mean(u2, axis=-1, keepdims=True) - n2 * jnp.mean(u2 * n2, axis=-1, keepdims=True)
    )
    dx2[...] = back
    d1 = (back * gate1).astype(BF16)
    d1_out[...] = d1
    for p in range(pieces):
        dattended[p][...] = dot(d1, flat(w_out[p])).astype(BF16)

    @pl.when(pl.program_id(0) == 0)
    def _():
        dadaptive[...] = jnp.zeros_like(dadaptive)

    for n, term in enumerate((back * branch1, da2, da2 * n2, upstream * branch2)):
        dadaptive[:, n * width : (n + 1) * width] += gather(member_flip[...], term)


def middle(place, x, member, member_flip, adaptive, dy, dy_moved, attended, weights):
    pieces = len(attended)
    rows, width = x.shape
    head_columns = attended[0].shape[1]
    hidden = 2 * head_columns
    tile = min(256, rows)

    def tiled(columns):
        return pl.BlockSpec((tile, columns), lambda i, s: (i, 0))

    def shaped(columns, kind):
        return jax.ShapeDtypeStruct((rows, columns), kind)

    shards, slices, own_rows, _ = weights.shape

    def resident(columns, at):
        return [
            pl.BlockSpec(
                (shards, 1, own_rows, columns),
                lambda i, s, piece=piece: (0, lax.rem(s[0] + piece, slices), 0, at),
                pipeline_mode=pl.Buffered(1),
            )
            for piece in range(pieces)
        ]

    cuts = resident(head_columns, 4) + resident(hidden, 0) + resident(hidden, 1)
    work = 2 * rows * width * pieces * (3 * hidden * 2 + head_columns * 2)
    results = pl.pallas_call(
        functools.partial(middle_kernel, pieces),
        grid_spec=pltpu.PrefetchScalarGridSpec(
        num_scalar_prefetch=1,
        grid=(rows // tile,),
        in_specs=[
            tiled(width),
            tiled(32),
            pl.BlockSpec((16, tile), lambda i, s: (0, i)),
            whole(adaptive.shape, 1),
            tiled(width),
            tiled(width),
        ]
        + [tiled(head_columns)] * pieces
        + cuts,
        out_specs=[tiled(width)] * 5
        + [whole((8, 4 * width))]
        + [tiled(hidden)] * (2 * pieces)
        + [tiled(head_columns)] * pieces,
        ),
        out_shape=[
            shaped(width, BF16),
            shaped(width, F32),
            shaped(width, BF16),
            shaped(width, BF16),
            shaped(width, BF16),
            jax.ShapeDtypeStruct((8, 4 * width), F32),
        ]
        + [shaped(hidden, BF16)] * (2 * pieces)
        + [shaped(head_columns, BF16)] * pieces,
        compiler_params=params(),
        cost_estimate=cost(work, rows * width * 30, rows * hidden * pieces),
        name="middle",
    )(place, x, member, member_flip, adaptive, dy, dy_moved, *attended, *[weights] * (3 * pieces))
    head, rest = results[:6], results[6:]
    return head, rest[:pieces], rest[pieces : 2 * pieces], rest[2 * pieces :]


def part_kernel(groups, *refs):
    slopes, weights, out = refs[:groups], refs[groups], refs[-1]
    slope = jnp.concatenate([slope[...] for slope in slopes], axis=1)
    out[...] = dot(slope, weights[...], NT).astype(BF16)


def input_part(slopes, weights, piece):
    rows = slopes[0].shape[1]
    width, columns = weights.shape
    tile = min(256, rows)
    groups = len(slopes)
    return pl.pallas_call(
        functools.partial(part_kernel, groups),
        grid=(rows // tile,),
        in_specs=[pl.BlockSpec((None, tile, s.shape[2]), lambda i: (piece, i, 0)) for s in slopes]
        + [whole(weights.shape, 1)],
        out_shape=jax.ShapeDtypeStruct((rows, width), BF16),
        out_specs=pl.BlockSpec((tile, width), lambda i: (i, 0)),
        compiler_params=params(20 * 1024 * 1024),
        cost_estimate=cost(2 * rows * width * columns, rows * width * 8),
        name="input_part",
    )(*slopes, weights)


def last_kernel(groups, arrivals, *refs):
    x, member, member_flip, adaptive, dx2 = refs[:5]
    refs = refs[5:]
    arrived, refs = refs[:arrivals], refs[arrivals:]
    slopes, refs = refs[:groups], refs[groups:]
    weights, grad, dadaptive = refs
    width = x.shape[1]
    normed, inverse = norm(x[...].astype(F32))
    scale = pick(member[...], adaptive[:, width : 2 * width])
    slope = jnp.concatenate([slope[...] for slope in slopes], axis=1)
    da1 = dot(slope, weights[...], NT)
    for piece in arrived:
        da1 = da1 + piece[...].astype(F32)
    u1 = da1 * (1.0 + scale)
    back = inverse * (
        u1
        - jnp.mean(u1, axis=-1, keepdims=True)
        - normed * jnp.mean(u1 * normed, axis=-1, keepdims=True)
    )
    grad[...] = (dx2[...] + back).astype(BF16)

    @pl.when(pl.program_id(0) == 0)
    def _():
        dadaptive[...] = jnp.zeros_like(dadaptive)

    dadaptive[:, :width] += gather(member_flip[...], da1)
    dadaptive[:, width:] += gather(member_flip[...], da1 * normed)


def last(half, x, member, member_flip, adaptive, dx2, arrived, slopes, weights):
    rows, width = x.shape[0] // 2, x.shape[1]
    tile = min(256, rows)
    first = half * (rows // tile)

    def tiled(columns):
        return pl.BlockSpec((tile, columns), lambda i: (first + i, 0))

    return pl.pallas_call(
        functools.partial(last_kernel, len(slopes), len(arrived)),
        grid=(rows // tile,),
        in_specs=[
            tiled(width),
            tiled(32),
            pl.BlockSpec((16, tile), lambda i: (0, first + i)),
            whole(adaptive.shape, 1),
            tiled(width),
        ]
        + [tiled(width)] * len(arrived)
        + [pl.BlockSpec((None, tile, s.shape[2]), lambda i: (0, first + i, 0)) for s in slopes]
        + [whole(weights.shape, 1)],
        out_shape=[
            jax.ShapeDtypeStruct((rows, width), BF16),
            jax.ShapeDtypeStruct((8, 2 * width), F32),
        ],
        out_specs=[pl.BlockSpec((tile, width), lambda i: (i, 0)), whole((8, 2 * width))],
        compiler_params=params(),
        cost_estimate=cost(2 * rows * width * sum(s.shape[2] for s in slopes), rows * width * 12),
        name="last",
    )(x, member, member_flip, adaptive, dx2, *arrived, *slopes, weights)


def time_vector(steps, width):
    halfway = width // 2
    rates = jnp.exp(jnp.arange(halfway, dtype=F32) * (-math.log(10000.0) / (halfway - 1)))
    angles = steps.astype(F32)[:, None] * rates[None, :]
    return jnp.concatenate([jnp.sin(angles), jnp.cos(angles)], axis=1)


def body(frames, clip_lengths, timesteps, w_qkv, w_out, w_up, w_down, w_ada, b_ada, grad_out):
    rows, width = frames.shape
    clips = clip_lengths.shape[0]
    pieces = lax.axis_size("hl") * 2
    group_rows = rows * pieces
    own_rows = w_qkv.shape[1]
    head_columns = width // pieces
    lanes = min(256, head_columns)
    pairs = head_columns // 128
    step = min(256, group_rows)
    place = lax.axis_index(SUB).astype(jnp.int32)

    qkv_shard = w_qkv.astype(BF16).reshape(3, own_rows, pairs, 128)
    qkv_shard = jnp.transpose(qkv_shard, (1, 2, 0, 3)).reshape(own_rows, 3 * head_columns)
    mlp_shard = jnp.concatenate(
        [w_up.astype(BF16), w_down.astype(BF16).T, w_out.astype(BF16).T], axis=1
    )
    qkv_shard = moved(qkv_shard)
    lengths = moved(clip_lengths)

    def around(value):
        return [value] + [from_sub(value, step) for step in range(1, pieces)]

    condition = jax.nn.silu(time_vector(timesteps, width))
    columns = w_ada.shape[1]
    devices = [lax.axis_size(axis) for axis in ALL]
    za, zb, cores, hh, hl = devices
    table = (
        jnp.dot(condition, lax.reduce_precision(w_ada, 8, 7), precision=HIGHEST)
        + lax.reduce_precision(b_ada, 8, 7)[None, :]
    )
    table, qkv_shard, lengths = together(table, qkv_shard, lengths)
    table = table.reshape(za, zb, 1, hh, 1, clips, columns)
    table = jnp.broadcast_to(table, (za, zb, cores, hh, hl, clips, columns))
    table = lax.all_to_all(table.reshape(-1, clips, columns), ALL, 0, 0, tiled=True)
    adaptive = jnp.transpose(table, (1, 0, 2)).reshape(clips, -1)
    adaptive = jnp.pad(adaptive, ((0, 8 - clips), (0, 0)))

    ends = jnp.cumsum(lengths, dtype=jnp.int32)
    starts = ends - lengths
    index = jnp.arange(group_rows, dtype=jnp.int32)
    segment = jnp.sum((index[:, None] >= ends[None, :]).astype(jnp.int32), axis=1, dtype=jnp.int32)
    edges = jnp.concatenate([jnp.zeros((1,), jnp.int32), ends])
    begins = jnp.max(jnp.where(index[:, None] >= edges[None, :], edges[None, :], 0), axis=1)
    position = (index - begins).astype(F32)
    lane = jnp.arange(128, dtype=jnp.int32) % HEAD_DIM
    rates = jnp.exp((lane % (HEAD_DIM // 2)).astype(F32) * (-2.0 * math.log(10000.0) / HEAD_DIM))
    angles = position[:, None] * rates[None, :]
    cosine = jnp.cos(angles)
    sine = jnp.sin(angles) * jnp.where(lane < HEAD_DIM // 2, -1.0, 1.0)[None, :]
    seg_col = segment[:, None]
    seg_row = segment[None, :]
    block_first = jnp.arange(0, group_rows, step, dtype=jnp.int32)
    first_seg = jnp.sum((block_first[:, None] >= ends[None, :]).astype(jnp.int32), axis=1)
    last_seg = jnp.sum((block_first[:, None] + (step - 1) >= ends[None, :]).astype(jnp.int32), axis=1)
    closing = jnp.concatenate([ends, jnp.full((1,), group_rows, jnp.int32)])
    low_at = jnp.sum(jnp.where(first_seg[:, None] == jnp.arange(clips + 1)[None, :], edges[None, :], 0), axis=1)
    high_at = jnp.sum(jnp.where(last_seg[:, None] == jnp.arange(clips + 1)[None, :], closing[None, :], 0), axis=1)
    low_at = low_at // 128 * 128
    widths = (high_at - low_at + step - 1) // step
    low_at = jnp.minimum(low_at, group_rows - widths * step)
    bounds = jnp.stack([low_at, widths]).astype(jnp.int32)
    own_index = place * rows + jnp.arange(rows, dtype=jnp.int32)
    member = ((own_index[:, None] >= starts[None, :]) & (own_index[:, None] < ends[None, :])).astype(F32)
    member = jnp.pad(member, ((0, 0), (0, 8 - clips))).astype(BF16)
    member_flip = jnp.pad(member.T, ((0, 8), (0, 0)))
    member = jnp.concatenate([member, member, member, jnp.zeros_like(member)], axis=1)

    x = sent(frames)
    stays = staying().astype(jnp.int32)
    held = gather_line(qkv_shard)
    held, adaptive, x, cosine, sine, member, mlp_shard = together(
        held, adaptive, x, cosine, sine, member, mlp_shard
    )
    near = gather_near(held)
    mlp_full = lax.all_gather(mlp_shard, ALL, axis=0, tiled=True)
    mlp_full = mlp_full.reshape(-1, pieces, own_rows, mlp_shard.shape[1])
    a1, x = first_norm(stays.reshape(1), frames, x, member, adaptive)
    near, a1, grad_out = together(near, a1, grad_out)
    far, a1_all = together(gather_far(*near), around(a1))
    qkv, qkv_full = project(place, a1_all, far, cosine, sine, lanes)
    at_place = place.reshape(1)
    qkv, grad_out = together(qkv, grad_out)
    dy = sent(grad_out)
    attended, lse = attend(at_place, bounds, seg_col, seg_row, qkv, lanes, step)
    attended, lse, dy = together(attended, lse, dy)
    attended_own = [attended[0]] + [
        from_sub_piece(attended, step_) for step_ in range(1, pieces)
    ]

    head, active, dhidden, dattended = middle(
        jnp.stack([place, stays]), x, member, member_flip, adaptive, grad_out, dy, attended_own, mlp_full
    )
    mixed, dx2, a2, d2, d1, dada_late = head
    grads_attended = [dattended[0]] + [
        from_sub_piece(dattended, step_) for step_ in range(1, pieces)
    ]
    mixed_back = sent(mixed)

    def summed(left, right):
        parts = [dot(left, part, TN).astype(BF16) for part in right]
        return [parts[0]] + [to_sub(parts[step], step) for step in range(1, pieces)]

    late = [summed(a2, dhidden), summed(d2, active), summed(d1, attended_own)]

    def back(first, count, qkv):
        return attend_back(
            at_place, bounds, seg_col, seg_row, qkv, attended, grads_attended, lse, cosine, sine,
            a1_all, first, count, step,
        )

    slopes, grads_qkv = [], []
    early = final = None

    def next_pairs(first, count):
        slope, grad = back(first, count, qkv)
        slopes.append(slope)
        grads_qkv.append(grad)

    late, grads_attended = together(late, grads_attended)
    late, qkv = together(cut_plane(late), qkv)
    late = swap_plane(late)
    for pair in range(max(pairs - 1, 1)):
        next_pairs(pair, 1)
    if pairs > 1:
        early = cut_plane([[grad] for grad in grads_qkv])
    late, early, slopes, grads_qkv, mixed_back = together(
        late, early, slopes, grads_qkv, mixed_back
    )
    late, qkv = together(cut_line(add_up(late), 1), qkv)
    late = swap_line(late, 1)
    if pairs > 1:
        early = swap_plane(early)
        next_pairs(pairs - 1, 1)
    late, early, slopes, grads_qkv = together(late, early, slopes, grads_qkv)
    final = cut_plane([grads_qkv[-1:]])
    late = add_up(late)
    if pairs > 1:
        early = cut_line(add_up(early), 1)
    final, early, late, slopes, dx2 = together(final, early, late, slopes, dx2)
    final = swap_plane(final)
    late = line_rest([late])
    if pairs > 1:
        early = swap_line(early, 1)
    parts = [input_part(slopes, qkv_full, piece) for piece in range(1, pieces)]
    final, early, late, parts = together(final, early, late, parts)
    arrived = [to_sub(part, piece) for piece, part in enumerate(parts, 1)]
    rest = [line_rest(cuts) for cuts in (early, final) if cuts]
    arrived, dx2, late = together(arrived, dx2, late)

    def rows_half(half, dx2):
        return last(half, x, member, member_flip, adaptive, dx2, arrived, slopes, qkv_full)

    late = moved(add_up(late))
    late, rest, dx2, (frames_low, dada_low) = together(late, rest, dx2, rows_half(0, dx2))
    rest = moved(jnp.concatenate([add_up(cuts) for cuts in rest], axis=1))
    late, rest, frames_low, (frames_high, dada_high) = together(
        late, rest, moved(frames_low), rows_half(1, dx2)
    )
    dada_early = dada_low + dada_high
    hidden_columns = w_up.shape[1]
    grad_up = late[:, :hidden_columns]
    grad_down = late[:, hidden_columns : 2 * hidden_columns]
    grad_outw = late[:, 2 * hidden_columns :]
    dadaptive = jnp.concatenate([dada_early, dada_late], axis=1)[:clips]
    dadaptive = jnp.transpose(dadaptive.reshape(clips, -1, columns), (1, 0, 2))
    dadaptive, frames_high, mixed, mixed_back = together(dadaptive, frames_high, mixed, mixed_back)
    mixed_back = jnp.where(staying(), mixed, mixed_back)
    dadaptive = lax.all_to_all(dadaptive, ALL, 0, 0, tiled=True)
    grad_frames = jnp.concatenate([frames_low, moved(frames_high)], axis=0).astype(F32)
    dadaptive = dadaptive.reshape(za, zb, cores, hh, hl, clips, columns)
    dadaptive = jnp.sum(dadaptive, axis=(2, 4)).reshape(-1, columns)
    grad_ada = dot(condition, dadaptive, TN, HIGHEST)
    grad_bias = jnp.sum(dadaptive, axis=0)

    grad_qkv = rest.reshape(own_rows, pairs, 3, 128)
    grad_qkv = jnp.transpose(grad_qkv, (2, 0, 1, 3)).reshape(w_qkv.shape).astype(F32)
    return (
        mixed_back,
        grad_frames,
        grad_qkv,
        grad_outw.astype(F32).T,
        grad_up.astype(F32),
        grad_down.astype(F32).T,
        grad_ada,
        grad_bias,
    )


def from_sub_piece(parts, step):
    pieces = len(parts)
    return from_sub(parts[pieces - step], step)


def solution(mesh):
    clip, head = mesh.shape["clip"], mesh.shape["head"]
    fine = Mesh(mesh.devices.reshape(clip // 4, 2, 2, 2, head // 2), ALL)
    by_clip = ("za", "zb", "core")
    by_head = ("hh", "hl")
    everywhere = by_clip + by_head
    placed = (
        P(everywhere, None),
        P(by_clip),
        P(),
        P(None, by_clip, by_head),
        P(by_head, by_clip),
        P(by_clip, by_head),
        P(by_head, by_clip),
        P(None, everywhere),
        P(everywhere),
        P(everywhere, None),
    )
    return jax.shard_map(
        body,
        mesh=fine,
        in_specs=placed,
        out_specs=(
            P(everywhere, None),
            P(everywhere, None),
            P(None, by_clip, by_head),
            P(by_head, by_clip),
            P(by_clip, by_head),
            P(by_head, by_clip),
            P(None, everywhere),
            P(everywhere),
        ),
        check_vma=False,
    )
```
